32 devices in a mesh: atoms: 8 (over z, x), bands: 4 (over y, core).
Axes of the slice: x: 2, y: 2, z: 4, core: 2. Of those that a mesh axis runs over, the one named last changes fastest.
Arguments:
- eigvecs: bfloat16 [8192, 8192], P('atoms', 'bands'), may hold values from -0.59765625 to 0.59765625
- occupations: float32 [8192], P('bands'), may hold values from 0.2 to 2
- energies: float32 [8192], P('bands'), may hold values from -1 to 0.5
- neighbours: int32 [64, 16], P('atoms'), may hold values from 0 to 63, as said below
Outputs:
- density: float32 [64, 16, 128, 128], P('atoms', None, 'bands')
- energy_density: float32 [64, 16, 128, 128], P('atoms', None, 'bands')
The draws below stay inside these ranges and needn't reach their ends.
Inputs may be any that keep to these rules, and one draw needn't show every extreme that they name: `neighbours`: every block named in the rows of one atoms domain lies in that domain or in one of the 2 domains on either side along the atoms axis, taken cyclically; from each of those 4 other domains the rows of one domain name exactly 2 distinct blocks.
All inputs are finite; a program needn't handle non-finite values.
Results may differ from the reference program's by a relative error of at most 0.014.
Values may be sent and summed in bfloat16 or wider, within the bound.
No kernel may reach another device: no remote copies, remote signals or barrier semaphores. Data moves between devices by JAX's collectives and lax.ppermute only.
A program may use at most 128 MiB of HBM per device.

```python
import jax
import jax.numpy as jnp
from jax import lax

NB_DEV = 8
K = 16
CAP = 2
R = 2
TILE = 128
NBAND = 8192
NB = 64
ORBITALS = 8192
N_BANDS = 4


def draw_neighbours(key, part):
    domain_count = NB // NB_DEV
    pool_size = NB_DEV + 2 * R * CAP
    total_slots = NB_DEV * K

    def one_domain(domain_key, domain):
        keys = jax.random.split(domain_key, 2 * R + 2)
        pools = [domain * NB_DEV + jnp.arange(NB_DEV, dtype=jnp.int32)]
        offsets = list(range(-R, 0)) + list(range(1, R + 1))
        for place, offset in enumerate(offsets):
            peer = (domain + offset) % domain_count
            picked = jax.random.permutation(keys[place], NB_DEV)[:CAP].astype(jnp.int32)
            pools.append(peer * NB_DEV + picked)
        pool = jnp.concatenate(pools, 0)
        extra = jax.random.randint(keys[2 * R], (total_slots,), 0, pool_size)
        slots = jnp.arange(total_slots, dtype=jnp.int32)
        which = jnp.where(slots < pool_size, slots, extra)
        values = pool[which]
        order = jax.random.permutation(keys[2 * R + 1], total_slots)
        return values[order].reshape(NB_DEV, K)
    domain_keys = jax.random.split(key, domain_count)
    result = jax.vmap(one_domain)(domain_keys, jnp.arange(domain_count, dtype=jnp.int32))
    return result.reshape(NB, K).astype(jnp.int32)


def levels(rng, shape, cuts, smallest, top_value):
    def one(position, shards_of):
        heights = jax.random.uniform(jax.random.fold_in(jax.random.fold_in(rng, 6), position), (shards_of,), jnp.float32, smallest / len(cuts), top_value / len(cuts))
        return jnp.repeat(jnp.exp(heights), shape[position] // shards_of).reshape((-1,) + (1,) * (len(shape) - position - 1))

    factor_of = one(*cuts[0])
    for cut in cuts[1:]:
        factor_of = factor_of * one(*cut)
    return factor_of


def scatter_about(stream_key, extent, width, most, pieces=(), kind=jnp.bfloat16):
    drawn = jax.random.normal(stream_key, extent, jnp.float32) * width
    if len(pieces) > 0:
        drawn = levels(stream_key, extent, pieces, -0.22, 0.18) * drawn
    return jnp.clip(drawn, min=-most, max=most).astype(kind)


def setup_inputs(seed: int = 0) -> dict:
    key_of = jax.random.split(jax.random.key(seed), 5)
    return {
        "eigvecs": scatter_about(key_of[0], (ORBITALS, NBAND), 0.1, 0.59765625, ((0, 8), (1, 4))),
        "occupations": jnp.clip(0.2 + 1.8 * jax.random.uniform(key_of[1], (NBAND,), jnp.float32) ** levels(key_of[1], (NBAND,), ((0, 4),), -0.2, 0.2), 0.2, 2.0),
        "energies": jnp.clip(-1.0 + 1.5 * jax.random.uniform(key_of[2], (NBAND,), jnp.float32) ** levels(key_of[2], (NBAND,), ((0, 4),), -0.2, 0.2), -1.0, 0.5),
        "neighbours": draw_neighbours(jax.random.fold_in(key_of[4], 71), 0),
    }


def reference(eigvecs, occupations, energies, neighbours):
    rows = eigvecs.reshape(NB, TILE, N_BANDS, NBAND // N_BANDS)
    occ_groups = occupations.reshape(N_BANDS, NBAND // N_BANDS)
    weight_groups = (occupations * energies).reshape(N_BANDS, NBAND // N_BANDS)
    scaled_p = (rows.astype(jnp.float32) * occ_groups).astype(jnp.bfloat16)
    scaled_w = (rows.astype(jnp.float32) * weight_groups).astype(jnp.bfloat16)
    scaled = jnp.stack([scaled_p, scaled_w], 1)

    def one_block(pair):
        left, block_ids = pair
        right = rows[block_ids.astype(jnp.int32)].astype(jnp.float32)
        part = jnp.einsum("sagb,kcgb->gksac", left.astype(jnp.float32), right)
        part = lax.optimization_barrier(part.astype(jnp.bfloat16))
        return jnp.sum(part.astype(jnp.float32), axis=0)

    tiles = lax.map(one_block, (scaled, neighbours))
    return tiles[:, :, 0], tiles[:, :, 1]
```

```python
import functools

import jax
import jax.numpy as jnp
from jax import lax
from jax.experimental import pallas as pl
from jax.experimental.pallas import tpu as pltpu
from jax.sharding import PartitionSpec as P

R = 2
VMEM_LIMIT = 48 * 1024 * 1024


def shifted(value, axis, steps):
    count = lax.axis_size(axis)
    pairs = [(source, (source + steps) % count) for source in range(count)]
    return lax.ppermute(value, axis, pairs)


def strip_target(group, chips, step, other_core):
    chip = lax.rem(lax.shift_right_logical(group, 1) + step, chips)
    return chip * 2 + ((group & 1) ^ other_core)


def to_strip_target(value, chips, step, other_core):
    pairs = [
        (group, (group // 2 + step) % chips * 2 + (group % 2 ^ other_core))
        for group in range(2 * chips)
    ]
    return lax.ppermute(value, "bands", pairs)


def pick_kernel(count, blocks, tile, place_ref, *refs):
    asks, (own, sib), outs = refs[:count], refs[count : count + 2], refs[count + 2 : -1]
    sems = refs[-1]
    first = place_ref[0] * blocks
    copies = []
    for index in range(count):
        ids = asks[index][...] - first
        mine = (ids >= 0) & (ids < blocks)
        lowest = jnp.min(jnp.where(mine, ids, blocks - 1))
        highest = jnp.max(jnp.where(mine, ids, 0))
        block = jnp.where(place_ref[1] == 0, lowest, highest)
        rows = pl.ds(pl.multiple_of(block * tile, tile), tile)
        for half, source in enumerate((own, sib)):
            copy = pltpu.make_async_copy(
                source.at[rows, :], outs[index].at[half], sems.at[index, half]
            )
            copy.start()
            copies.append(copy)
    for copy in copies:
        copy.wait()


def pick(place, asks, own, sib, tile):
    blocks, bands = asks[0].shape[0], own.shape[1]
    count = len(asks)
    return pl.pallas_call(
        functools.partial(pick_kernel, count, blocks, tile),
        out_shape=[jax.ShapeDtypeStruct((2, tile, bands), own.dtype)] * count,
        in_specs=[pl.BlockSpec(memory_space=pltpu.SMEM)]
        + [pl.BlockSpec(memory_space=pltpu.VMEM)] * count
        + [pl.BlockSpec(memory_space=pl.ANY)] * 2,
        out_specs=[pl.BlockSpec(memory_space=pl.ANY)] * count,
        scratch_shapes=[pltpu.SemaphoreType.DMA((count, 2))],
        name="pick_blocks",
        cost_estimate=pl.CostEstimate(
            flops=0, bytes_accessed=8 * count * tile * bands, transcendentals=0
        ),
    )(place, *asks, own, sib)


def tiles_kernel(n_right, n_strips, tile, place_ref, *refs):
    own, sib = refs[:2]
    rights = refs[2:4]
    weights = refs[4:6]
    outs = refs[6 : 6 + n_strips]
    scaled, total = refs[6 + n_strips :]
    strip = tile // n_strips
    n_left = own.shape[0] // tile

    @pl.when(pl.program_id(0) == 0)
    def _():
        for j in range(n_right):
            for half in range(2):
                block = rights[half][j * tile : (j + 1) * tile, :].astype(jnp.float32)
                for kind in range(2):
                    value = block * weights[half][kind : kind + 1, :]
                    scaled[j, half, kind * tile : (kind + 1) * tile, :] = value.astype(
                        scaled.dtype
                    )

    for j in range(n_right):
        contract = (((1,), (1,)), ((), ()))
        value = lax.dot_general(
            own[...], scaled[j, 0], contract, preferred_element_type=jnp.float32
        )
        value += lax.dot_general(
            sib[...], scaled[j, 1], contract, preferred_element_type=jnp.float32
        )
        total[...] = value
        for index in range(n_strips):
            start = place_ref[2 + index] * strip
            for i in range(n_left):
                rows = pl.ds(pl.multiple_of(i * tile + start, strip), strip)
                outs[index][j, i] = total[rows, :].astype(outs[index].dtype)


def tiles(place, own, sib, arrived, weights, n_strips, tile, step_blocks):
    rows, bands = own.shape
    n_right = rows // tile // 2 if arrived is None else 1
    blocks = rows // tile
    steps = blocks // step_blocks
    strip = tile // n_strips
    left = pl.BlockSpec((step_blocks * tile, bands), lambda i, place: (i, 0))
    if arrived is None:
        rights = [own, sib]
        right = pl.BlockSpec((n_right * tile, bands), lambda i, place: (place[1], 0))
        right_specs = [right, right]
    else:
        rights = [arrived, arrived]
        right_specs = [
            pl.BlockSpec((None, tile, bands), lambda i, place: (0, 0, 0)),
            pl.BlockSpec((None, tile, bands), lambda i, place: (1, 0, 0)),
        ]
    weight = pl.BlockSpec((2, bands), lambda i, place: (0, 0))
    return pl.pallas_call(
        functools.partial(tiles_kernel, n_right, n_strips, tile),
        out_shape=[
            jax.ShapeDtypeStruct((n_right, blocks, strip, 2 * tile), jnp.bfloat16)
        ]
        * n_strips,
        grid_spec=pltpu.PrefetchScalarGridSpec(
            num_scalar_prefetch=1,
            grid=(steps,),
            in_specs=[left, left] + right_specs + [weight, weight],
            out_specs=[
                pl.BlockSpec(
                    (n_right, step_blocks, strip, 2 * tile),
                    lambda i, place: (0, i, 0, 0),
                )
            ]
            * n_strips,
            scratch_shapes=[
                pltpu.VMEM((n_right, 2, 2 * tile, bands), jnp.bfloat16),
                pltpu.VMEM((step_blocks * tile, 2 * tile), jnp.float32),
            ],
        ),
        name="tiles",
        compiler_params=pltpu.CompilerParams(vmem_limit_bytes=VMEM_LIMIT),
        cost_estimate=pl.CostEstimate(
            flops=2 * rows * (n_right * 2 * tile) * 2 * bands,
            bytes_accessed=4 * rows * bands + 4 * n_right * tile * bands,
            transcendentals=0,
        ),
    )(place, own, sib, *rights, *weights)


def place_kernel(chips, sizes, tile, where_ref, *refs):
    n_chunks = len(sizes)
    per_core = sum(sizes)
    ins = refs[: 2 * chips * n_chunks]
    density, energy, pool = refs[2 * chips * n_chunks :]
    for other_core in range(2):
        first = 0
        for chunk in range(n_chunks):
            for j in range(sizes[chunk]):
                total = None
                for step in range(chips):
                    ref = ins[(step * 2 + other_core) * n_chunks + chunk]
                    value = ref[j, 0].astype(jnp.float32)
                    total = value if total is None else total + value
                pool[other_core * per_core + first + j] = total
            first += sizes[chunk]
    i = pl.program_id(0)
    for slot in range(density.shape[1]):
        where = where_ref[i, slot]
        density[0, slot] = pool[where, :, :tile]
        energy[0, slot] = pool[where, :, tile:]


def place_tiles(where, strips, chips, tile):
    sizes = [value.shape[0] for value in strips[0]]
    _, blocks, strip, width = strips[0][0].shape
    slots = where.shape[1]
    out = jax.ShapeDtypeStruct((blocks, slots, strip, tile), jnp.float32)
    flat = [value for group in strips for value in group]
    return pl.pallas_call(
        functools.partial(place_kernel, chips, sizes, tile),
        out_shape=[out, out],
        grid_spec=pltpu.PrefetchScalarGridSpec(
            num_scalar_prefetch=1,
            grid=(blocks,),
            in_specs=[
                pl.BlockSpec(
                    (value.shape[0], 1, strip, width), lambda i, where: (0, i, 0, 0)
                )
                for value in flat
            ],
            out_specs=[
                pl.BlockSpec((1, slots, strip, tile), lambda i, where: (i, 0, 0, 0))
            ]
            * 2,
            scratch_shapes=[pltpu.VMEM((2 * sum(sizes), strip, width), jnp.float32)],
        ),
        name="place_tiles",
        compiler_params=pltpu.CompilerParams(vmem_limit_bytes=VMEM_LIMIT),
        cost_estimate=pl.CostEstimate(
            flops=0,
            bytes_accessed=sum(2 * value.size for value in flat)
            + 8 * blocks * slots * strip * tile,
            transcendentals=0,
        ),
    )(where, *flat)


def body(eigvecs, occupations, energies, neighbours):
    n_atoms = lax.axis_size("atoms")
    n_bands = lax.axis_size("bands")
    chips = n_bands // 2
    own_index = lax.axis_index("atoms").astype(jnp.int32)
    group = lax.axis_index("bands").astype(jnp.int32)
    core = group & 1
    blocks = neighbours.shape[0]
    tile = eigvecs.shape[0] // blocks
    half_blocks = blocks // 2
    offsets = [-1, 1, 2, -2]

    asks = [shifted(neighbours, "atoms", offset) for offset in offsets]
    sib = to_strip_target(eigvecs, chips, 0, 1)
    own_weights = jnp.stack([occupations, occupations * energies], 0)
    sib_weights = to_strip_target(own_weights, chips, 0, 1)
    weights = (own_weights, sib_weights)

    targets = [
        strip_target(group, chips, step, other)
        for step in range(chips)
        for other in range(2)
    ]
    place = jnp.stack([own_index, core] + targets).astype(jnp.int32)

    near = pick(place, asks[:2], eigvecs, sib, tile)
    far = pick(place, asks[2:], eigvecs, sib, tile)
    arrived = [
        shifted(value, "atoms", -offset)
        for value, offset in zip(list(near) + list(far), offsets)
    ]

    def exchanged(parts):
        return [
            part if index == 0 else to_strip_target(part, chips, index // 2, index % 2)
            for index, part in enumerate(parts)
        ]

    chunks = [
        exchanged(
            tiles(place, eigvecs, sib, None, weights, n_bands, tile, 2)
        )
    ]
    for value in arrived:
        chunks.append(
            exchanged(
                tiles(place, eigvecs, sib, value, weights, n_bands, tile, 2)
            )
        )
    strips = [[chunk[index] for chunk in chunks] for index in range(n_bands)]

    owners = neighbours // blocks
    within = neighbours % blocks
    distance = (owners - own_index) % n_atoms
    spot = within % half_blocks
    side = within // half_blocks
    for index, offset in enumerate(offsets):
        from_it = distance == offset % n_atoms
        highest = jnp.max(jnp.where(from_it, within, -1))
        side = jnp.where(from_it, (within == highest).astype(jnp.int32), side)
        spot = jnp.where(from_it, half_blocks + index, spot)
    per_core = half_blocks + len(offsets)
    where = ((side + core) % 2) * per_core + spot
    density, energy = place_tiles(where.astype(jnp.int32), strips, chips, tile)
    return density, energy


def solution(mesh):
    return jax.shard_map(
        body,
        mesh=mesh,
        in_specs=(P("atoms", "bands"), P("bands"), P("bands"), P("atoms", None)),
        out_specs=(P("atoms", None, "bands", None), P("atoms", None, "bands", None)),
        check_vma=False,
    )
```

```python
import functools

import jax
import jax.numpy as jnp
from jax import lax
from jax.experimental import pallas as pl
from jax.experimental.pallas import tpu as pltpu
from jax.sharding import PartitionSpec as P

R = 2
VMEM_LIMIT = 40 * 1024 * 1024


def shifted(value, axis, steps):
    count = lax.axis_size(axis)
    pairs = [(source, (source + steps) % count) for source in range(count)]
    return lax.ppermute(value, axis, pairs)


def strip_target(group, chips, step, other_core):
    chip = lax.rem(lax.shift_right_logical(group, 1) + step, chips)
    return chip * 2 + ((group & 1) ^ other_core)


def to_strip_target(value, chips, step, other_core):
    pairs = [
        (group, (group // 2 + step) % chips * 2 + (group % 2 ^ other_core))
        for group in range(2 * chips)
    ]
    return lax.ppermute(value, "bands", pairs)


def pick_kernel(count, blocks, tile, place_ref, *refs):
    asks, (own, sib), outs = refs[:count], refs[count : count + 2], refs[count + 2 : -1]
    sems = refs[-1]
    first = place_ref[0] * blocks
    copies = []
    for index in range(count):
        ids = asks[index][...] - first
        mine = (ids >= 0) & (ids < blocks)
        lowest = jnp.min(jnp.where(mine, ids, blocks - 1))
        highest = jnp.max(jnp.where(mine, ids, 0))
        block = jnp.where(place_ref[1] == 0, lowest, highest)
        rows = pl.ds(pl.multiple_of(block * tile, tile), tile)
        for half, source in enumerate((own, sib)):
            copy = pltpu.make_async_copy(
                source.at[rows, :], outs[index].at[half], sems.at[index, half]
            )
            copy.start()
            copies.append(copy)
    for copy in copies:
        copy.wait()


def pick(place, asks, own, sib, tile):
    blocks, bands = asks[0].shape[0], own.shape[1]
    count = len(asks)
    return pl.pallas_call(
        functools.partial(pick_kernel, count, blocks, tile),
        out_shape=[jax.ShapeDtypeStruct((2, tile, bands), own.dtype)] * count,
        in_specs=[pl.BlockSpec(memory_space=pltpu.SMEM)]
        + [pl.BlockSpec(memory_space=pltpu.VMEM)] * count
        + [pl.BlockSpec(memory_space=pl.ANY)] * 2,
        out_specs=[pl.BlockSpec(memory_space=pltpu.VMEM)] * count,
        scratch_shapes=[pltpu.SemaphoreType.DMA((count, 2))],
        name="pick_blocks",
        compiler_params=pltpu.CompilerParams(vmem_limit_bytes=VMEM_LIMIT),
        cost_estimate=pl.CostEstimate(
            flops=0, bytes_accessed=8 * count * tile * bands, transcendentals=0
        ),
    )(place, *asks, own, sib)


def tiles_kernel(n_right, n_strips, tile, local, place_ref, *refs):
    own, sib, own_weight, sib_weight = refs[:4]
    refs = refs[4:]
    arrived = None
    if not local:
        arrived, refs = refs[0], refs[1:]
    outs, (scaled, total) = refs[:n_strips], refs[n_strips:]
    strip = tile // n_strips
    n_left = own.shape[0] // tile
    step, n_steps = pl.program_id(0), pl.num_programs(0)

    @pl.when(step == 0)
    def _():
        total[...] = jnp.zeros_like(total)

    def add(left, weight):
        for j in range(n_right):
            if local:
                first = pl.multiple_of((place_ref[1] * n_right + j) * tile, tile)
                block = left[pl.ds(first, tile), :]
            else:
                block = arrived[0]
            block = block.astype(jnp.float32)
            for kind in range(2):
                rows = pl.ds((2 * j + kind) * tile, tile)
                scaled[rows, :] = (block * weight[kind : kind + 1, :]).astype(scaled.dtype)
        total[...] += lax.dot_general(
            left[...],
            scaled[...],
            (((1,), (1,)), ((), ())),
            preferred_element_type=jnp.float32,
        )

    @pl.when(step < n_steps // 2)
    def _():
        add(own, own_weight)

    @pl.when(step >= n_steps // 2)
    def _():
        add(sib, sib_weight)

    @pl.when(step == n_steps - 1)
    def _():
        for index in range(n_strips):
            start = place_ref[2 + index] * strip
            for i in range(n_left):
                rows = pl.ds(pl.multiple_of(i * tile + start, strip), strip)
                for j in range(n_right):
                    value = total[rows, 2 * tile * j : 2 * tile * (j + 1)]
                    outs[index][j, i] = value.astype(outs[index].dtype)


def tiles(place, own, sib, arrived, weights, n_strips, tile):
    rows, bands = own.shape
    local = arrived is None
    blocks = rows // tile
    n_right = blocks // 2 if local else 1
    strip = tile // n_strips
    depth = min(bands, 1024 if local else 512)
    steps = bands // depth
    width = n_right * 2 * tile

    def first_half(s, place):
        return 0, jnp.minimum(s, steps - 1)

    def second_half(s, place):
        return 0, jnp.maximum(s - steps, 0)

    in_specs = [
        pl.BlockSpec((rows, depth), first_half),
        pl.BlockSpec((rows, depth), second_half),
        pl.BlockSpec((2, depth), first_half),
        pl.BlockSpec((2, depth), second_half),
    ]
    operands = [own, sib, *weights]
    if not local:
        in_specs.append(
            pl.BlockSpec(
                (1, tile, depth),
                lambda s, place: (lax.div(s, steps), 0, lax.rem(s, steps)),
            )
        )
        operands.append(arrived)
    return pl.pallas_call(
        functools.partial(tiles_kernel, n_right, n_strips, tile, local),
        out_shape=[
            jax.ShapeDtypeStruct((n_right, blocks, strip, 2 * tile), jnp.bfloat16)
        ]
        * n_strips,
        grid_spec=pltpu.PrefetchScalarGridSpec(
            num_scalar_prefetch=1,
            grid=(2 * steps,),
            in_specs=in_specs,
            out_specs=[
                pl.BlockSpec(
                    (n_right, blocks, strip, 2 * tile), lambda s, place: (0, 0, 0, 0)
                )
            ]
            * n_strips,
            scratch_shapes=[
                pltpu.VMEM((width, depth), jnp.bfloat16),
                pltpu.VMEM((rows, width), jnp.float32),
            ],
        ),
        name="tiles",
        compiler_params=pltpu.CompilerParams(vmem_limit_bytes=VMEM_LIMIT),
        cost_estimate=pl.CostEstimate(
            flops=2 * rows * width * 2 * bands,
            bytes_accessed=4 * rows * bands + 4 * tile * bands,
            transcendentals=0,
        ),
    )(place, *operands)


def place_kernel(chips, sizes, tile, where_ref, *refs):
    n_chunks = len(sizes)
    per_core = sum(sizes)
    ins = refs[: 2 * chips * n_chunks]
    density, energy, pool = refs[2 * chips * n_chunks :]
    for other_core in range(2):
        first = 0
        for chunk in range(n_chunks):
            for j in range(sizes[chunk]):
                total = None
                for step in range(chips):
                    ref = ins[(step * 2 + other_core) * n_chunks + chunk]
                    value = ref[j, 0].astype(jnp.float32)
                    total = value if total is None else total + value
                pool[other_core * per_core + first + j] = total
            first += sizes[chunk]
    i = pl.program_id(0)
    for slot in range(density.shape[1]):
        where = where_ref[i, slot]
        density[0, slot] = pool[where, :, :tile]
        energy[0, slot] = pool[where, :, tile:]


def place_tiles(where, strips, chips, tile):
    sizes = [value.shape[0] for value in strips[0]]
    _, blocks, strip, width = strips[0][0].shape
    slots = where.shape[1]
    out = jax.ShapeDtypeStruct((blocks, slots, strip, tile), jnp.float32)
    flat = [value for group in strips for value in group]
    return pl.pallas_call(
        functools.partial(place_kernel, chips, sizes, tile),
        out_shape=[out, out],
        grid_spec=pltpu.PrefetchScalarGridSpec(
            num_scalar_prefetch=1,
            grid=(blocks,),
            in_specs=[
                pl.BlockSpec(
                    (value.shape[0], 1, strip, width), lambda i, where: (0, i, 0, 0)
                )
                for value in flat
            ],
            out_specs=[
                pl.BlockSpec((1, slots, strip, tile), lambda i, where: (i, 0, 0, 0))
            ]
            * 2,
            scratch_shapes=[pltpu.VMEM((2 * sum(sizes), strip, width), jnp.float32)],
        ),
        name="place_tiles",
        compiler_params=pltpu.CompilerParams(vmem_limit_bytes=VMEM_LIMIT),
        cost_estimate=pl.CostEstimate(
            flops=0,
            bytes_accessed=sum(2 * value.size for value in flat)
            + 8 * blocks * slots * strip * tile,
            transcendentals=0,
        ),
    )(where, *flat)


def body(eigvecs, occupations, energies, neighbours):
    n_atoms = lax.axis_size("atoms")
    n_bands = lax.axis_size("bands")
    chips = n_bands // 2
    own_index = lax.axis_index("atoms").astype(jnp.int32)
    group = lax.axis_index("bands").astype(jnp.int32)
    core = group & 1
    blocks = neighbours.shape[0]
    tile = eigvecs.shape[0] // blocks
    half_blocks = blocks // 2
    offsets = [-1, 1, 2, -2]

    asks = [shifted(neighbours, "atoms", offset) for offset in offsets]
    sib = to_strip_target(eigvecs, chips, 0, 1)
    own_weights = jnp.stack([occupations, occupations * energies], 0)
    sib_weights = to_strip_target(own_weights, chips, 0, 1)
    weights = (own_weights, sib_weights)

    targets = [
        strip_target(group, chips, step, other)
        for step in range(chips)
        for other in range(2)
    ]
    place = jnp.stack([own_index, core] + targets).astype(jnp.int32)

    picked = pick(place, asks, eigvecs, sib, tile)
    arrived = [
        shifted(value, "atoms", -offset)
        for value, offset in zip(picked[:3], offsets[:3])
    ]
    *arrived[:2], last = lax.optimization_barrier((*arrived[:2], picked[3]))
    arrived.append(shifted(last, "atoms", -offsets[3]))

    owners = lax.div(neighbours, blocks)
    within = lax.rem(neighbours, blocks)
    distance = lax.rem(owners - own_index + n_atoms, n_atoms)
    spot = lax.rem(within, half_blocks)
    side = lax.div(within, half_blocks)
    for index, offset in enumerate(offsets):
        from_it = distance == offset % n_atoms
        highest = jnp.max(jnp.where(from_it, within, -1))
        side = jnp.where(from_it, (within == highest).astype(jnp.int32), side)
        spot = jnp.where(from_it, half_blocks + index, spot)
    per_core = half_blocks + len(offsets)
    where = (side ^ core) * per_core + spot
    where, place = lax.optimization_barrier((where.astype(jnp.int32), place))

    def exchanged(parts):
        return [
            part if index == 0 else to_strip_target(part, chips, index // 2, index % 2)
            for index, part in enumerate(parts)
        ]

    chunks = [
        exchanged(
            tiles(place, eigvecs, sib, None, weights, n_bands, tile)
        )
    ]
    for value in arrived:
        chunks.append(
            exchanged(
                tiles(place, eigvecs, sib, value, weights, n_bands, tile)
            )
        )
    strips = [[chunk[index] for chunk in chunks] for index in range(n_bands)]

    density, energy = place_tiles(where, strips, chips, tile)
    return density, energy


def solution(mesh):
    return jax.shard_map(
        body,
        mesh=mesh,
        in_specs=(P("atoms", "bands"), P("bands"), P("bands"), P("atoms", None)),
        out_specs=(P("atoms", None, "bands", None), P("atoms", None, "bands", None)),
        check_vma=False,
    )
```

```python
import functools

import jax
import jax.numpy as jnp
from jax import lax
from jax.experimental import pallas as pl
from jax.experimental.pallas import tpu as pltpu
from jax.sharding import PartitionSpec as P

R = 2
VMEM_LIMIT = 24 * 1024 * 1024
PICK_VMEM_LIMIT = 24 * 1024 * 1024


def shifted(value, axis, steps):
    count = lax.axis_size(axis)
    pairs = [(source, (source + steps) % count) for source in range(count)]
    return lax.ppermute(value, axis, pairs)


def strip_target(group, chips, step, other_core):
    chip = lax.rem(lax.shift_right_logical(group, 1) + step, chips)
    return chip * 2 + ((group & 1) ^ other_core)


def to_strip_target(value, chips, step, other_core):
    pairs = [
        (group, (group // 2 + step) % chips * 2 + (group % 2 ^ other_core))
        for group in range(2 * chips)
    ]
    return lax.ppermute(value, "bands", pairs)


def pick_kernel(count, blocks, tile, place_ref, *refs):
    asks, (own, sib), outs = refs[:count], refs[count : count + 2], refs[count + 2 : -1]
    sems = refs[-1]
    first = place_ref[0] * blocks
    copies = []
    for index in range(count):
        ids = asks[index][...] - first
        mine = (ids >= 0) & (ids < blocks)
        lowest = jnp.min(jnp.where(mine, ids, blocks - 1))
        highest = jnp.max(jnp.where(mine, ids, 0))
        block = jnp.where(place_ref[1] == 0, lowest, highest)
        rows = pl.ds(pl.multiple_of(block * tile, tile), tile)
        for half, source in enumerate((own, sib)):
            copy = pltpu.make_async_copy(
                source.at[rows, :], outs[index].at[half], sems.at[index, half]
            )
            copy.start()
            copies.append(copy)
    if len(outs) > count:
        copy = pltpu.make_async_copy(own, outs[count], sems.at[count, 0])
        copy.start()
        copies.append(copy)
    for copy in copies:
        copy.wait()


def pick(place, asks, own, sib, tile, keep_own):
    blocks, bands = asks[0].shape[0], own.shape[1]
    count = len(asks)
    out_shape = [jax.ShapeDtypeStruct((2, tile, bands), own.dtype)] * count
    if keep_own:
        out_shape.append(jax.ShapeDtypeStruct(own.shape, own.dtype))
    return pl.pallas_call(
        functools.partial(pick_kernel, count, blocks, tile),
        out_shape=out_shape,
        in_specs=[pl.BlockSpec(memory_space=pltpu.SMEM)]
        + [pl.BlockSpec(memory_space=pltpu.VMEM)] * count
        + [pl.BlockSpec(memory_space=pl.ANY)] * 2,
        out_specs=[pl.BlockSpec(memory_space=pltpu.VMEM)] * len(out_shape),
        scratch_shapes=[pltpu.SemaphoreType.DMA((count + 1, 2))],
        name="pick_blocks",
        compiler_params=pltpu.CompilerParams(vmem_limit_bytes=PICK_VMEM_LIMIT),
        cost_estimate=pl.CostEstimate(
            flops=0, bytes_accessed=8 * count * tile * bands, transcendentals=0
        ),
    )(place, *asks, own, sib)


def tiles_kernel(n_arrived, n_right, n_strips, tile, place_ref, *refs):
    lefts, weights = refs[:2], refs[2:4]
    arrived, refs = refs[4 : 4 + n_arrived], refs[4 + n_arrived :]
    outs, (scaled, total) = refs[:n_strips], refs[n_strips:]
    strip = tile // n_strips
    n_left = lefts[0].shape[0] // tile
    for j in range(n_right):
        slot = j % 2
        for half in range(2):
            if n_arrived:
                block = arrived[j][half]
            else:
                first = pl.multiple_of((place_ref[0] * n_right + j) * tile, tile)
                block = lefts[half][pl.ds(first, tile), :]
            block = block.astype(jnp.float32)
            for kind in range(2):
                value = block * weights[half][kind : kind + 1, :]
                rows = pl.ds(kind * tile, tile)
                scaled[slot, half, rows, :] = value.astype(scaled.dtype)
        for half in range(2):
            value = lax.dot_general(
                lefts[half][...],
                scaled[slot, half],
                (((1,), (1,)), ((), ())),
                preferred_element_type=jnp.float32,
            )
            if half == 0:
                total[slot] = value
            else:
                total[slot] += value
        for index in range(n_strips):
            start = place_ref[1 + index] * strip
            for i in range(n_left):
                rows = pl.ds(pl.multiple_of(i * tile + start, strip), strip)
                outs[index][j, i] = total[slot, rows, :].astype(outs[index].dtype)


def tiles(place, own, sib, arrived, weights, n_strips, tile):
    rows, bands = own.shape
    blocks = rows // tile
    n_right = len(arrived) if arrived else blocks // 2
    strip = tile // n_strips
    slots = min(n_right, 2)
    vmem = pl.BlockSpec(memory_space=pltpu.VMEM)
    return pl.pallas_call(
        functools.partial(tiles_kernel, len(arrived), n_right, n_strips, tile),
        out_shape=[
            jax.ShapeDtypeStruct((n_right, blocks, strip, 2 * tile), jnp.bfloat16)
        ]
        * n_strips,
        in_specs=[pl.BlockSpec(memory_space=pltpu.SMEM)] + [vmem] * (4 + len(arrived)),
        out_specs=[vmem] * n_strips,
        scratch_shapes=[
            pltpu.VMEM((slots, 2, 2 * tile, bands), jnp.bfloat16),
            pltpu.VMEM((slots, rows, 2 * tile), jnp.float32),
        ],
        name="tiles",
        compiler_params=pltpu.CompilerParams(vmem_limit_bytes=VMEM_LIMIT),
        cost_estimate=pl.CostEstimate(
            flops=2 * rows * n_right * 2 * tile * 2 * bands,
            bytes_accessed=4 * rows * bands + 4 * n_right * tile * bands,
            transcendentals=0,
        ),
    )(place, own, sib, *weights, *arrived)


def place_kernel(chips, sizes, tile, where_ref, *refs):
    n_chunks = len(sizes)
    per_core = sum(sizes)
    ins = refs[: 2 * chips * n_chunks]
    density, energy, pool = refs[2 * chips * n_chunks :]
    for other_core in range(2):
        first = 0
        for chunk in range(n_chunks):
            for j in range(sizes[chunk]):
                total = None
                for step in range(chips):
                    ref = ins[(step * 2 + other_core) * n_chunks + chunk]
                    value = ref[j, 0].astype(jnp.float32)
                    total = value if total is None else total + value
                pool[other_core * per_core + first + j] = total
            first += sizes[chunk]
    i = pl.program_id(0)
    for slot in range(density.shape[1]):
        where = where_ref[i, slot]
        density[0, slot] = pool[where, :, :tile]
        energy[0, slot] = pool[where, :, tile:]


def place_tiles(where, strips, chips, tile):
    sizes = [value.shape[0] for value in strips[0]]
    _, blocks, strip, width = strips[0][0].shape
    slots = where.shape[1]
    out = jax.ShapeDtypeStruct((blocks, slots, strip, tile), jnp.float32)
    flat = [value for group in strips for value in group]
    return pl.pallas_call(
        functools.partial(place_kernel, chips, sizes, tile),
        out_shape=[out, out],
        grid_spec=pltpu.PrefetchScalarGridSpec(
            num_scalar_prefetch=1,
            grid=(blocks,),
            in_specs=[
                pl.BlockSpec(
                    (value.shape[0], 1, strip, width), lambda i, where: (0, i, 0, 0)
                )
                for value in flat
            ],
            out_specs=[
                pl.BlockSpec((1, slots, strip, tile), lambda i, where: (i, 0, 0, 0))
            ]
            * 2,
            scratch_shapes=[pltpu.VMEM((2 * sum(sizes), strip, width), jnp.float32)],
        ),
        name="place_tiles",
        compiler_params=pltpu.CompilerParams(vmem_limit_bytes=VMEM_LIMIT),
        cost_estimate=pl.CostEstimate(
            flops=0,
            bytes_accessed=sum(2 * value.size for value in flat)
            + 8 * blocks * slots * strip * tile,
            transcendentals=0,
        ),
    )(where, *flat)


def body(eigvecs, occupations, energies, neighbours):
    n_atoms = lax.axis_size("atoms")
    n_bands = lax.axis_size("bands")
    chips = n_bands // 2
    own_index = lax.axis_index("atoms").astype(jnp.int32)
    group = lax.axis_index("bands").astype(jnp.int32)
    core = group & 1
    blocks = neighbours.shape[0]
    tile = eigvecs.shape[0] // blocks
    half_blocks = blocks // 2
    offsets = [-1, 1, 2, -2]

    asks = [shifted(neighbours, "atoms", offset) for offset in offsets]
    sib = to_strip_target(eigvecs, chips, 0, 1)
    own_weights = jnp.stack([occupations, occupations * energies], 0)
    sib_weights = to_strip_target(own_weights, chips, 0, 1)
    weights = (own_weights, sib_weights)

    targets = [
        strip_target(group, chips, step, other)
        for step in range(chips)
        for other in range(2)
    ]
    here = jnp.stack([own_index, core]).astype(jnp.int32)
    place = jnp.stack([core] + targets).astype(jnp.int32)

    near = list(pick(here, asks[:2], eigvecs, sib, tile, False))
    here, near[0] = lax.optimization_barrier((here, near[0]))
    far = list(pick(here, asks[2:], eigvecs, sib, tile, True))
    own = far.pop()
    near = [shifted(near[0], "atoms", -offsets[0]), shifted(near[1], "atoms", -offsets[1])]
    third = shifted(far[0], "atoms", -offsets[2])

    owners = lax.div(neighbours, blocks)
    within = lax.rem(neighbours, blocks)
    distance = lax.rem(owners - own_index + n_atoms, n_atoms)
    spot = lax.rem(within, half_blocks)
    side = lax.div(within, half_blocks)
    for index, offset in enumerate(offsets):
        from_it = distance == offset % n_atoms
        highest = jnp.max(jnp.where(from_it, within, -1))
        side = jnp.where(from_it, (within == highest).astype(jnp.int32), side)
        spot = jnp.where(from_it, half_blocks + index, spot)
    per_core = half_blocks + len(offsets)
    where = (side ^ core) * per_core + spot
    where, place = lax.optimization_barrier((where.astype(jnp.int32), place))

    def exchanged(parts):
        return [
            part if index == 0 else to_strip_target(part, chips, index // 2, index % 2)
            for index, part in enumerate(parts)
        ]

    def strips_of(*arrived):
        return exchanged(tiles(place, own, sib, arrived, weights, n_bands, tile))

    chunks = [strips_of()]
    *near, source, chunks[0][:3] = lax.optimization_barrier(
        (*near, far[1], chunks[0][:3])
    )
    fourth = shifted(source, "atoms", -offsets[3])
    chunks.append(strips_of(*near))
    third, chunks[1][0] = lax.optimization_barrier((third, chunks[1][0]))
    chunks.append(strips_of(third))
    fourth, chunks[1], chunks[2][:3] = lax.optimization_barrier((fourth, chunks[1], chunks[2][:3]))
    chunks.append(strips_of(fourth))
    strips = [[chunk[index] for chunk in chunks] for index in range(n_bands)]

    density, energy = place_tiles(where, strips, chips, tile)
    return density, energy


def solution(mesh):
    return jax.shard_map(
        body,
        mesh=mesh,
        in_specs=(P("atoms", "bands"), P("bands"), P("bands"), P("atoms", None)),
        out_specs=(P("atoms", None, "bands", None), P("atoms", None, "bands", None)),
        check_vma=False,
    )
```

```python
import functools

import jax
import jax.numpy as jnp
from jax import lax
from jax.experimental import pallas as pl
from jax.experimental.pallas import tpu as pltpu
from jax.sharding import PartitionSpec as P

R = 2
VMEM_LIMIT = 24 * 1024 * 1024
SOON = pl.CostEstimate(flops=0, bytes_accessed=0, transcendentals=0)


def shifted(value, axis, steps):
    count = lax.axis_size(axis)
    pairs = [(source, (source + steps) % count) for source in range(count)]
    return lax.ppermute(value, axis, pairs)


def strip_target(group, chips, step, other_core):
    chip = lax.rem(lax.shift_right_logical(group, 1) + step, chips)
    return chip * 2 + ((group & 1) ^ other_core)


def to_strip_target(value, chips, step, other_core):
    pairs = [
        (group, (group // 2 + step) % chips * 2 + (group % 2 ^ other_core))
        for group in range(2 * chips)
    ]
    return lax.ppermute(value, "bands", pairs)


def pick_kernel(count, blocks, tile, place_ref, *refs):
    asks, (own, sib), outs = refs[:count], refs[count : count + 2], refs[count + 2 : -1]
    sems = refs[-1]
    first = place_ref[0] * blocks
    copies = []
    for index in range(count):
        ids = asks[index][...] - first
        mine = (ids >= 0) & (ids < blocks)
        lowest = jnp.min(jnp.where(mine, ids, blocks - 1))
        highest = jnp.max(jnp.where(mine, ids, 0))
        block = jnp.where(place_ref[1] == 0, lowest, highest)
        rows = pl.ds(pl.multiple_of(block * tile, tile), tile)
        for half, source in enumerate((own, sib)):
            copy = pltpu.make_async_copy(
                source.at[rows, :], outs[index].at[half], sems.at[index, half]
            )
            copy.start()
            copies.append(copy)
    for copy in copies:
        copy.wait()


def pick(place, asks, own, sib, tile):
    blocks, bands = asks[0].shape[0], own.shape[1]
    count = len(asks)
    out_shape = [jax.ShapeDtypeStruct((2, tile, bands), own.dtype)] * count
    return pl.pallas_call(
        functools.partial(pick_kernel, count, blocks, tile),
        out_shape=out_shape,
        in_specs=[pl.BlockSpec(memory_space=pltpu.SMEM)]
        + [pl.BlockSpec(memory_space=pltpu.VMEM)] * count
        + [pl.BlockSpec(memory_space=pl.ANY)] * 2,
        out_specs=[pl.BlockSpec(memory_space=pltpu.VMEM)] * len(out_shape),
        scratch_shapes=[pltpu.SemaphoreType.DMA((count, 2))],
        name="pick_blocks",
        compiler_params=pltpu.CompilerParams(vmem_limit_bytes=VMEM_LIMIT),
        cost_estimate=SOON,
    )(place, *asks, own, sib)


def tiles_kernel(n_arrived, n_right, n_strips, tile, place_ref, *refs):
    lefts, weights = refs[:2], refs[2:4]
    arrived, refs = refs[4 : 4 + n_arrived], refs[4 + n_arrived :]
    outs, (scaled, total) = refs[:n_strips], refs[n_strips:]
    strip = tile // n_strips
    n_left = lefts[0].shape[0] // tile
    for j in range(n_right):
        slot = j % 2
        for half in range(2):
            if n_arrived:
                block = arrived[j][half]
            else:
                first = pl.multiple_of((place_ref[0] * n_right + j) * tile, tile)
                block = lefts[half][pl.ds(first, tile), :]
            block = block.astype(jnp.float32)
            for kind in range(2):
                value = block * weights[half][kind : kind + 1, :]
                rows = pl.ds(kind * tile, tile)
                scaled[slot, half, rows, :] = value.astype(scaled.dtype)
        for half in range(2):
            value = lax.dot_general(
                lefts[half][...],
                scaled[slot, half],
                (((1,), (1,)), ((), ())),
                preferred_element_type=jnp.float32,
            )
            if half == 0:
                total[slot] = value
            else:
                total[slot] += value
        for index in range(n_strips):
            start = place_ref[1 + index] * strip
            for i in range(n_left):
                rows = pl.ds(pl.multiple_of(i * tile + start, strip), strip)
                outs[index][j, i] = total[slot, rows, :].astype(outs[index].dtype)


def tiles(place, own, sib, arrived, weights, n_strips, tile):
    rows, bands = own.shape
    blocks = rows // tile
    n_right = len(arrived) if arrived else blocks // 2
    strip = tile // n_strips
    slots = min(n_right, 2)
    vmem = pl.BlockSpec(memory_space=pltpu.VMEM)
    return pl.pallas_call(
        functools.partial(tiles_kernel, len(arrived), n_right, n_strips, tile),
        out_shape=[
            jax.ShapeDtypeStruct((n_right, blocks, strip, 2 * tile), jnp.bfloat16)
        ]
        * n_strips,
        in_specs=[pl.BlockSpec(memory_space=pltpu.SMEM)] + [vmem] * (4 + len(arrived)),
        out_specs=[vmem] * n_strips,
        scratch_shapes=[
            pltpu.VMEM((slots, 2, 2 * tile, bands), jnp.bfloat16),
            pltpu.VMEM((slots, rows, 2 * tile), jnp.float32),
        ],
        name="tiles",
        compiler_params=pltpu.CompilerParams(vmem_limit_bytes=VMEM_LIMIT),
        cost_estimate=SOON,
    )(place, own, sib, *weights, *arrived)


def strip_sum(ins, chips, n_chunks, other_core, chunk, j, i):
    total = None
    for step in range(chips):
        value = ins[(step * 2 + other_core) * n_chunks + chunk][j, i].astype(jnp.float32)
        total = value if total is None else total + value
    return total


def place_early_kernel(chips, sizes, per_core, tile, where_ref, *refs):
    n_chunks = len(sizes)
    ins = refs[: 2 * chips * n_chunks]
    density, energy, later, pool = refs[2 * chips * n_chunks :]
    for other_core in range(2):
        first = other_core * per_core
        for chunk in range(n_chunks):
            for j in range(sizes[chunk]):
                pool[first + j] = strip_sum(ins, chips, n_chunks, other_core, chunk, j, 0)
            first += sizes[chunk]
    i = pl.program_id(0)
    slots = density.shape[1]

    @pl.when(i == 0)
    def _():
        later[0] = 0

    for slot in range(slots):
        where = where_ref[i, slot]
        density[0, slot] = pool[where, :, :tile]
        energy[0, slot] = pool[where, :, tile:]

        @pl.when(lax.rem(where, per_core) == per_core - 1)
        def _():
            count = later[0] + 1
            later[count] = i * slots + slot
            later[0] = count


def place_early(where, strips, chips, per_core, tile):
    sizes = [value.shape[0] for value in strips[0]]
    _, blocks, strip, width = strips[0][0].shape
    slots = where.shape[1]
    out = jax.ShapeDtypeStruct((blocks, slots, strip, tile), jnp.float32)
    flat = [value for group in strips for value in group]
    return pl.pallas_call(
        functools.partial(place_early_kernel, chips, sizes, per_core, tile),
        out_shape=[out, out, jax.ShapeDtypeStruct((blocks * slots + 1,), jnp.int32)],
        grid_spec=pltpu.PrefetchScalarGridSpec(
            num_scalar_prefetch=1,
            grid=(blocks,),
            in_specs=[
                pl.BlockSpec(
                    (value.shape[0], 1, strip, width), lambda i, where: (0, i, 0, 0)
                )
                for value in flat
            ],
            out_specs=[
                pl.BlockSpec((1, slots, strip, tile), lambda i, where: (i, 0, 0, 0))
            ]
            * 2
            + [pl.BlockSpec(memory_space=pltpu.SMEM)],
            scratch_shapes=[pltpu.VMEM((2 * per_core, strip, width), jnp.float32)],
        ),
        name="place_early",
        compiler_params=pltpu.CompilerParams(vmem_limit_bytes=VMEM_LIMIT),
        cost_estimate=SOON,
    )(where, *flat)


def place_late_kernel(chips, per_core, tile, where_ref, later, *refs):
    ins, refs = refs[: 2 * chips], refs[2 * chips + 2 :]
    density, energy, pool, sems = refs
    blocks, slots = density.shape[:2]
    for other_core in range(2):
        for i in range(blocks):
            total = strip_sum(ins, chips, 1, other_core, 0, 0, i)
            pool[other_core, i, 0] = total[:, :tile]
            pool[other_core, i, 1] = total[:, tile:]
    count = later[0]

    def copies(n):
        entry = jnp.clip(later[n + 1], 0, blocks * slots - 1)
        i, slot = lax.div(entry, slots), lax.rem(entry, slots)
        other_core = jnp.clip(lax.div(where_ref[i, slot], per_core), 0, 1)
        return [
            pltpu.make_async_copy(
                pool.at[other_core, i, kind], out.at[i, slot], sems.at[kind]
            )
            for kind, out in enumerate((density, energy))
        ]

    @pl.loop(0, count)
    def _(n):
        for copy in copies(n):
            copy.start()

    @pl.loop(0, count)
    def _(n):
        for copy in copies(n):
            copy.wait()


def place_late(where, later, strips, density, energy, chips, per_core, tile):
    _, blocks, strip, _ = strips[0].shape
    smem = pl.BlockSpec(memory_space=pltpu.SMEM)
    anywhere = pl.BlockSpec(memory_space=pl.ANY)
    out = jax.ShapeDtypeStruct(density.shape, density.dtype)
    n_strips = len(strips)
    return pl.pallas_call(
        functools.partial(place_late_kernel, chips, per_core, tile),
        out_shape=[out, out],
        in_specs=[smem, smem]
        + [pl.BlockSpec(memory_space=pltpu.VMEM)] * n_strips
        + [anywhere] * 2,
        out_specs=[anywhere] * 2,
        scratch_shapes=[
            pltpu.VMEM((2, blocks, 2, strip, tile), jnp.float32),
            pltpu.SemaphoreType.DMA((2,)),
        ],
        input_output_aliases={2 + n_strips: 0, 3 + n_strips: 1},
        name="place_late",
        compiler_params=pltpu.CompilerParams(vmem_limit_bytes=VMEM_LIMIT),
        cost_estimate=SOON,
    )(where, later, *strips, density, energy)


def body(eigvecs, occupations, energies, neighbours):
    n_atoms = lax.axis_size("atoms")
    n_bands = lax.axis_size("bands")
    chips = n_bands // 2
    own_index = lax.axis_index("atoms").astype(jnp.int32)
    group = lax.axis_index("bands").astype(jnp.int32)
    core = group & 1
    blocks = neighbours.shape[0]
    tile = eigvecs.shape[0] // blocks
    half_blocks = blocks // 2
    offsets = [-1, 1, 2, -2]

    asks = [shifted(neighbours, "atoms", offset) for offset in offsets]
    sib = to_strip_target(eigvecs, chips, 0, 1)
    targets = [
        strip_target(group, chips, step, other)
        for step in range(chips)
        for other in range(2)
    ]
    here = jnp.stack([own_index, core]).astype(jnp.int32)
    place = jnp.stack([core] + targets).astype(jnp.int32)

    near = list(pick(here, asks[:2], eigvecs, sib, tile))
    here, near[0] = lax.optimization_barrier((here, near[0]))
    far = list(pick(here, asks[2:], eigvecs, sib, tile))
    occupations, far[0] = lax.optimization_barrier((occupations, far[0]))
    near = [shifted(near[0], "atoms", -offsets[0]), shifted(near[1], "atoms", -offsets[1])]
    third = shifted(far[0], "atoms", -offsets[2])
    own_weights = jnp.stack([occupations, occupations * energies], 0)
    sib_weights = to_strip_target(own_weights, chips, 0, 1)
    weights = (own_weights, sib_weights)

    def strips_of(*arrived):
        parts = list(tiles(place, eigvecs, sib, arrived, weights, n_bands, tile))
        parts[1] = to_strip_target(parts[1], chips, 0, 1)
        for index in range(2, n_bands):
            if index % 2:
                parts[index], parts[1] = lax.optimization_barrier((parts[index], parts[1]))
            parts[index] = to_strip_target(parts[index], chips, index // 2, index % 2)
        return parts

    chunks = [strips_of()]
    neighbours, chunks[0][0] = lax.optimization_barrier((neighbours, chunks[0][0]))

    owners = lax.div(neighbours, blocks)
    within = lax.rem(neighbours, blocks)
    distance = lax.rem(owners - own_index + n_atoms, n_atoms)
    spot = lax.rem(within, half_blocks)
    side = lax.div(within, half_blocks)
    for index, offset in enumerate(offsets):
        from_it = distance == offset % n_atoms
        highest = jnp.max(jnp.where(from_it, within, -1))
        side = jnp.where(from_it, (within == highest).astype(jnp.int32), side)
        spot = jnp.where(from_it, half_blocks + index, spot)
    per_core = half_blocks + len(offsets)
    where = ((side ^ core) * per_core + spot).astype(jnp.int32)

    near, source, chunks[0][:3] = lax.optimization_barrier((near, far[1], chunks[0][:3]))
    fourth = shifted(source, "atoms", -offsets[3])
    chunks.append(strips_of(*near, third))
    where, fourth, chunks[0], chunks[1][:3] = lax.optimization_barrier(
        (where, fourth, chunks[0], chunks[1][:3])
    )
    last = strips_of(fourth)
    where, last[0] = lax.optimization_barrier((where, last[0]))
    strips = [[chunk[index] for chunk in chunks] for index in range(n_bands)]
    density, energy, later = place_early(where, strips, chips, per_core, tile)
    return place_late(where, later, last, density, energy, chips, per_core, tile)


def solution(mesh):
    return jax.shard_map(
        body,
        mesh=mesh,
        in_specs=(P("atoms", "bands"), P("bands"), P("bands"), P("atoms", None)),
        out_specs=(P("atoms", None, "bands", None), P("atoms", None, "bands", None)),
        check_vma=False,
    )
```

```python
import functools

import jax
import jax.numpy as jnp
from jax import lax
from jax.experimental import pallas as pl
from jax.experimental.pallas import tpu as pltpu
from jax.sharding import PartitionSpec as P

R = 2
VMEM_LIMIT = 24 * 1024 * 1024
SOON = pl.CostEstimate(flops=0, bytes_accessed=0, transcendentals=0)


def shifted(value, axis, steps):
    count = lax.axis_size(axis)
    pairs = [(source, (source + steps) % count) for source in range(count)]
    return lax.ppermute(value, axis, pairs)


def strip_target(group, chips, step, other_core):
    chip = lax.rem(lax.shift_right_logical(group, 1) + step, chips)
    return chip * 2 + ((group & 1) ^ other_core)


def to_strip_target(value, chips, step, other_core):
    pairs = [
        (group, (group // 2 + step) % chips * 2 + (group % 2 ^ other_core))
        for group in range(2 * chips)
    ]
    return lax.ppermute(value, "bands", pairs)


def pick_kernel(count, blocks, tile, place_ref, *refs):
    asks, (own, sib), outs = refs[:count], refs[count : count + 2], refs[count + 2 : -1]
    sems = refs[-1]
    first = place_ref[0] * blocks
    copies = []
    for index in range(count):
        ids = asks[index][...] - first
        mine = (ids >= 0) & (ids < blocks)
        lowest = jnp.min(jnp.where(mine, ids, blocks - 1))
        highest = jnp.max(jnp.where(mine, ids, 0))
        block = jnp.where(place_ref[1] == 0, lowest, highest)
        rows = pl.ds(pl.multiple_of(block * tile, tile), tile)
        for half, source in enumerate((own, sib)):
            copy = pltpu.make_async_copy(
                source.at[rows, :], outs[index].at[half], sems.at[index, half]
            )
            copy.start()
            copies.append(copy)
    for copy in copies:
        copy.wait()


def pick(place, asks, own, sib, tile):
    blocks, bands = asks[0].shape[0], own.shape[1]
    count = len(asks)
    out_shape = [jax.ShapeDtypeStruct((2, tile, bands), own.dtype)] * count
    return pl.pallas_call(
        functools.partial(pick_kernel, count, blocks, tile),
        out_shape=out_shape,
        in_specs=[pl.BlockSpec(memory_space=pltpu.SMEM)]
        + [pl.BlockSpec(memory_space=pltpu.VMEM)] * count
        + [pl.BlockSpec(memory_space=pl.ANY)] * 2,
        out_specs=[pl.BlockSpec(memory_space=pltpu.VMEM)] * len(out_shape),
        scratch_shapes=[pltpu.SemaphoreType.DMA((count, 2))],
        name="pick_blocks",
        compiler_params=pltpu.CompilerParams(vmem_limit_bytes=VMEM_LIMIT),
        cost_estimate=SOON,
    )(place, *asks, own, sib)


def tiles_kernel(n_arrived, n_right, n_strips, tile, place_ref, *refs):
    lefts, weights = refs[:2], refs[2:4]
    arrived, refs = refs[4 : 4 + n_arrived], refs[4 + n_arrived :]
    outs, (scaled, total) = refs[:n_strips], refs[n_strips:]
    strip = tile // n_strips
    n_left = lefts[0].shape[0] // tile
    for j in range(n_right):
        slot = j % 2
        for half in range(2):
            if n_arrived:
                block = arrived[j][half]
            else:
                first = pl.multiple_of((place_ref[0] * n_right + j) * tile, tile)
                block = lefts[half][pl.ds(first, tile), :]
            block = block.astype(jnp.float32)
            for kind in range(2):
                value = block * weights[half][kind : kind + 1, :]
                rows = pl.ds(kind * tile, tile)
                scaled[slot, half, rows, :] = value.astype(scaled.dtype)
        for half in range(2):
            value = lax.dot_general(
                lefts[half][...],
                scaled[slot, half],
                (((1,), (1,)), ((), ())),
                preferred_element_type=jnp.float32,
            )
            if half == 0:
                total[slot] = value
            else:
                total[slot] += value
        for index in range(n_strips):
            start = place_ref[1 + index] * strip
            for i in range(n_left):
                rows = pl.ds(pl.multiple_of(i * tile + start, strip), strip)
                outs[index][j, i] = total[slot, rows, :].astype(outs[index].dtype)


def tiles(place, own, sib, arrived, weights, n_strips, tile):
    rows, bands = own.shape
    blocks = rows // tile
    n_right = len(arrived) if arrived else blocks // 2
    strip = tile // n_strips
    slots = min(n_right, 2)
    vmem = pl.BlockSpec(memory_space=pltpu.VMEM)
    return pl.pallas_call(
        functools.partial(tiles_kernel, len(arrived), n_right, n_strips, tile),
        out_shape=[
            jax.ShapeDtypeStruct((n_right, blocks, strip, 2 * tile), jnp.bfloat16)
        ]
        * n_strips,
        in_specs=[pl.BlockSpec(memory_space=pltpu.SMEM)] + [vmem] * (4 + len(arrived)),
        out_specs=[vmem] * n_strips,
        scratch_shapes=[
            pltpu.VMEM((slots, 2, 2 * tile, bands), jnp.bfloat16),
            pltpu.VMEM((slots, rows, 2 * tile), jnp.float32),
        ],
        name="tiles",
        compiler_params=pltpu.CompilerParams(vmem_limit_bytes=VMEM_LIMIT),
        cost_estimate=SOON,
    )(place, own, sib, *weights, *arrived)


def strip_sum(ins, chips, n_chunks, other_core, chunk, j, i):
    total = None
    for step in range(chips):
        value = ins[(step * 2 + other_core) * n_chunks + chunk][j, i].astype(jnp.float32)
        total = value if total is None else total + value
    return total


def place_early_kernel(chips, sizes, per_core, tile, where_ref, *refs):
    n_chunks = len(sizes)
    ins = refs[: 2 * chips * n_chunks]
    density, energy, later, pool = refs[2 * chips * n_chunks :]
    for other_core in range(2):
        first = other_core * per_core
        for chunk in range(n_chunks):
            for j in range(sizes[chunk]):
                pool[first + j] = strip_sum(ins, chips, n_chunks, other_core, chunk, j, 0)
            first += sizes[chunk]
    i = pl.program_id(0)
    slots = density.shape[1]

    @pl.when(i == 0)
    def _():
        later[0] = 0

    for slot in range(slots):
        where = where_ref[i, slot]
        density[0, slot] = pool[where, :, :tile]
        energy[0, slot] = pool[where, :, tile:]

        @pl.when(lax.rem(where, per_core) == per_core - 1)
        def _():
            count = later[0] + 1
            later[count] = i * slots + slot
            later[0] = count


def place_early(where, strips, chips, per_core, tile):
    sizes = [value.shape[0] for value in strips[0]]
    _, blocks, strip, width = strips[0][0].shape
    slots = where.shape[1]
    out = jax.ShapeDtypeStruct((blocks, slots, strip, tile), jnp.float32)
    flat = [value for group in strips for value in group]
    return pl.pallas_call(
        functools.partial(place_early_kernel, chips, sizes, per_core, tile),
        out_shape=[out, out, jax.ShapeDtypeStruct((blocks * slots + 1,), jnp.int32)],
        grid_spec=pltpu.PrefetchScalarGridSpec(
            num_scalar_prefetch=1,
            grid=(blocks,),
            in_specs=[
                pl.BlockSpec(
                    (value.shape[0], 1, strip, width), lambda i, where: (0, i, 0, 0)
                )
                for value in flat
            ],
            out_specs=[
                pl.BlockSpec((1, slots, strip, tile), lambda i, where: (i, 0, 0, 0))
            ]
            * 2
            + [pl.BlockSpec(memory_space=pltpu.SMEM)],
            scratch_shapes=[pltpu.VMEM((2 * per_core, strip, width), jnp.float32)],
        ),
        name="place_early",
        compiler_params=pltpu.CompilerParams(vmem_limit_bytes=VMEM_LIMIT),
        cost_estimate=SOON,
    )(where, *flat)


def place_late_kernel(chips, per_core, tile, where_ref, later, *refs):
    ins, refs = refs[: 2 * chips], refs[2 * chips + 2 :]
    density, energy, pool, sems = refs
    blocks, slots = density.shape[:2]
    for other_core in range(2):
        for i in range(blocks):
            total = strip_sum(ins, chips, 1, other_core, 0, 0, i)
            pool[other_core, i, 0] = total[:, :tile]
            pool[other_core, i, 1] = total[:, tile:]
    count = later[0]

    def copies(n):
        entry = jnp.clip(later[n + 1], 0, blocks * slots - 1)
        i, slot = lax.div(entry, slots), lax.rem(entry, slots)
        other_core = jnp.clip(lax.div(where_ref[i, slot], per_core), 0, 1)
        return [
            pltpu.make_async_copy(
                pool.at[other_core, i, kind], out.at[i, slot], sems.at[kind]
            )
            for kind, out in enumerate((density, energy))
        ]

    @pl.loop(0, count)
    def _(n):
        for copy in copies(n):
            copy.start()

    @pl.loop(0, count)
    def _(n):
        for copy in copies(n):
            copy.wait()


def place_late(where, later, strips, density, energy, chips, per_core, tile):
    _, blocks, strip, _ = strips[0].shape
    smem = pl.BlockSpec(memory_space=pltpu.SMEM)
    anywhere = pl.BlockSpec(memory_space=pl.ANY)
    out = jax.ShapeDtypeStruct(density.shape, density.dtype)
    n_strips = len(strips)
    return pl.pallas_call(
        functools.partial(place_late_kernel, chips, per_core, tile),
        out_shape=[out, out],
        in_specs=[smem, smem]
        + [pl.BlockSpec(memory_space=pltpu.VMEM)] * n_strips
        + [anywhere] * 2,
        out_specs=[anywhere] * 2,
        scratch_shapes=[
            pltpu.VMEM((2, blocks, 2, strip, tile), jnp.float32),
            pltpu.SemaphoreType.DMA((2,)),
        ],
        input_output_aliases={2 + n_strips: 0, 3 + n_strips: 1},
        name="place_late",
        compiler_params=pltpu.CompilerParams(vmem_limit_bytes=VMEM_LIMIT),
        cost_estimate=SOON,
    )(where, later, *strips, density, energy)


def body(eigvecs, occupations, energies, neighbours):
    n_atoms = lax.axis_size("atoms")
    n_bands = lax.axis_size("bands")
    chips = n_bands // 2
    own_index = lax.axis_index("atoms").astype(jnp.int32)
    group = lax.axis_index("bands").astype(jnp.int32)
    core = group & 1
    blocks = neighbours.shape[0]
    tile = eigvecs.shape[0] // blocks
    half_blocks = blocks // 2
    offsets = [-1, 1, 2, -2]

    asks = [shifted(neighbours, "atoms", offset) for offset in offsets]
    sib = to_strip_target(eigvecs, chips, 0, 1)
    targets = [
        strip_target(group, chips, step, other)
        for step in range(chips)
        for other in range(2)
    ]
    here = jnp.stack([own_index, core]).astype(jnp.int32)
    place = jnp.stack([core] + targets).astype(jnp.int32)

    asks = lax.optimization_barrier(asks)
    near = list(pick(here, asks[:2], eigvecs, sib, tile))
    here, near[0] = lax.optimization_barrier((here, near[0]))
    far = list(pick(here, asks[2:], eigvecs, sib, tile))
    occupations, far[0] = lax.optimization_barrier((occupations, far[0]))
    near = [shifted(near[0], "atoms", -offsets[0]), shifted(near[1], "atoms", -offsets[1])]
    own_weights = jnp.stack([occupations, occupations * energies], 0)
    sib_weights = to_strip_target(own_weights, chips, 0, 1)
    weights = (own_weights, sib_weights)

    def strips_of(*arrived):
        parts = list(tiles(place, eigvecs, sib, arrived, weights, n_bands, tile))
        parts[1] = to_strip_target(parts[1], chips, 0, 1)
        for index in range(2, n_bands):
            if index % 2:
                parts[index], parts[1] = lax.optimization_barrier((parts[index], parts[1]))
            parts[index] = to_strip_target(parts[index], chips, index // 2, index % 2)
        return parts

    chunks = [strips_of()]
    neighbours, chunks[0][0], far[0] = lax.optimization_barrier(
        (neighbours, chunks[0][0], far[0])
    )
    third = shifted(far[0], "atoms", -offsets[2])

    owners = lax.div(neighbours, blocks)
    within = lax.rem(neighbours, blocks)
    distance = lax.rem(owners - own_index + n_atoms, n_atoms)
    spot = lax.rem(within, half_blocks)
    side = lax.div(within, half_blocks)
    for index, offset in enumerate(offsets):
        from_it = distance == offset % n_atoms
        highest = jnp.max(jnp.where(from_it, within, -1))
        side = jnp.where(from_it, (within == highest).astype(jnp.int32), side)
        spot = jnp.where(from_it, half_blocks + index, spot)
    per_core = half_blocks + len(offsets)
    where = ((side ^ core) * per_core + spot).astype(jnp.int32)

    near, chunks[0][:3] = lax.optimization_barrier((near, chunks[0][:3]))
    chunks.append(strips_of(*near))
    source, chunks[1][0] = lax.optimization_barrier((far[1], chunks[1][0]))
    fourth = shifted(source, "atoms", -offsets[3])
    third, chunks[0], chunks[1][:2] = lax.optimization_barrier(
        (third, chunks[0], chunks[1][:2])
    )
    chunks.append(strips_of(third))
    where, fourth, chunks[1], chunks[2][:3] = lax.optimization_barrier(
        (where, fourth, chunks[1], chunks[2][:3])
    )
    last = strips_of(fourth)
    where, last[0] = lax.optimization_barrier((where, last[0]))
    strips = [[chunk[index] for chunk in chunks] for index in range(n_bands)]
    density, energy, later = place_early(where, strips, chips, per_core, tile)
    return place_late(where, later, last, density, energy, chips, per_core, tile)


def solution(mesh):
    return jax.shard_map(
        body,
        mesh=mesh,
        in_specs=(P("atoms", "bands"), P("bands"), P("bands"), P("atoms", None)),
        out_specs=(P("atoms", None, "bands", None), P("atoms", None, "bands", None)),
        check_vma=False,
    )
```

```python
import functools

import jax
import jax.numpy as jnp
from jax import lax
from jax.experimental import pallas as pl
from jax.experimental.pallas import tpu as pltpu
from jax.sharding import PartitionSpec as P

R = 2
VMEM_LIMIT = 24 * 1024 * 1024
SOON = pl.CostEstimate(flops=0, bytes_accessed=0, transcendentals=0)


def in_hbm(value):
    return pltpu.with_memory_space_constraint(value, pltpu.HBM)


def in_vmem(value):
    return pltpu.with_memory_space_constraint(value, pltpu.VMEM)


def shifted(value, axis, steps):
    count = lax.axis_size(axis)
    pairs = [(source, (source + steps) % count) for source in range(count)]
    return lax.ppermute(value, axis, pairs)


def strip_target(group, chips, step, other_core):
    chip = lax.rem(lax.shift_right_logical(group, 1) + step, chips)
    return chip * 2 + ((group & 1) ^ other_core)


def to_strip_target(value, chips, step, other_core):
    pairs = [
        (group, (group // 2 + step) % chips * 2 + (group % 2 ^ other_core))
        for group in range(2 * chips)
    ]
    return lax.ppermute(value, "bands", pairs)


def pick_kernel(count, blocks, tile, place_ref, *refs):
    asks, (own, sib), outs = refs[:count], refs[count : count + 2], refs[count + 2 : -1]
    sems = refs[-1]
    first = place_ref[0] * blocks
    copies = []
    for index in range(count):
        ids = asks[index][...] - first
        mine = (ids >= 0) & (ids < blocks)
        lowest = jnp.min(jnp.where(mine, ids, blocks - 1))
        highest = jnp.max(jnp.where(mine, ids, 0))
        block = jnp.where(place_ref[1] == 0, lowest, highest)
        rows = pl.ds(pl.multiple_of(block * tile, tile), tile)
        for half, source in enumerate((own, sib)):
            copy = pltpu.make_async_copy(
                source.at[rows, :], outs[index].at[half], sems.at[index, half]
            )
            copy.start()
            copies.append(copy)
    for copy in copies:
        copy.wait()


def pick(place, asks, own, sib, tile):
    blocks, bands = asks[0].shape[0], own.shape[1]
    count = len(asks)
    return pl.pallas_call(
        functools.partial(pick_kernel, count, blocks, tile),
        out_shape=[pltpu.VMEM((2, tile, bands), own.dtype)] * count,
        in_specs=[pl.BlockSpec(memory_space=pltpu.SMEM)]
        + [pl.BlockSpec(memory_space=pltpu.VMEM)] * count
        + [pl.BlockSpec(memory_space=pl.ANY)] * 2,
        out_specs=[pl.BlockSpec(memory_space=pltpu.VMEM)] * count,
        scratch_shapes=[pltpu.SemaphoreType.DMA((count, 2))],
        name="pick_blocks",
        compiler_params=pltpu.CompilerParams(vmem_limit_bytes=VMEM_LIMIT),
        cost_estimate=SOON,
    )(place, *asks, in_hbm(own), in_hbm(sib))


def keep_kernel(own, sib, own_out, sib_out, sems):
    copies = []
    for half, (source, out) in enumerate(((own, own_out), (sib, sib_out))):
        copies.append(pltpu.make_async_copy(source, out, sems.at[half]))
    for copy in copies:
        copy.start()
    for copy in copies:
        copy.wait()


def keep(own, sib):
    return pl.pallas_call(
        keep_kernel,
        out_shape=[pltpu.VMEM(own.shape, own.dtype)] * 2,
        in_specs=[pl.BlockSpec(memory_space=pl.ANY)] * 2,
        out_specs=[pl.BlockSpec(memory_space=pltpu.VMEM)] * 2,
        scratch_shapes=[pltpu.SemaphoreType.DMA((2,))],
        name="keep",
        compiler_params=pltpu.CompilerParams(vmem_limit_bytes=VMEM_LIMIT),
        cost_estimate=SOON,
    )(in_hbm(own), in_hbm(sib))


def tiles_kernel(n_arrived, n_right, n_strips, tile, paired, place_ref, *refs):
    lefts, weights = refs[:2], refs[2:4]
    arrived, refs = refs[4 : 4 + n_arrived], refs[4 + n_arrived :]
    outs, (scaled, total) = refs[:-2], refs[-2:]
    if paired:
        outs = outs[:2] + tuple(out.at[index] for out in outs[2:] for index in range(2))
    strip = tile // n_strips
    n_left = lefts[0].shape[0] // tile
    for j in range(n_right):
        slot = j % 2
        for half in range(2):
            if n_arrived:
                block = arrived[j][half]
            else:
                first = pl.multiple_of((place_ref[0] * n_right + j) * tile, tile)
                block = lefts[half][pl.ds(first, tile), :]
            block = block.astype(jnp.float32)
            for kind in range(2):
                value = block * weights[half][kind : kind + 1, :]
                rows = pl.ds(kind * tile, tile)
                scaled[slot, half, rows, :] = value.astype(scaled.dtype)
        for half in range(2):
            value = lax.dot_general(
                lefts[half][...],
                scaled[slot, half],
                (((1,), (1,)), ((), ())),
                preferred_element_type=jnp.float32,
            )
            if half == 0:
                total[slot] = value
            else:
                total[slot] += value
        for index in range(n_strips):
            start = place_ref[1 + index] * strip
            for i in range(n_left):
                rows = pl.ds(pl.multiple_of(i * tile + start, strip), strip)
                outs[index][j, i] = total[slot, rows, :].astype(outs[index].dtype)


def tiles(place, own, sib, arrived, weights, n_strips, tile, paired):
    rows, bands = own.shape
    blocks = rows // tile
    n_right = len(arrived) if arrived else blocks // 2
    strip = tile // n_strips
    slots = min(n_right, 2)
    vmem = pl.BlockSpec(memory_space=pltpu.VMEM)
    out = jax.ShapeDtypeStruct((n_right, blocks, strip, 2 * tile), jnp.bfloat16)
    pair = jax.ShapeDtypeStruct((2, *out.shape), out.dtype)
    outs = [out, out] + [pair] * (n_strips // 2 - 1) if paired else [out] * n_strips
    return pl.pallas_call(
        functools.partial(tiles_kernel, len(arrived), n_right, n_strips, tile, paired),
        out_shape=outs,
        in_specs=[pl.BlockSpec(memory_space=pltpu.SMEM)] + [vmem] * (4 + len(arrived)),
        out_specs=[vmem] * len(outs),
        scratch_shapes=[
            pltpu.VMEM((slots, 2, 2 * tile, bands), jnp.bfloat16),
            pltpu.VMEM((slots, rows, 2 * tile), jnp.float32),
        ],
        name="tiles",
        compiler_params=pltpu.CompilerParams(vmem_limit_bytes=VMEM_LIMIT),
        cost_estimate=SOON,
    )(place, in_vmem(own), in_vmem(sib), *weights, *arrived)


def strip_sum(ins, chips, n_chunks, other_core, chunk, j, i):
    total = None
    for step in range(chips):
        value = ins[(step * 2 + other_core) * n_chunks + chunk][j, i].astype(jnp.float32)
        total = value if total is None else total + value
    return total


def place_early_kernel(chips, sizes, per_core, tile, where_ref, *refs):
    n_chunks = len(sizes)
    ins = refs[: 2 * chips * n_chunks]
    density, energy, later, pool = refs[2 * chips * n_chunks :]
    for other_core in range(2):
        first = other_core * per_core
        for chunk in range(n_chunks):
            for j in range(sizes[chunk]):
                pool[first + j] = strip_sum(ins, chips, n_chunks, other_core, chunk, j, 0)
            first += sizes[chunk]
    i = pl.program_id(0)
    slots = density.shape[1]

    @pl.when(i == 0)
    def _():
        later[0] = 0

    for slot in range(slots):
        where = where_ref[i, slot]
        density[0, slot] = pool[where, :, :tile]
        energy[0, slot] = pool[where, :, tile:]

        @pl.when(lax.rem(where, per_core) == per_core - 1)
        def _():
            count = later[0] + 1
            later[count] = i * slots + slot
            later[0] = count


def place_early(where, strips, chips, per_core, tile):
    sizes = [value.shape[0] for value in strips[0]]
    _, blocks, strip, width = strips[0][0].shape
    slots = where.shape[1]
    out = jax.ShapeDtypeStruct((blocks, slots, strip, tile), jnp.float32)
    flat = [value for group in strips for value in group]
    return pl.pallas_call(
        functools.partial(place_early_kernel, chips, sizes, per_core, tile),
        out_shape=[out, out, jax.ShapeDtypeStruct((blocks * slots + 1,), jnp.int32)],
        grid_spec=pltpu.PrefetchScalarGridSpec(
            num_scalar_prefetch=1,
            grid=(blocks,),
            in_specs=[
                pl.BlockSpec(
                    (value.shape[0], 1, strip, width), lambda i, where: (0, i, 0, 0)
                )
                for value in flat
            ],
            out_specs=[
                pl.BlockSpec((1, slots, strip, tile), lambda i, where: (i, 0, 0, 0))
            ]
            * 2
            + [pl.BlockSpec(memory_space=pltpu.SMEM)],
            scratch_shapes=[pltpu.VMEM((2 * per_core, strip, width), jnp.float32)],
        ),
        name="place_early",
        compiler_params=pltpu.CompilerParams(vmem_limit_bytes=VMEM_LIMIT),
        cost_estimate=SOON,
    )(where, *flat)


def place_late_kernel(chips, per_core, tile, where_ref, later, *refs):
    ins, refs = refs[: 2 * chips], refs[2 * chips + 2 :]
    density, energy, pool, sems = refs
    blocks, slots = density.shape[:2]
    for other_core in range(2):
        for i in range(blocks):
            total = strip_sum(ins, chips, 1, other_core, 0, 0, i)
            pool[other_core, i, 0] = total[:, :tile]
            pool[other_core, i, 1] = total[:, tile:]
    count = later[0]

    def copies(n):
        entry = jnp.clip(later[n + 1], 0, blocks * slots - 1)
        i, slot = lax.div(entry, slots), lax.rem(entry, slots)
        other_core = jnp.clip(lax.div(where_ref[i, slot], per_core), 0, 1)
        return [
            pltpu.make_async_copy(
                pool.at[other_core, i, kind], out.at[i, slot], sems.at[kind]
            )
            for kind, out in enumerate((density, energy))
        ]

    @pl.loop(0, count)
    def _(n):
        for copy in copies(n):
            copy.start()

    @pl.loop(0, count)
    def _(n):
        for copy in copies(n):
            copy.wait()


def place_late(where, later, strips, density, energy, chips, per_core, tile):
    _, blocks, strip, _ = strips[0].shape
    smem = pl.BlockSpec(memory_space=pltpu.SMEM)
    anywhere = pl.BlockSpec(memory_space=pl.ANY)
    out = jax.ShapeDtypeStruct(density.shape, density.dtype)
    n_strips = len(strips)
    return pl.pallas_call(
        functools.partial(place_late_kernel, chips, per_core, tile),
        out_shape=[out, out],
        in_specs=[smem, smem]
        + [pl.BlockSpec(memory_space=pltpu.VMEM)] * n_strips
        + [anywhere] * 2,
        out_specs=[anywhere] * 2,
        scratch_shapes=[
            pltpu.VMEM((2, blocks, 2, strip, tile), jnp.float32),
            pltpu.SemaphoreType.DMA((2,)),
        ],
        input_output_aliases={2 + n_strips: 0, 3 + n_strips: 1},
        name="place_late",
        compiler_params=pltpu.CompilerParams(vmem_limit_bytes=VMEM_LIMIT),
        cost_estimate=SOON,
    )(where, later, *strips, density, energy)


def body(eigvecs, occupations, energies, neighbours):
    n_atoms = lax.axis_size("atoms")
    n_bands = lax.axis_size("bands")
    chips = n_bands // 2
    own_index = lax.axis_index("atoms").astype(jnp.int32)
    group = lax.axis_index("bands").astype(jnp.int32)
    core = group & 1
    blocks = neighbours.shape[0]
    tile = eigvecs.shape[0] // blocks
    half_blocks = blocks // 2
    offsets = [2, -1, 1, -2]

    asks = [shifted(neighbours, "atoms", offset) for offset in offsets[:3]]
    sib = to_strip_target(eigvecs, chips, 0, 1)
    own_weights = jnp.stack([occupations, occupations * energies], 0)
    sib_weights = to_strip_target(own_weights, chips, 0, 1)
    weights = (own_weights, sib_weights)

    targets = [
        strip_target(group, chips, step, other)
        for step in range(chips)
        for other in range(2)
    ]
    here = jnp.stack([own_index, core]).astype(jnp.int32)
    place = jnp.stack([core] + targets).astype(jnp.int32)

    asks = lax.optimization_barrier(asks)
    picked = list(pick(here, asks, eigvecs, sib, tile))
    late_neighbours, picked[0] = lax.optimization_barrier((neighbours, picked[0]))
    arrived = [
        shifted(value, "atoms", -offset) for value, offset in zip(picked, offsets)
    ]
    last_ask = shifted(late_neighbours, "atoms", offsets[3])
    kept_eigvecs, picked[0] = lax.optimization_barrier((eigvecs, picked[0]))
    own, kept_sib = keep(kept_eigvecs, sib)

    def strips_of(arrived, paired):
        parts = list(tiles(place, own, kept_sib, arrived, weights, n_bands, tile, paired))
        for index in range(1, len(parts)):
            step, other = (max(index - 1, 0), index == 1) if paired else (index // 2, index % 2)
            parts[index] = to_strip_target(parts[index], chips, step, int(other))
        return parts

    def passed_on(parts):
        singles = parts[:2]
        for pair in parts[2:]:
            singles += [pair[0], to_strip_target(pair[1], chips, 0, 1)]
        return singles

    chunks = [strips_of((), True)]
    neighbours, here, last_ask, chunks[0][0] = lax.optimization_barrier(
        (neighbours, here, last_ask, chunks[0][0])
    )
    (last_picked,) = pick(here, [last_ask], eigvecs, sib, tile)

    owners = lax.div(neighbours, blocks)
    within = lax.rem(neighbours, blocks)
    distance = lax.rem(owners - own_index + n_atoms, n_atoms)
    spot = lax.rem(within, half_blocks)
    side = lax.div(within, half_blocks)
    for index, offset in enumerate(offsets):
        from_it = distance == offset % n_atoms
        highest = jnp.max(jnp.where(from_it, within, -1))
        side = jnp.where(from_it, (within == highest).astype(jnp.int32), side)
        spot = jnp.where(from_it, half_blocks + index, spot)
    per_core = half_blocks + len(offsets)
    where = ((side ^ core) * per_core + spot).astype(jnp.int32)

    arrived, last_picked, chunks[0] = lax.optimization_barrier(
        (arrived, last_picked, chunks[0])
    )
    fourth = shifted(last_picked, "atoms", -offsets[3])
    chunks.append(strips_of(arrived, True))
    where, fourth, chunks[1] = lax.optimization_barrier((where, fourth, chunks[1]))
    last = strips_of((fourth,), False)
    chunks = [passed_on(chunk) for chunk in chunks]
    where, last[0] = lax.optimization_barrier((where, last[0]))
    strips = [[chunk[index] for chunk in chunks] for index in range(n_bands)]
    density, energy, later = place_early(where, strips, chips, per_core, tile)
    return place_late(where, later, last, density, energy, chips, per_core, tile)


def solution(mesh):
    return jax.shard_map(
        body,
        mesh=mesh,
        in_specs=(P("atoms", "bands"), P("bands"), P("bands"), P("atoms", None)),
        out_specs=(P("atoms", None, "bands", None), P("atoms", None, "bands", None)),
        check_vma=False,
    )
```

```python
import functools

import jax
import jax.numpy as jnp
from jax import lax
from jax.experimental import pallas as pl
from jax.experimental.pallas import tpu as pltpu
from jax.sharding import PartitionSpec as P

R = 2
VMEM_LIMIT = 24 * 1024 * 1024
SOON = pl.CostEstimate(flops=0, bytes_accessed=0, transcendentals=0)


def in_hbm(value):
    return pltpu.with_memory_space_constraint(value, pltpu.HBM)


def in_vmem(value):
    return pltpu.with_memory_space_constraint(value, pltpu.VMEM)


def shifted(value, axis, steps):
    count = lax.axis_size(axis)
    pairs = [(source, (source + steps) % count) for source in range(count)]
    return lax.ppermute(value, axis, pairs)


def strip_target(group, chips, step, other_core):
    chip = lax.rem(lax.shift_right_logical(group, 1) + step, chips)
    return chip * 2 + ((group & 1) ^ other_core)


def to_strip_target(value, chips, step, other_core):
    pairs = [
        (group, (group // 2 + step) % chips * 2 + (group % 2 ^ other_core))
        for group in range(2 * chips)
    ]
    return lax.ppermute(value, "bands", pairs)


def pick_kernel(count, blocks, tile, place_ref, *refs):
    asks, (own, sib), outs = refs[:count], refs[count : count + 2], refs[count + 2 : -1]
    sems = refs[-1]
    first = place_ref[0] * blocks
    copies = []
    for index in range(count):
        ids = asks[index][...] - first
        mine = (ids >= 0) & (ids < blocks)
        ids = jnp.where(place_ref[1] == 0, blocks - 1 - ids, ids)
        block = jnp.max(jnp.where(mine, ids, 0))
        block = jnp.where(place_ref[1] == 0, blocks - 1 - block, block)
        rows = pl.ds(pl.multiple_of(block * tile, tile), tile)
        for half, source in enumerate((own, sib)):
            copy = pltpu.make_async_copy(
                source.at[rows, :], outs[index].at[half], sems.at[index, half]
            )
            copy.start()
            copies.append(copy)
    for copy in copies:
        copy.wait()


def pick(place, asks, own, sib, tile):
    blocks, bands = asks[0].shape[0], own.shape[1]
    count = len(asks)
    return pl.pallas_call(
        functools.partial(pick_kernel, count, blocks, tile),
        out_shape=[pltpu.VMEM((2, tile, bands), own.dtype)] * count,
        in_specs=[pl.BlockSpec(memory_space=pltpu.SMEM)]
        + [pl.BlockSpec(memory_space=pltpu.VMEM)] * count
        + [pl.BlockSpec(memory_space=pl.ANY)] * 2,
        out_specs=[pl.BlockSpec(memory_space=pltpu.VMEM)] * count,
        scratch_shapes=[pltpu.SemaphoreType.DMA((count, 2))],
        name="pick_blocks",
        compiler_params=pltpu.CompilerParams(vmem_limit_bytes=VMEM_LIMIT),
        cost_estimate=SOON,
    )(place, *asks, in_hbm(own), in_hbm(sib))


def keep_kernel(own, sib, own_out, sib_out, sems):
    copies = []
    for half, (source, out) in enumerate(((own, own_out), (sib, sib_out))):
        copies.append(pltpu.make_async_copy(source, out, sems.at[half]))
    for copy in copies:
        copy.start()
    for copy in copies:
        copy.wait()


def keep(own, sib):
    return pl.pallas_call(
        keep_kernel,
        out_shape=[pltpu.VMEM(own.shape, own.dtype)] * 2,
        in_specs=[pl.BlockSpec(memory_space=pl.ANY)] * 2,
        out_specs=[pl.BlockSpec(memory_space=pltpu.VMEM)] * 2,
        scratch_shapes=[pltpu.SemaphoreType.DMA((2,))],
        name="keep",
        compiler_params=pltpu.CompilerParams(vmem_limit_bytes=VMEM_LIMIT),
        cost_estimate=SOON,
    )(in_hbm(own), in_hbm(sib))


def tiles_kernel(n_arrived, n_right, n_strips, tile, paired, place_ref, *refs):
    lefts, weights = refs[:2], refs[2:4]
    arrived, refs = refs[4 : 4 + n_arrived], refs[4 + n_arrived :]
    outs, (scaled, total) = refs[:-2], refs[-2:]
    if paired:
        outs = outs[:2] + tuple(out.at[index] for out in outs[2:] for index in range(2))
    strip = tile // n_strips
    n_left = lefts[0].shape[0] // tile
    for j in range(n_right):
        slot = j % 2
        for half in range(2):
            if n_arrived:
                block = arrived[j][half]
            else:
                first = pl.multiple_of((place_ref[0] * n_right + j) * tile, tile)
                block = lefts[half][pl.ds(first, tile), :]
            block = block.astype(jnp.float32)
            for kind in range(2):
                value = block * weights[half][kind : kind + 1, :]
                rows = pl.ds(kind * tile, tile)
                scaled[slot, half, rows, :] = value.astype(scaled.dtype)
        for half in range(2):
            value = lax.dot_general(
                lefts[half][...],
                scaled[slot, half],
                (((1,), (1,)), ((), ())),
                preferred_element_type=jnp.float32,
            )
            if half == 0:
                total[slot] = value
            else:
                total[slot] += value
        for index in range(n_strips):
            start = place_ref[1 + index] * strip
            for i in range(n_left):
                rows = pl.ds(pl.multiple_of(i * tile + start, strip), strip)
                outs[index][j, i] = total[slot, rows, :].astype(outs[index].dtype)


def tiles(place, own, sib, arrived, weights, n_strips, tile, paired):
    rows, bands = own.shape
    blocks = rows // tile
    n_right = len(arrived) if arrived else blocks // 2
    strip = tile // n_strips
    slots = min(n_right, 2)
    vmem = pl.BlockSpec(memory_space=pltpu.VMEM)
    out = jax.ShapeDtypeStruct((n_right, blocks, strip, 2 * tile), jnp.bfloat16)
    pair = jax.ShapeDtypeStruct((2, *out.shape), out.dtype)
    outs = [out, out] + [pair] * (n_strips // 2 - 1) if paired else [out] * n_strips
    return pl.pallas_call(
        functools.partial(tiles_kernel, len(arrived), n_right, n_strips, tile, paired),
        out_shape=outs,
        in_specs=[pl.BlockSpec(memory_space=pltpu.SMEM)] + [vmem] * (4 + len(arrived)),
        out_specs=[vmem] * len(outs),
        scratch_shapes=[
            pltpu.VMEM((slots, 2, 2 * tile, bands), jnp.bfloat16),
            pltpu.VMEM((slots, rows, 2 * tile), jnp.float32),
        ],
        name="tiles",
        compiler_params=pltpu.CompilerParams(vmem_limit_bytes=VMEM_LIMIT),
        cost_estimate=SOON,
    )(place, in_vmem(own), in_vmem(sib), *weights, *arrived)


def strip_sum(ins, chips, n_chunks, other_core, chunk, j, i):
    total = None
    for step in range(chips):
        value = ins[(step * 2 + other_core) * n_chunks + chunk][j, i].astype(jnp.float32)
        total = value if total is None else total + value
    return total


def place_early_kernel(chips, sizes, per_core, tile, where_ref, *refs):
    n_chunks = len(sizes)
    ins = refs[: 2 * chips * n_chunks]
    density, energy, later, pool = refs[2 * chips * n_chunks :]
    for other_core in range(2):
        first = other_core * per_core
        for chunk in range(n_chunks):
            for j in range(sizes[chunk]):
                pool[first + j] = strip_sum(ins, chips, n_chunks, other_core, chunk, j, 0)
            first += sizes[chunk]
    i = pl.program_id(0)
    slots = density.shape[1]

    @pl.when(i == 0)
    def _():
        later[0] = 0

    for slot in range(slots):
        where = where_ref[i, slot]
        density[0, slot] = pool[where, :, :tile]
        energy[0, slot] = pool[where, :, tile:]

        @pl.when(lax.rem(where, per_core) == per_core - 1)
        def _():
            count = later[0] + 1
            later[count] = i * slots + slot
            later[0] = count


def place_early(where, strips, chips, per_core, tile):
    sizes = [value.shape[0] for value in strips[0]]
    _, blocks, strip, width = strips[0][0].shape
    slots = where.shape[1]
    out = jax.ShapeDtypeStruct((blocks, slots, strip, tile), jnp.float32)
    flat = [value for group in strips for value in group]
    return pl.pallas_call(
        functools.partial(place_early_kernel, chips, sizes, per_core, tile),
        out_shape=[out, out, jax.ShapeDtypeStruct((blocks * slots + 1,), jnp.int32)],
        grid_spec=pltpu.PrefetchScalarGridSpec(
            num_scalar_prefetch=1,
            grid=(blocks,),
            in_specs=[
                pl.BlockSpec(
                    (value.shape[0], 1, strip, width), lambda i, where: (0, i, 0, 0)
                )
                for value in flat
            ],
            out_specs=[
                pl.BlockSpec((1, slots, strip, tile), lambda i, where: (i, 0, 0, 0))
            ]
            * 2
            + [pl.BlockSpec(memory_space=pltpu.SMEM)],
            scratch_shapes=[pltpu.VMEM((2 * per_core, strip, width), jnp.float32)],
        ),
        name="place_early",
        compiler_params=pltpu.CompilerParams(vmem_limit_bytes=VMEM_LIMIT),
        cost_estimate=SOON,
    )(where, *flat)


def place_late_kernel(chips, per_core, tile, where_ref, later, *refs):
    ins, refs = refs[: 2 * chips], refs[2 * chips + 2 :]
    density, energy, pool, sems = refs
    blocks, slots = density.shape[:2]
    for other_core in range(2):
        for i in range(blocks):
            total = strip_sum(ins, chips, 1, other_core, 0, 0, i)
            pool[other_core, i, 0] = total[:, :tile]
            pool[other_core, i, 1] = total[:, tile:]
    count = later[0]

    def copies(n):
        entry = jnp.clip(later[n + 1], 0, blocks * slots - 1)
        i, slot = lax.div(entry, slots), lax.rem(entry, slots)
        other_core = jnp.clip(lax.div(where_ref[i, slot], per_core), 0, 1)
        return [
            pltpu.make_async_copy(
                pool.at[other_core, i, kind], out.at[i, slot], sems.at[kind]
            )
            for kind, out in enumerate((density, energy))
        ]

    @pl.loop(0, count)
    def _(n):
        for copy in copies(n):
            copy.start()

    @pl.loop(0, count)
    def _(n):
        for copy in copies(n):
            copy.wait()


def place_late(where, later, strips, density, energy, chips, per_core, tile):
    _, blocks, strip, _ = strips[0].shape
    smem = pl.BlockSpec(memory_space=pltpu.SMEM)
    anywhere = pl.BlockSpec(memory_space=pl.ANY)
    out = jax.ShapeDtypeStruct(density.shape, density.dtype)
    n_strips = len(strips)
    return pl.pallas_call(
        functools.partial(place_late_kernel, chips, per_core, tile),
        out_shape=[out, out],
        in_specs=[smem, smem]
        + [pl.BlockSpec(memory_space=pltpu.VMEM)] * n_strips
        + [anywhere] * 2,
        out_specs=[anywhere] * 2,
        scratch_shapes=[
            pltpu.VMEM((2, blocks, 2, strip, tile), jnp.float32),
            pltpu.SemaphoreType.DMA((2,)),
        ],
        input_output_aliases={2 + n_strips: 0, 3 + n_strips: 1},
        name="place_late",
        compiler_params=pltpu.CompilerParams(vmem_limit_bytes=VMEM_LIMIT),
        cost_estimate=SOON,
    )(where, later, *strips, density, energy)


def body(eigvecs, occupations, energies, neighbours):
    n_atoms = lax.axis_size("atoms")
    n_bands = lax.axis_size("bands")
    chips = n_bands // 2
    own_index = lax.axis_index("atoms").astype(jnp.int32)
    group = lax.axis_index("bands").astype(jnp.int32)
    core = group & 1
    blocks = neighbours.shape[0]
    tile = eigvecs.shape[0] // blocks
    half_blocks = blocks // 2
    offsets = [2, -1, 1, -2]

    asks = [shifted(neighbours, "atoms", offset) for offset in offsets]
    sib = to_strip_target(eigvecs, chips, 0, 1)
    own_weights = jnp.stack([occupations, occupations * energies], 0)

    targets = [
        strip_target(group, chips, step, other)
        for step in range(chips)
        for other in range(2)
    ]
    here = jnp.stack([own_index, core]).astype(jnp.int32)
    place = jnp.stack([core] + targets).astype(jnp.int32)

    asks, own_weights = lax.optimization_barrier((asks, own_weights))
    weights = (own_weights, to_strip_target(own_weights, chips, 0, 1))
    picked = list(pick(here, asks[:3], eigvecs, sib, tile))
    arrived = [
        shifted(value, "atoms", -offset) for value, offset in zip(picked, offsets)
    ]
    kept_eigvecs, picked[0] = lax.optimization_barrier((eigvecs, picked[0]))
    own, kept_sib = keep(kept_eigvecs, sib)

    def strips_of(arrived, paired):
        parts = list(tiles(place, own, kept_sib, arrived, weights, n_bands, tile, paired))
        for index in range(1, len(parts)):
            step, other = (max(index - 1, 0), index == 1) if paired else (index // 2, index % 2)
            parts[index] = to_strip_target(parts[index], chips, step, int(other))
        return parts

    def passed_on(parts):
        singles = parts[:2]
        for pair in parts[2:]:
            singles += [pair[0], to_strip_target(pair[1], chips, 0, 1)]
        return singles

    chunks = [strips_of((), True)]
    neighbours, here, chunks[0][0] = lax.optimization_barrier(
        (neighbours, here, chunks[0][0])
    )
    (last_picked,) = pick(here, asks[3:], eigvecs, sib, tile)

    owners = lax.div(neighbours, blocks)
    within = lax.rem(neighbours, blocks)
    distance = lax.rem(owners - own_index + n_atoms, n_atoms)
    spot = lax.rem(within, half_blocks)
    side = lax.div(within, half_blocks)
    for index, offset in enumerate(offsets):
        from_it = distance == offset % n_atoms
        highest = jnp.max(jnp.where(from_it, within, -1))
        side = jnp.where(from_it, (within == highest).astype(jnp.int32), side)
        spot = jnp.where(from_it, half_blocks + index, spot)
    per_core = half_blocks + len(offsets)
    where = ((side ^ core) * per_core + spot).astype(jnp.int32)

    arrived[0], last_picked, chunks[0][:2] = lax.optimization_barrier(
        (arrived[0], last_picked, chunks[0][:2])
    )
    fourth = shifted(last_picked, "atoms", -offsets[3])
    parts = list(tiles(place, own, kept_sib, arrived[:1], weights, n_bands, tile, True))
    pairs = [
        to_strip_target(pair, chips, step + 1, 0) for step, pair in enumerate(parts[2:])
    ]
    near, parts[:2], pairs, chunks = lax.optimization_barrier(
        (arrived[1:], parts[:2], pairs, chunks)
    )
    chunks.append([parts[0], to_strip_target(parts[1], chips, 0, 1)] + pairs)
    direct = strips_of(near, False)
    chunks, direct[0] = lax.optimization_barrier((chunks, direct[0]))
    chunks = [passed_on(chunk) for chunk in chunks] + [direct]
    where, fourth, chunks = lax.optimization_barrier((where, fourth, chunks))
    last = strips_of((fourth,), False)
    where, last[0] = lax.optimization_barrier((where, last[0]))
    strips = [[chunk[index] for chunk in chunks] for index in range(n_bands)]
    density, energy, later = place_early(where, strips, chips, per_core, tile)
    return place_late(where, later, last, density, energy, chips, per_core, tile)


def solution(mesh):
    return jax.shard_map(
        body,
        mesh=mesh,
        in_specs=(P("atoms", "bands"), P("bands"), P("bands"), P("atoms", None)),
        out_specs=(P("atoms", None, "bands", None), P("atoms", None, "bands", None)),
        check_vma=False,
    )
```

```python
import functools

import jax
import jax.numpy as jnp
from jax import lax
from jax.experimental import pallas as pl
from jax.experimental.pallas import tpu as pltpu
from jax.sharding import PartitionSpec as P

R = 2
VMEM_LIMIT = 24 * 1024 * 1024
SOON = pl.CostEstimate(flops=0, bytes_accessed=0, transcendentals=0)


def in_hbm(value):
    return pltpu.with_memory_space_constraint(value, pltpu.HBM)


def in_vmem(value):
    return pltpu.with_memory_space_constraint(value, pltpu.VMEM)


def shifted(value, axis, steps):
    count = lax.axis_size(axis)
    pairs = [(source, (source + steps) % count) for source in range(count)]
    return lax.ppermute(value, axis, pairs)


def strip_target(group, chips, step, other_core):
    chip = lax.rem(lax.shift_right_logical(group, 1) + step, chips)
    return chip * 2 + ((group & 1) ^ other_core)


def to_strip_target(value, chips, step, other_core):
    pairs = [
        (group, (group // 2 + step) % chips * 2 + (group % 2 ^ other_core))
        for group in range(2 * chips)
    ]
    return lax.ppermute(value, "bands", pairs)


def pick_kernel(count, blocks, tile, parts, place_ref, *refs):
    asks, (own, sib), outs = refs[:count], refs[count : count + 2], refs[count + 2 : -1]
    sems = refs[-1]
    first = place_ref[0] * blocks
    copies = []
    for index in range(count):
        ids = asks[index][...] - first
        mine = (ids >= 0) & (ids < blocks)
        lowest = jnp.min(jnp.where(mine, ids, blocks - 1))
        highest = jnp.max(jnp.where(mine, ids, 0))
        block = jnp.where(place_ref[1] == 0, lowest, highest)
        for part in range(parts):
            height = tile // parts
            start = pl.multiple_of(block * tile + part * height, height)
            out = outs[index * parts + part]
            for half, source in enumerate((own, sib)):
                copy = pltpu.make_async_copy(
                    source.at[pl.ds(start, height), :],
                    out.at[half],
                    sems.at[index * parts + part, half],
                )
                copy.start()
                copies.append(copy)
    for copy in copies:
        copy.wait()


def pick(place, asks, own, sib, tile, parts):
    blocks, bands = asks[0].shape[0], own.shape[1]
    count = len(asks)
    n_outs = count * parts
    return pl.pallas_call(
        functools.partial(pick_kernel, count, blocks, tile, parts),
        out_shape=[pltpu.VMEM((2, tile // parts, bands), own.dtype)] * n_outs,
        in_specs=[pl.BlockSpec(memory_space=pltpu.SMEM)]
        + [pl.BlockSpec(memory_space=pltpu.VMEM)] * count
        + [pl.BlockSpec(memory_space=pl.ANY)] * 2,
        out_specs=[pl.BlockSpec(memory_space=pltpu.VMEM)] * n_outs,
        scratch_shapes=[pltpu.SemaphoreType.DMA((n_outs, 2))],
        name="pick_blocks",
        compiler_params=pltpu.CompilerParams(vmem_limit_bytes=VMEM_LIMIT),
        cost_estimate=SOON,
    )(place, *asks, in_hbm(own), in_hbm(sib))


def keep_kernel(own, sib, own_out, sib_out, sems):
    copies = []
    for half, (source, out) in enumerate(((own, own_out), (sib, sib_out))):
        copies.append(pltpu.make_async_copy(source, out, sems.at[half]))
    for copy in copies:
        copy.start()
    for copy in copies:
        copy.wait()


def keep(own, sib):
    return pl.pallas_call(
        keep_kernel,
        out_shape=[pltpu.VMEM(own.shape, own.dtype)] * 2,
        in_specs=[pl.BlockSpec(memory_space=pl.ANY)] * 2,
        out_specs=[pl.BlockSpec(memory_space=pltpu.VMEM)] * 2,
        scratch_shapes=[pltpu.SemaphoreType.DMA((2,))],
        name="keep",
        compiler_params=pltpu.CompilerParams(vmem_limit_bytes=VMEM_LIMIT),
        cost_estimate=SOON,
    )(in_hbm(own), in_hbm(sib))


def tiles_kernel(heights, n_arrived, n_strips, tile, paired, place_ref, *refs):
    lefts, weights = refs[:2], refs[2:4]
    arrived, refs = refs[4 : 4 + n_arrived], refs[4 + n_arrived :]
    outs, (scaled, total) = refs[:-2], refs[-2:]
    if paired:
        outs = outs[:2] + tuple(out.at[index] for out in outs[2:] for index in range(2))
    strip = tile // n_strips
    n_left = lefts[0].shape[0] // tile
    unit = 0
    for j, height in enumerate(heights):
        slot = j % 2
        for half in range(2):
            if n_arrived:
                block = arrived[j][half]
            else:
                first = pl.multiple_of((place_ref[0] * len(heights) + j) * tile, tile)
                block = lefts[half][pl.ds(first, tile), :]
            block = block.astype(jnp.float32)
            for kind in range(2):
                value = block * weights[half][kind : kind + 1, :]
                rows = pl.ds(kind * height, height)
                scaled[slot, half, rows, :] = value.astype(scaled.dtype)
        width = 2 * height
        for half in range(2):
            value = lax.dot_general(
                lefts[half][...],
                scaled[slot, half, :width, :],
                (((1,), (1,)), ((), ())),
                preferred_element_type=jnp.float32,
            )
            if half == 0:
                total[slot, :, :width] = value
            else:
                total[slot, :, :width] += value
        for lane in range(0, width, tile):
            for index in range(n_strips):
                start = place_ref[1 + index] * strip
                for i in range(n_left):
                    rows = pl.ds(pl.multiple_of(i * tile + start, strip), strip)
                    value = total[slot, rows, lane : lane + tile]
                    outs[index][unit, i] = value.astype(outs[index].dtype)
            unit += 1


def tiles(place, own, sib, arrived, weights, n_strips, tile, paired):
    rows, bands = own.shape
    blocks = rows // tile
    heights = [value.shape[1] for value in arrived] or [tile] * (blocks // 2)
    strip = tile // n_strips
    slots = min(len(heights), 2)
    vmem = pl.BlockSpec(memory_space=pltpu.VMEM)
    units = sum(2 * height // tile for height in heights)
    out = jax.ShapeDtypeStruct((units, blocks, strip, tile), jnp.bfloat16)
    pair = jax.ShapeDtypeStruct((2, *out.shape), out.dtype)
    outs = [out, out] + [pair] * (n_strips // 2 - 1) if paired else [out] * n_strips
    return pl.pallas_call(
        functools.partial(tiles_kernel, heights, len(arrived), n_strips, tile, paired),
        out_shape=outs,
        in_specs=[pl.BlockSpec(memory_space=pltpu.SMEM)] + [vmem] * (4 + len(arrived)),
        out_specs=[vmem] * len(outs),
        scratch_shapes=[
            pltpu.VMEM((slots, 2, 2 * max(heights), bands), jnp.bfloat16),
            pltpu.VMEM((slots, rows, 2 * max(heights)), jnp.float32),
        ],
        name="tiles",
        compiler_params=pltpu.CompilerParams(vmem_limit_bytes=VMEM_LIMIT),
        cost_estimate=SOON,
    )(place, in_vmem(own), in_vmem(sib), *weights, *arrived)


def strip_sum(ins, chips, n_chunks, other_core, chunk, unit, i):
    total = None
    for step in range(chips):
        ref = ins[(step * 2 + other_core) * n_chunks + chunk]
        value = ref[unit, i].astype(jnp.float32)
        total = value if total is None else total + value
    return total


def place_early_kernel(chips, sizes, per_core, where_ref, *refs):
    n_chunks = len(sizes)
    ins = refs[: 2 * chips * n_chunks]
    density, energy, later, pool = refs[2 * chips * n_chunks :]
    for other_core in range(2):
        first = other_core * per_core
        for chunk in range(n_chunks):
            for unit in range(2 * sizes[chunk]):
                pool[first + unit // 2, unit % 2] = strip_sum(
                    ins, chips, n_chunks, other_core, chunk, unit, 0
                )
            first += sizes[chunk]
    i = pl.program_id(0)
    slots = density.shape[1]

    @pl.when(i == 0)
    def _():
        later[0] = 0

    for slot in range(slots):
        where = where_ref[i, slot]
        density[0, slot] = pool[where, 0]
        energy[0, slot] = pool[where, 1]

        @pl.when(lax.rem(where, per_core) == per_core - 1)
        def _():
            count = later[0] + 1
            later[count] = i * slots + slot
            later[0] = count


def place_early(where, strips, sizes, chips, per_core):
    _, blocks, strip, tile = strips[0][0].shape
    slots = where.shape[1]
    out = jax.ShapeDtypeStruct((blocks, slots, strip, tile), jnp.float32)
    flat = [value for group in strips for value in group]
    return pl.pallas_call(
        functools.partial(place_early_kernel, chips, sizes, per_core),
        out_shape=[out, out, jax.ShapeDtypeStruct((blocks * slots + 1,), jnp.int32)],
        grid_spec=pltpu.PrefetchScalarGridSpec(
            num_scalar_prefetch=1,
            grid=(blocks,),
            in_specs=[
                pl.BlockSpec(
                    (value.shape[0], 1, strip, tile), lambda i, where: (0, i, 0, 0)
                )
                for value in flat
            ],
            out_specs=[
                pl.BlockSpec((1, slots, strip, tile), lambda i, where: (i, 0, 0, 0))
            ]
            * 2
            + [pl.BlockSpec(memory_space=pltpu.SMEM)],
            scratch_shapes=[pltpu.VMEM((2 * per_core, 2, strip, tile), jnp.float32)],
        ),
        name="place_early",
        compiler_params=pltpu.CompilerParams(vmem_limit_bytes=VMEM_LIMIT),
        cost_estimate=SOON,
    )(where, *flat)


def place_late_kernel(chips, per_core, where_ref, later, *refs):
    lower, upper = refs[: 2 * chips], refs[2 * chips : 4 * chips]
    density, energy, pool, sems = refs[4 * chips + 2 :]
    blocks, slots = density.shape[:2]
    cut = density.shape[3] // 2
    unit = lower[0].shape[0] - 1
    for other_core in range(2):
        for i in range(blocks):
            low = strip_sum(lower, chips, 1, other_core, 0, unit, i)
            high = strip_sum(upper, chips, 1, other_core, 0, 0, i)
            pool[other_core, i, 0] = jnp.concatenate([low[:, :cut], high[:, :cut]], 1)
            pool[other_core, i, 1] = jnp.concatenate([low[:, cut:], high[:, cut:]], 1)
    count = later[0]

    def copies(n):
        entry = jnp.clip(later[n + 1], 0, blocks * slots - 1)
        i, slot = lax.div(entry, slots), lax.rem(entry, slots)
        other_core = jnp.clip(lax.div(where_ref[i, slot], per_core), 0, 1)
        return [
            pltpu.make_async_copy(
                pool.at[other_core, i, kind], out.at[i, slot], sems.at[kind]
            )
            for kind, out in enumerate((density, energy))
        ]

    @pl.loop(0, count)
    def _(n):
        for copy in copies(n):
            copy.start()

    @pl.loop(0, count)
    def _(n):
        for copy in copies(n):
            copy.wait()


def place_late(where, later, lower, upper, density, energy, chips, per_core):
    blocks, _, strip, tile = density.shape
    smem = pl.BlockSpec(memory_space=pltpu.SMEM)
    anywhere = pl.BlockSpec(memory_space=pl.ANY)
    out = jax.ShapeDtypeStruct(density.shape, density.dtype)
    strips = [*lower, *upper]
    return pl.pallas_call(
        functools.partial(place_late_kernel, chips, per_core),
        out_shape=[out, out],
        in_specs=[smem, smem]
        + [pl.BlockSpec(memory_space=pltpu.VMEM)] * len(strips)
        + [anywhere] * 2,
        out_specs=[anywhere] * 2,
        scratch_shapes=[
            pltpu.VMEM((2, blocks, 2, strip, tile), jnp.float32),
            pltpu.SemaphoreType.DMA((2,)),
        ],
        input_output_aliases={2 + len(strips): 0, 3 + len(strips): 1},
        name="place_late",
        compiler_params=pltpu.CompilerParams(vmem_limit_bytes=VMEM_LIMIT),
        cost_estimate=SOON,
    )(where, later, *strips, density, energy)


def body(eigvecs, occupations, energies, neighbours):
    n_atoms = lax.axis_size("atoms")
    n_bands = lax.axis_size("bands")
    chips = n_bands // 2
    own_index = lax.axis_index("atoms").astype(jnp.int32)
    group = lax.axis_index("bands").astype(jnp.int32)
    core = group & 1
    blocks = neighbours.shape[0]
    tile = eigvecs.shape[0] // blocks
    half_blocks = blocks // 2
    offsets = [-1, 1, 2, -2]

    asks = [shifted(neighbours, "atoms", offset) for offset in offsets]
    sib = to_strip_target(eigvecs, chips, 0, 1)
    own_weights = jnp.stack([occupations, occupations * energies], 0)

    targets = [
        strip_target(group, chips, step, other)
        for step in range(chips)
        for other in range(2)
    ]
    here = jnp.stack([own_index, core]).astype(jnp.int32)
    place = jnp.stack([core] + targets).astype(jnp.int32)

    asks, own_weights = lax.optimization_barrier((asks, own_weights))
    weights = (own_weights, to_strip_target(own_weights, chips, 0, 1))
    picked = list(pick(here, asks[:3], eigvecs, sib, tile, 1))
    arrived = [
        shifted(value, "atoms", -offset) for value, offset in zip(picked, offsets)
    ]
    kept_eigvecs, picked[0] = lax.optimization_barrier((eigvecs, picked[0]))
    own, kept_sib = keep(kept_eigvecs, sib)

    def strips_of(arrived, paired):
        parts = list(tiles(place, own, kept_sib, arrived, weights, n_bands, tile, paired))
        for index in range(1, len(parts)):
            step, other = (max(index - 1, 0), index == 1) if paired else (index // 2, index % 2)
            parts[index] = to_strip_target(parts[index], chips, step, int(other))
        return parts

    def passed_on(parts):
        singles = parts[:2]
        for pair in parts[2:]:
            singles += [pair[0], to_strip_target(pair[1], chips, 0, 1)]
        return singles

    chunks = [strips_of((), True)]
    neighbours, here, chunks[0][0] = lax.optimization_barrier(
        (neighbours, here, chunks[0][0])
    )
    halves = list(pick(here, asks[3:], eigvecs, sib, tile, 2))

    owners = lax.div(neighbours, blocks)
    within = lax.rem(neighbours, blocks)
    distance = lax.rem(owners - own_index + n_atoms, n_atoms)
    spot = lax.rem(within, half_blocks)
    side = lax.div(within, half_blocks)
    for index, offset in enumerate(offsets):
        from_it = distance == offset % n_atoms
        highest = jnp.max(jnp.where(from_it, within, -1))
        side = jnp.where(from_it, (within == highest).astype(jnp.int32), side)
        spot = jnp.where(from_it, half_blocks + index, spot)
    per_core = half_blocks + len(offsets)
    where = ((side ^ core) * per_core + spot).astype(jnp.int32)

    *near, third = arrived
    third, halves, chunks[0][:1] = lax.optimization_barrier((third, halves, chunks[0][:1]))
    lower = shifted(halves[0], "atoms", -offsets[3])
    parts = list(tiles(place, own, kept_sib, [third], weights, n_bands, tile, True))
    pairs = [
        to_strip_target(pair, chips, step + 1, 0) for step, pair in enumerate(parts[2:])
    ]
    near, lower, halves[1], parts[:2], pairs, chunks = lax.optimization_barrier(
        (near, lower, halves[1], parts[:2], pairs, chunks)
    )
    upper = shifted(halves[1], "atoms", -offsets[3])
    chunks.append([parts[0], to_strip_target(parts[1], chips, 0, 1)] + pairs)
    direct = strips_of([*near, lower], False)
    chunks, direct[0] = lax.optimization_barrier((chunks, direct[0]))
    chunks = [passed_on(chunk) for chunk in chunks] + [direct]
    where, upper, chunks = lax.optimization_barrier((where, upper, chunks))
    last = strips_of([upper], False)
    where, last[0] = lax.optimization_barrier((where, last[0]))
    local, far, direct = chunks
    strips = list(zip(local, direct, far))
    sizes = [half_blocks, 2, 1]
    density, energy, later = place_early(where, strips, sizes, chips, per_core)
    return place_late(where, later, direct, last, density, energy, chips, per_core)


def solution(mesh):
    return jax.shard_map(
        body,
        mesh=mesh,
        in_specs=(P("atoms", "bands"), P("bands"), P("bands"), P("atoms", None)),
        out_specs=(P("atoms", None, "bands", None), P("atoms", None, "bands", None)),
        check_vma=False,
    )
```

```python
import functools

import jax
import jax.numpy as jnp
from jax import lax
from jax.experimental import pallas as pl
from jax.experimental.pallas import tpu as pltpu
from jax.sharding import PartitionSpec as P

R = 2
VMEM_LIMIT = 24 * 1024 * 1024
SOON = pl.CostEstimate(flops=0, bytes_accessed=0, transcendentals=0)


def in_hbm(value):
    return pltpu.with_memory_space_constraint(value, pltpu.HBM)


def in_vmem(value):
    return pltpu.with_memory_space_constraint(value, pltpu.VMEM)


def shifted(value, axis, steps):
    count = lax.axis_size(axis)
    pairs = [(source, (source + steps) % count) for source in range(count)]
    return lax.ppermute(value, axis, pairs)


def strip_target(group, chips, step, other_core):
    chip = lax.rem(lax.shift_right_logical(group, 1) + step, chips)
    return chip * 2 + ((group & 1) ^ other_core)


def to_strip_target(value, chips, step, other_core):
    pairs = [
        (group, (group // 2 + step) % chips * 2 + (group % 2 ^ other_core))
        for group in range(2 * chips)
    ]
    return lax.ppermute(value, "bands", pairs)


def pick_kernel(count, blocks, tile, parts, place_ref, *refs):
    asks, (own, sib), outs = refs[:count], refs[count : count + 2], refs[count + 2 : -1]
    sems = refs[-1]
    first = place_ref[0] * blocks
    copies = []
    for index in range(count):
        ids = asks[index][...] - first
        mine = (ids >= 0) & (ids < blocks)
        lowest = jnp.min(jnp.where(mine, ids, blocks - 1))
        highest = jnp.max(jnp.where(mine, ids, 0))
        block = jnp.where(place_ref[1] == 0, lowest, highest)
        for part in range(parts):
            height = tile // parts
            start = pl.multiple_of(block * tile + part * height, height)
            out = outs[index * parts + part]
            for half, source in enumerate((own, sib)):
                copy = pltpu.make_async_copy(
                    source.at[pl.ds(start, height), :],
                    out.at[half],
                    sems.at[index * parts + part, half],
                )
                copy.start()
                copies.append(copy)
    for copy in copies:
        copy.wait()


def pick(place, asks, own, sib, tile, parts):
    blocks, bands = asks[0].shape[0], own.shape[1]
    count = len(asks)
    n_outs = count * parts
    return pl.pallas_call(
        functools.partial(pick_kernel, count, blocks, tile, parts),
        out_shape=[pltpu.VMEM((2, tile // parts, bands), own.dtype)] * n_outs,
        in_specs=[pl.BlockSpec(memory_space=pltpu.SMEM)]
        + [pl.BlockSpec(memory_space=pltpu.VMEM)] * count
        + [pl.BlockSpec(memory_space=pl.ANY)] * 2,
        out_specs=[pl.BlockSpec(memory_space=pltpu.VMEM)] * n_outs,
        scratch_shapes=[pltpu.SemaphoreType.DMA((n_outs, 2))],
        name="pick_blocks",
        compiler_params=pltpu.CompilerParams(vmem_limit_bytes=VMEM_LIMIT),
        cost_estimate=SOON,
    )(place, *asks, in_hbm(own), in_hbm(sib))


def keep_kernel(own, sib, own_out, sib_out, sems):
    copies = []
    for half, (source, out) in enumerate(((own, own_out), (sib, sib_out))):
        copies.append(pltpu.make_async_copy(source, out, sems.at[half]))
    for copy in copies:
        copy.start()
    for copy in copies:
        copy.wait()


def keep(own, sib):
    return pl.pallas_call(
        keep_kernel,
        out_shape=[pltpu.VMEM(own.shape, own.dtype)] * 2,
        in_specs=[pl.BlockSpec(memory_space=pl.ANY)] * 2,
        out_specs=[pl.BlockSpec(memory_space=pltpu.VMEM)] * 2,
        scratch_shapes=[pltpu.SemaphoreType.DMA((2,))],
        name="keep",
        compiler_params=pltpu.CompilerParams(vmem_limit_bytes=VMEM_LIMIT),
        cost_estimate=SOON,
    )(in_hbm(own), in_hbm(sib))


def tiles_kernel(heights, n_arrived, n_strips, tile, paired, place_ref, *refs):
    lefts, weights = refs[:2], refs[2:4]
    arrived, refs = refs[4 : 4 + n_arrived], refs[4 + n_arrived :]
    outs, (scaled, total) = refs[:-2], refs[-2:]
    if paired:
        outs = outs[:2] + tuple(out.at[index] for out in outs[2:] for index in range(2))
    strip = tile // n_strips
    n_left = lefts[0].shape[0] // tile
    unit = 0
    for j, height in enumerate(heights):
        slot = j % 2
        for half in range(2):
            if n_arrived:
                block = arrived[j][half]
            else:
                first = pl.multiple_of((place_ref[0] * len(heights) + j) * tile, tile)
                block = lefts[half][pl.ds(first, tile), :]
            block = block.astype(jnp.float32)
            for kind in range(2):
                value = block * weights[half][kind : kind + 1, :]
                rows = pl.ds(kind * height, height)
                scaled[slot, half, rows, :] = value.astype(scaled.dtype)
        width = 2 * height
        for half in range(2):
            value = lax.dot_general(
                lefts[half][...],
                scaled[slot, half, :width, :],
                (((1,), (1,)), ((), ())),
                preferred_element_type=jnp.float32,
            )
            if half == 0:
                total[slot, :, :width] = value
            else:
                total[slot, :, :width] += value
        for lane in range(0, width, tile):
            for index in range(n_strips):
                start = place_ref[1 + index] * strip
                for i in range(n_left):
                    rows = pl.ds(pl.multiple_of(i * tile + start, strip), strip)
                    value = total[slot, rows, lane : lane + tile]
                    outs[index][unit, i] = value.astype(outs[index].dtype)
            unit += 1


def tiles(place, own, sib, arrived, weights, n_strips, tile, paired):
    rows, bands = own.shape
    blocks = rows // tile
    heights = [value.shape[1] for value in arrived] or [tile] * (blocks // 2)
    strip = tile // n_strips
    slots = min(len(heights), 2)
    vmem = pl.BlockSpec(memory_space=pltpu.VMEM)
    units = sum(2 * height // tile for height in heights)
    out = jax.ShapeDtypeStruct((units, blocks, strip, tile), jnp.bfloat16)
    pair = jax.ShapeDtypeStruct((2, *out.shape), out.dtype)
    outs = [out, out] + [pair] * (n_strips // 2 - 1) if paired else [out] * n_strips
    return pl.pallas_call(
        functools.partial(tiles_kernel, heights, len(arrived), n_strips, tile, paired),
        out_shape=outs,
        in_specs=[pl.BlockSpec(memory_space=pltpu.SMEM)] + [vmem] * (4 + len(arrived)),
        out_specs=[vmem] * len(outs),
        scratch_shapes=[
            pltpu.VMEM((slots, 2, 2 * max(heights), bands), jnp.bfloat16),
            pltpu.VMEM((slots, rows, 2 * max(heights)), jnp.float32),
        ],
        name="tiles",
        compiler_params=pltpu.CompilerParams(vmem_limit_bytes=VMEM_LIMIT),
        cost_estimate=SOON,
    )(place, in_vmem(own), in_vmem(sib), *weights, *arrived)


def strip_sum(ins, chips, n_chunks, other_core, chunk, unit, i):
    total = None
    for step in range(chips):
        ref = ins[(step * 2 + other_core) * n_chunks + chunk]
        value = ref[unit, i].astype(jnp.float32)
        total = value if total is None else total + value
    return total


def place_early_kernel(chips, sizes, per_core, where_ref, *refs):
    n_chunks = len(sizes)
    ins = refs[: 2 * chips * n_chunks]
    density, energy, later, pool = refs[2 * chips * n_chunks :]
    for other_core in range(2):
        first = other_core * per_core
        for chunk in range(n_chunks):
            for unit in range(2 * sizes[chunk]):
                pool[first + unit // 2, unit % 2] = strip_sum(
                    ins, chips, n_chunks, other_core, chunk, unit, 0
                )
            first += sizes[chunk]
    i = pl.program_id(0)
    slots = density.shape[1]

    @pl.when(i == 0)
    def _():
        later[0] = 0

    for slot in range(slots):
        where = where_ref[i, slot]
        density[0, slot] = pool[where, 0]
        energy[0, slot] = pool[where, 1]

        @pl.when(lax.rem(where, per_core) == per_core - 1)
        def _():
            count = later[0] + 1
            later[count] = i * slots + slot
            later[0] = count


def place_early(where, strips, sizes, chips, per_core):
    _, blocks, strip, tile = strips[0][0].shape
    slots = where.shape[1]
    out = jax.ShapeDtypeStruct((blocks, slots, strip, tile), jnp.float32)
    flat = [value for group in strips for value in group]
    return pl.pallas_call(
        functools.partial(place_early_kernel, chips, sizes, per_core),
        out_shape=[out, out, jax.ShapeDtypeStruct((blocks * slots + 1,), jnp.int32)],
        grid_spec=pltpu.PrefetchScalarGridSpec(
            num_scalar_prefetch=1,
            grid=(blocks,),
            in_specs=[
                pl.BlockSpec(
                    (value.shape[0], 1, strip, tile), lambda i, where: (0, i, 0, 0)
                )
                for value in flat
            ],
            out_specs=[
                pl.BlockSpec((1, slots, strip, tile), lambda i, where: (i, 0, 0, 0))
            ]
            * 2
            + [pl.BlockSpec(memory_space=pltpu.SMEM)],
            scratch_shapes=[pltpu.VMEM((2 * per_core, 2, strip, tile), jnp.float32)],
        ),
        name="place_early",
        compiler_params=pltpu.CompilerParams(vmem_limit_bytes=VMEM_LIMIT),
        cost_estimate=SOON,
    )(where, *flat)


def place_late_kernel(chips, per_core, where_ref, later, *refs):
    lower, upper = refs[: 2 * chips], refs[2 * chips : 4 * chips]
    density, energy, pool, sems = refs[4 * chips + 2 :]
    blocks, slots = density.shape[:2]
    cut = density.shape[3] // 2
    unit = lower[0].shape[0] - 1
    for other_core in range(2):
        for i in range(blocks):
            low = strip_sum(lower, chips, 1, other_core, 0, unit, i)
            high = strip_sum(upper, chips, 1, other_core, 0, 0, i)
            pool[other_core, i, 0] = jnp.concatenate([low[:, :cut], high[:, :cut]], 1)
            pool[other_core, i, 1] = jnp.concatenate([low[:, cut:], high[:, cut:]], 1)
    count = later[0]

    def copies(n):
        entry = jnp.clip(later[n + 1], 0, blocks * slots - 1)
        i, slot = lax.div(entry, slots), lax.rem(entry, slots)
        other_core = jnp.clip(lax.div(where_ref[i, slot], per_core), 0, 1)
        return [
            pltpu.make_async_copy(
                pool.at[other_core, i, kind], out.at[i, slot], sems.at[kind]
            )
            for kind, out in enumerate((density, energy))
        ]

    @pl.loop(0, count)
    def _(n):
        for copy in copies(n):
            copy.start()

    @pl.loop(0, count)
    def _(n):
        for copy in copies(n):
            copy.wait()


def place_late(where, later, lower, upper, density, energy, chips, per_core):
    blocks, _, strip, tile = density.shape
    smem = pl.BlockSpec(memory_space=pltpu.SMEM)
    anywhere = pl.BlockSpec(memory_space=pl.ANY)
    out = jax.ShapeDtypeStruct(density.shape, density.dtype)
    strips = [*lower, *upper]
    return pl.pallas_call(
        functools.partial(place_late_kernel, chips, per_core),
        out_shape=[out, out],
        in_specs=[smem, smem]
        + [pl.BlockSpec(memory_space=pltpu.VMEM)] * len(strips)
        + [anywhere] * 2,
        out_specs=[anywhere] * 2,
        scratch_shapes=[
            pltpu.VMEM((2, blocks, 2, strip, tile), jnp.float32),
            pltpu.SemaphoreType.DMA((2,)),
        ],
        input_output_aliases={2 + len(strips): 0, 3 + len(strips): 1},
        name="place_late",
        compiler_params=pltpu.CompilerParams(vmem_limit_bytes=VMEM_LIMIT),
        cost_estimate=SOON,
    )(where, later, *strips, density, energy)


def body(eigvecs, occupations, energies, neighbours):
    n_atoms = lax.axis_size("atoms")
    n_bands = lax.axis_size("bands")
    chips = n_bands // 2
    own_index = lax.axis_index("atoms").astype(jnp.int32)
    group = lax.axis_index("bands").astype(jnp.int32)
    core = group & 1
    blocks = neighbours.shape[0]
    tile = eigvecs.shape[0] // blocks
    half_blocks = blocks // 2
    offsets = [-1, 1, 2, -2]

    asks = [shifted(neighbours, "atoms", offset) for offset in offsets]
    sib = to_strip_target(eigvecs, chips, 0, 1)
    own_weights = jnp.stack([occupations, occupations * energies], 0)

    targets = [
        strip_target(group, chips, step, other)
        for step in range(chips)
        for other in range(2)
    ]
    here = jnp.stack([own_index, core]).astype(jnp.int32)
    place = jnp.stack([core] + targets).astype(jnp.int32)

    asks, own_weights = lax.optimization_barrier((asks, own_weights))
    weights = (own_weights, to_strip_target(own_weights, chips, 0, 1))
    picked = list(pick(here, asks[:3], eigvecs, sib, tile, 1))
    arrived = [
        shifted(value, "atoms", -offset) for value, offset in zip(picked, offsets)
    ]
    kept_eigvecs, picked[0] = lax.optimization_barrier((eigvecs, picked[0]))
    own, kept_sib = keep(kept_eigvecs, sib)

    def strips_of(arrived, paired):
        parts = list(tiles(place, own, kept_sib, arrived, weights, n_bands, tile, paired))
        for index in range(1, len(parts)):
            step, other = (max(index - 1, 0), index == 1) if paired else (index // 2, index % 2)
            parts[index] = to_strip_target(parts[index], chips, step, int(other))
        return parts

    def passed_on(parts):
        singles = parts[:2]
        for pair in parts[2:]:
            singles += [pair[0], to_strip_target(pair[1], chips, 0, 1)]
        return singles

    chunks = [strips_of((), True)]
    neighbours, here, chunks[0][0] = lax.optimization_barrier(
        (neighbours, here, chunks[0][0])
    )
    halves = list(pick(here, asks[3:], eigvecs, sib, tile, 2))

    owners = lax.div(neighbours, blocks)
    within = lax.rem(neighbours, blocks)
    distance = lax.rem(owners - own_index + n_atoms, n_atoms)
    spot = lax.rem(within, half_blocks)
    side = lax.div(within, half_blocks)
    for index, offset in enumerate(offsets):
        from_it = distance == offset % n_atoms
        highest = jnp.max(jnp.where(from_it, within, -1))
        side = jnp.where(from_it, (within == highest).astype(jnp.int32), side)
        spot = jnp.where(from_it, half_blocks + index, spot)
    per_core = half_blocks + len(offsets)
    where = ((side ^ core) * per_core + spot).astype(jnp.int32)

    *near, third = arrived
    third, halves, chunks[0][:1] = lax.optimization_barrier((third, halves, chunks[0][:1]))
    lower = shifted(halves[0], "atoms", -offsets[3])
    parts = list(tiles(place, own, kept_sib, [third], weights, n_bands, tile, True))
    pairs = [
        to_strip_target(pair, chips, step + 1, 0) for step, pair in enumerate(parts[2:])
    ]
    near, parts[:2], pairs, chunks, halves = lax.optimization_barrier((near, parts[:2], pairs, chunks, halves))
    upper = shifted(halves[1], "atoms", -offsets[3])
    chunks.append([parts[0], to_strip_target(parts[1], chips, 0, 1)] + pairs)
    chunks = [passed_on(chunk) for chunk in chunks]
    direct = strips_of(near, False)
    lower, direct[:2] = lax.optimization_barrier((lower, direct[:2]))
    lower = strips_of([lower], False)
    where, upper, lower[:2], chunks, direct = lax.optimization_barrier(
        (where, upper, lower[:2], chunks, direct)
    )
    chunks.append(direct)
    last = strips_of([upper], False)
    where, last[0] = lax.optimization_barrier((where, last[0]))
    local, far, direct = chunks
    strips = list(zip(local, direct, far))
    sizes = [half_blocks, 2, 1]
    density, energy, later = place_early(where, strips, sizes, chips, per_core)
    return place_late(where, later, lower, last, density, energy, chips, per_core)


def solution(mesh):
    return jax.shard_map(
        body,
        mesh=mesh,
        in_specs=(P("atoms", "bands"), P("bands"), P("bands"), P("atoms", None)),
        out_specs=(P("atoms", None, "bands", None), P("atoms", None, "bands", None)),
        check_vma=False,
    )
```

```python
import functools

import jax
import jax.numpy as jnp
from jax import lax
from jax.experimental import pallas as pl
from jax.experimental.pallas import tpu as pltpu
from jax.sharding import PartitionSpec as P

R = 2
VMEM_LIMIT = 24 * 1024 * 1024
SOON = pl.CostEstimate(flops=0, bytes_accessed=0, transcendentals=0)


def in_hbm(value):
    return pltpu.with_memory_space_constraint(value, pltpu.HBM)


def in_vmem(value):
    return pltpu.with_memory_space_constraint(value, pltpu.VMEM)


def shifted(value, axis, steps):
    count = lax.axis_size(axis)
    pairs = [(source, (source + steps) % count) for source in range(count)]
    return lax.ppermute(value, axis, pairs)


def strip_target(group, chips, step, other_core):
    chip = lax.rem(lax.shift_right_logical(group, 1) + step, chips)
    return chip * 2 + ((group & 1) ^ other_core)


def to_strip_target(value, chips, step, other_core):
    pairs = [
        (group, (group // 2 + step) % chips * 2 + (group % 2 ^ other_core))
        for group in range(2 * chips)
    ]
    return lax.ppermute(value, "bands", pairs)


def pick_kernel(count, blocks, tile, parts, place_ref, *refs):
    asks, (own, sib), outs = refs[:count], refs[count : count + 2], refs[count + 2 : -1]
    sems = refs[-1]
    first = place_ref[0] * blocks
    copies = []
    for index in range(count):
        ids = asks[index][...] - first
        mine = (ids >= 0) & (ids < blocks)
        lowest = jnp.min(jnp.where(mine, ids, blocks - 1))
        highest = jnp.max(jnp.where(mine, ids, 0))
        block = jnp.where(place_ref[1] == 0, lowest, highest)
        for part in range(parts):
            height = tile // parts
            start = pl.multiple_of(block * tile + part * height, height)
            out = outs[index * parts + part]
            for half, source in enumerate((own, sib)):
                copy = pltpu.make_async_copy(
                    source.at[pl.ds(start, height), :],
                    out.at[half],
                    sems.at[index * parts + part, half],
                )
                copy.start()
                copies.append(copy)
    for copy in copies:
        copy.wait()


def pick(place, asks, own, sib, tile, parts):
    blocks, bands = asks[0].shape[0], own.shape[1]
    count = len(asks)
    n_outs = count * parts
    return pl.pallas_call(
        functools.partial(pick_kernel, count, blocks, tile, parts),
        out_shape=[pltpu.VMEM((2, tile // parts, bands), own.dtype)] * n_outs,
        in_specs=[pl.BlockSpec(memory_space=pltpu.SMEM)]
        + [pl.BlockSpec(memory_space=pltpu.VMEM)] * count
        + [pl.BlockSpec(memory_space=pl.ANY)] * 2,
        out_specs=[pl.BlockSpec(memory_space=pltpu.VMEM)] * n_outs,
        scratch_shapes=[pltpu.SemaphoreType.DMA((n_outs, 2))],
        name="pick_blocks",
        compiler_params=pltpu.CompilerParams(vmem_limit_bytes=VMEM_LIMIT),
        cost_estimate=SOON,
    )(place, *asks, in_hbm(own), in_hbm(sib))


def keep_kernel(own, sib, own_out, sib_out, sems):
    copies = []
    for half, (source, out) in enumerate(((own, own_out), (sib, sib_out))):
        copies.append(pltpu.make_async_copy(source, out, sems.at[half]))
    for copy in copies:
        copy.start()
    for copy in copies:
        copy.wait()


def keep(own, sib):
    return pl.pallas_call(
        keep_kernel,
        out_shape=[pltpu.VMEM(own.shape, own.dtype)] * 2,
        in_specs=[pl.BlockSpec(memory_space=pl.ANY)] * 2,
        out_specs=[pl.BlockSpec(memory_space=pltpu.VMEM)] * 2,
        scratch_shapes=[pltpu.SemaphoreType.DMA((2,))],
        name="keep",
        compiler_params=pltpu.CompilerParams(vmem_limit_bytes=VMEM_LIMIT),
        cost_estimate=SOON,
    )(in_hbm(own), in_hbm(sib))


def tiles_kernel(heights, n_arrived, n_strips, tile, paired, place_ref, *refs):
    lefts, weights = refs[:2], refs[2:4]
    arrived, refs = refs[4 : 4 + n_arrived], refs[4 + n_arrived :]
    outs, (scaled, total) = refs[:-2], refs[-2:]
    if paired:
        outs = outs[:2] + tuple(out.at[index] for out in outs[2:] for index in range(2))
    strip = tile // n_strips
    n_left = lefts[0].shape[0] // tile
    unit = 0
    for j, height in enumerate(heights):
        slot = j % 2
        for half in range(2):
            if n_arrived:
                block = arrived[j][half]
            else:
                first = pl.multiple_of((place_ref[0] * len(heights) + j) * tile, tile)
                block = lefts[half][pl.ds(first, tile), :]
            block = block.astype(jnp.float32)
            for kind in range(2):
                value = block * weights[half][kind : kind + 1, :]
                rows = pl.ds(kind * height, height)
                scaled[slot, half, rows, :] = value.astype(scaled.dtype)
        width = 2 * height
        for half in range(2):
            value = lax.dot_general(
                lefts[half][...],
                scaled[slot, half, :width, :],
                (((1,), (1,)), ((), ())),
                preferred_element_type=jnp.float32,
            )
            if half == 0:
                total[slot, :, :width] = value
            else:
                total[slot, :, :width] += value
        for lane in range(0, width, tile):
            for index in range(n_strips):
                start = place_ref[1 + index] * strip
                for i in range(n_left):
                    rows = pl.ds(pl.multiple_of(i * tile + start, strip), strip)
                    value = total[slot, rows, lane : lane + tile]
                    outs[index][unit, i] = value.astype(outs[index].dtype)
            unit += 1


def tiles(place, own, sib, arrived, weights, n_strips, tile, paired):
    rows, bands = own.shape
    blocks = rows // tile
    heights = [value.shape[1] for value in arrived] or [tile] * (blocks // 2)
    strip = tile // n_strips
    slots = min(len(heights), 2)
    vmem = pl.BlockSpec(memory_space=pltpu.VMEM)
    units = sum(2 * height // tile for height in heights)
    out = jax.ShapeDtypeStruct((units, blocks, strip, tile), jnp.bfloat16)
    pair = jax.ShapeDtypeStruct((2, *out.shape), out.dtype)
    outs = [out, out] + [pair] * (n_strips // 2 - 1) if paired else [out] * n_strips
    return pl.pallas_call(
        functools.partial(tiles_kernel, heights, len(arrived), n_strips, tile, paired),
        out_shape=outs,
        in_specs=[pl.BlockSpec(memory_space=pltpu.SMEM)] + [vmem] * (4 + len(arrived)),
        out_specs=[vmem] * len(outs),
        scratch_shapes=[
            pltpu.VMEM((slots, 2, 2 * max(heights), bands), jnp.bfloat16),
            pltpu.VMEM((slots, rows, 2 * max(heights)), jnp.float32),
        ],
        name="tiles",
        compiler_params=pltpu.CompilerParams(vmem_limit_bytes=VMEM_LIMIT),
        cost_estimate=SOON,
    )(place, in_vmem(own), in_vmem(sib), *weights, *arrived)


def strip_sum(ins, chips, n_chunks, other_core, chunk, unit, i):
    total = None
    for step in range(chips):
        ref = ins[(step * 2 + other_core) * n_chunks + chunk]
        value = ref[unit, i].astype(jnp.float32)
        total = value if total is None else total + value
    return total


def place_early_kernel(chips, sizes, per_core, where_ref, *refs):
    n_chunks = len(sizes)
    ins = refs[: 2 * chips * n_chunks]
    density, energy, later, pool, tiles_out, sems = refs[2 * chips * n_chunks :]
    blocks, slots = density.shape[:2]
    later[0] = 0

    def copies(i, buffer):
        return [
            pltpu.make_async_copy(
                tiles_out.at[buffer, kind], out.at[i], sems.at[buffer, kind]
            )
            for kind, out in enumerate((density, energy))
        ]

    @pl.loop(0, blocks)
    def _(i):
        buffer = lax.rem(i, 2)
        for other_core in range(2):
            first = other_core * per_core
            for chunk in range(n_chunks):
                for unit in range(2 * sizes[chunk]):
                    pool[first + unit // 2, unit % 2] = strip_sum(
                        ins, chips, n_chunks, other_core, chunk, unit, i
                    )
                first += sizes[chunk]

        @pl.when(i >= 2)
        def _():
            for copy in copies(i - 2, buffer):
                copy.wait()

        for slot in range(slots):
            where = where_ref[i, slot]
            for kind in range(2):
                tiles_out[buffer, kind, slot] = pool[where, kind]

            @pl.when(lax.rem(where, per_core) == per_core - 1)
            def _():
                count = later[0] + 1
                later[count] = i * slots + slot
                later[0] = count

        for copy in copies(i, buffer):
            copy.start()

    for i in range(max(blocks - 2, 0), blocks):
        for copy in copies(i, i % 2):
            copy.wait()


def place_early(where, strips, sizes, chips, per_core):
    _, blocks, strip, tile = strips[0][0].shape
    slots = where.shape[1]
    out = jax.ShapeDtypeStruct((blocks, slots, strip, tile), jnp.float32)
    flat = [value for group in strips for value in group]
    smem = pl.BlockSpec(memory_space=pltpu.SMEM)
    return pl.pallas_call(
        functools.partial(place_early_kernel, chips, sizes, per_core),
        out_shape=[out, out, jax.ShapeDtypeStruct((blocks * slots + 1,), jnp.int32)],
        in_specs=[smem] + [pl.BlockSpec(memory_space=pltpu.VMEM)] * len(flat),
        out_specs=[pl.BlockSpec(memory_space=pl.ANY)] * 2 + [smem],
        scratch_shapes=[
            pltpu.VMEM((2 * per_core, 2, strip, tile), jnp.float32),
            pltpu.VMEM((2, 2, slots, strip, tile), jnp.float32),
            pltpu.SemaphoreType.DMA((2, 2)),
        ],
        name="place_early",
        compiler_params=pltpu.CompilerParams(vmem_limit_bytes=VMEM_LIMIT),
        cost_estimate=SOON,
    )(where, *flat)


def place_late_kernel(chips, per_core, where_ref, later, *refs):
    lower, upper = refs[: 2 * chips], refs[2 * chips : 4 * chips]
    density, energy, pool, sems = refs[4 * chips + 2 :]
    blocks, slots = density.shape[:2]
    cut = density.shape[3] // 2
    unit = lower[0].shape[0] - 1
    for other_core in range(2):
        for i in range(blocks):
            low = strip_sum(lower, chips, 1, other_core, 0, unit, i)
            high = strip_sum(upper, chips, 1, other_core, 0, 0, i)
            pool[other_core, i, 0] = jnp.concatenate([low[:, :cut], high[:, :cut]], 1)
            pool[other_core, i, 1] = jnp.concatenate([low[:, cut:], high[:, cut:]], 1)
    count = later[0]

    def copies(n):
        entry = jnp.clip(later[n + 1], 0, blocks * slots - 1)
        i, slot = lax.div(entry, slots), lax.rem(entry, slots)
        other_core = jnp.clip(lax.div(where_ref[i, slot], per_core), 0, 1)
        return [
            pltpu.make_async_copy(
                pool.at[other_core, i, kind], out.at[i, slot], sems.at[kind]
            )
            for kind, out in enumerate((density, energy))
        ]

    @pl.loop(0, count)
    def _(n):
        for copy in copies(n):
            copy.start()

    @pl.loop(0, count)
    def _(n):
        for copy in copies(n):
            copy.wait()


def place_late(where, later, lower, upper, density, energy, chips, per_core):
    blocks, _, strip, tile = density.shape
    smem = pl.BlockSpec(memory_space=pltpu.SMEM)
    anywhere = pl.BlockSpec(memory_space=pl.ANY)
    out = jax.ShapeDtypeStruct(density.shape, density.dtype)
    strips = [*lower, *upper]
    return pl.pallas_call(
        functools.partial(place_late_kernel, chips, per_core),
        out_shape=[out, out],
        in_specs=[smem, smem]
        + [pl.BlockSpec(memory_space=pltpu.VMEM)] * len(strips)
        + [anywhere] * 2,
        out_specs=[anywhere] * 2,
        scratch_shapes=[
            pltpu.VMEM((2, blocks, 2, strip, tile), jnp.float32),
            pltpu.SemaphoreType.DMA((2,)),
        ],
        input_output_aliases={2 + len(strips): 0, 3 + len(strips): 1},
        name="place_late",
        compiler_params=pltpu.CompilerParams(vmem_limit_bytes=VMEM_LIMIT),
        cost_estimate=SOON,
    )(where, later, *strips, density, energy)


def body(eigvecs, occupations, energies, neighbours):
    n_atoms = lax.axis_size("atoms")
    n_bands = lax.axis_size("bands")
    chips = n_bands // 2
    own_index = lax.axis_index("atoms").astype(jnp.int32)
    group = lax.axis_index("bands").astype(jnp.int32)
    core = group & 1
    blocks = neighbours.shape[0]
    tile = eigvecs.shape[0] // blocks
    half_blocks = blocks // 2
    offsets = [-1, 1, 2, -2]

    asks = [shifted(neighbours, "atoms", offset) for offset in offsets]
    sib = to_strip_target(eigvecs, chips, 0, 1)
    own_weights = jnp.stack([occupations, occupations * energies], 0)

    targets = [
        strip_target(group, chips, step, other)
        for step in range(chips)
        for other in range(2)
    ]
    here = jnp.stack([own_index, core]).astype(jnp.int32)
    place = jnp.stack([core] + targets).astype(jnp.int32)

    asks, own_weights = lax.optimization_barrier((asks, own_weights))
    weights = (own_weights, to_strip_target(own_weights, chips, 0, 1))
    picked = list(pick(here, asks[:3], eigvecs, sib, tile, 1))
    arrived = [
        shifted(value, "atoms", -offset) for value, offset in zip(picked, offsets)
    ]
    kept_eigvecs, picked[0] = lax.optimization_barrier((eigvecs, picked[0]))
    own, kept_sib = keep(kept_eigvecs, sib)

    def strips_of(arrived, paired):
        parts = list(tiles(place, own, kept_sib, arrived, weights, n_bands, tile, paired))
        for index in range(1, len(parts)):
            step, other = (max(index - 1, 0), index == 1) if paired else (index // 2, index % 2)
            parts[index] = to_strip_target(parts[index], chips, step, int(other))
        return parts

    def passed_on(parts):
        singles = parts[:2]
        for pair in parts[2:]:
            singles += [pair[0], to_strip_target(pair[1], chips, 0, 1)]
        return singles

    chunks = [strips_of((), True)]
    neighbours, here, chunks[0][0] = lax.optimization_barrier(
        (neighbours, here, chunks[0][0])
    )
    halves = list(pick(here, asks[3:], eigvecs, sib, tile, 2))

    owners = lax.div(neighbours, blocks)
    within = lax.rem(neighbours, blocks)
    distance = lax.rem(owners - own_index + n_atoms, n_atoms)
    spot = lax.rem(within, half_blocks)
    side = lax.div(within, half_blocks)
    for index, offset in enumerate(offsets):
        from_it = distance == offset % n_atoms
        highest = jnp.max(jnp.where(from_it, within, -1))
        side = jnp.where(from_it, (within == highest).astype(jnp.int32), side)
        spot = jnp.where(from_it, half_blocks + index, spot)
    per_core = half_blocks + len(offsets)
    where = ((side ^ core) * per_core + spot).astype(jnp.int32)

    *near, third = arrived
    third, halves, chunks[0][:1] = lax.optimization_barrier((third, halves, chunks[0][:1]))
    lower = shifted(halves[0], "atoms", -offsets[3])
    parts = list(tiles(place, own, kept_sib, [third], weights, n_bands, tile, True))
    pairs = [
        to_strip_target(pair, chips, step + 1, 0) for step, pair in enumerate(parts[2:])
    ]
    near, where, parts[:2], pairs, chunks, halves = lax.optimization_barrier(
        (near, where, parts[:2], pairs, chunks, halves)
    )
    upper = shifted(halves[1], "atoms", -offsets[3])
    chunks.append([parts[0], to_strip_target(parts[1], chips, 0, 1)] + pairs)
    chunks = [passed_on(chunk) for chunk in chunks]
    direct = strips_of(near, False)
    lower, direct[:2], chunks = lax.optimization_barrier((lower, direct[:2], chunks))
    lower = list(tiles(place, own, kept_sib, [lower], weights, n_bands, tile, False))
    lower_sib = lower[1]
    for index in range(2, n_bands):
        lower[index] = to_strip_target(lower[index], chips, index // 2, index % 2)
    where, upper, lower[0], direct = lax.optimization_barrier(
        (where, upper, lower[0], direct)
    )
    chunks.append(direct)
    last = strips_of([upper], False)
    where, last[0] = lax.optimization_barrier((where, last[0]))
    lower[1] = to_strip_target(lower_sib, chips, 0, 1)
    where, lower = lax.optimization_barrier((where, lower))
    local, far, direct = chunks
    strips = list(zip(local, direct, far))
    sizes = [half_blocks, 2, 1]
    density, energy, later = place_early(where, strips, sizes, chips, per_core)
    return place_late(where, later, lower, last, density, energy, chips, per_core)


def solution(mesh):
    return jax.shard_map(
        body,
        mesh=mesh,
        in_specs=(P("atoms", "bands"), P("bands"), P("bands"), P("atoms", None)),
        out_specs=(P("atoms", None, "bands", None), P("atoms", None, "bands", None)),
        check_vma=False,
    )
```

```python
import functools

import jax
import jax.numpy as jnp
from jax import lax
from jax.experimental import pallas as pl
from jax.experimental.pallas import tpu as pltpu
from jax.sharding import PartitionSpec as P

R = 2
VMEM_LIMIT = 24 * 1024 * 1024
SOON = pl.CostEstimate(flops=0, bytes_accessed=0, transcendentals=0)


def in_hbm(value):
    return pltpu.with_memory_space_constraint(value, pltpu.HBM)


def in_vmem(value):
    return pltpu.with_memory_space_constraint(value, pltpu.VMEM)


def shifted(value, axis, steps):
    count = lax.axis_size(axis)
    pairs = [(source, (source + steps) % count) for source in range(count)]
    return lax.ppermute(value, axis, pairs)


def strip_target(group, chips, step, other_core):
    chip = lax.rem(lax.shift_right_logical(group, 1) + step, chips)
    return chip * 2 + ((group & 1) ^ other_core)


def to_strip_target(value, chips, step, other_core):
    pairs = [
        (group, (group // 2 + step) % chips * 2 + (group % 2 ^ other_core))
        for group in range(2 * chips)
    ]
    return lax.ppermute(value, "bands", pairs)


def pick_kernel(count, blocks, tile, parts, place_ref, *refs):
    asks, (own, sib), outs = refs[:count], refs[count : count + 2], refs[count + 2 : -1]
    sems = refs[-1]
    first = place_ref[0] * blocks
    copies = []
    for index in range(count):
        ids = asks[index][...] - first
        mine = (ids >= 0) & (ids < blocks)
        lowest = jnp.min(jnp.where(mine, ids, blocks - 1))
        highest = jnp.max(jnp.where(mine, ids, 0))
        block = jnp.where(place_ref[1] == 0, lowest, highest)
        for part in range(parts):
            height = tile // parts
            start = pl.multiple_of(block * tile + part * height, height)
            out = outs[index * parts + part]
            for half, source in enumerate((own, sib)):
                copy = pltpu.make_async_copy(
                    source.at[pl.ds(start, height), :],
                    out.at[half],
                    sems.at[index * parts + part, half],
                )
                copy.start()
                copies.append(copy)
    for copy in copies:
        copy.wait()


def pick(place, asks, own, sib, tile, parts):
    blocks, bands = asks[0].shape[0], own.shape[1]
    count = len(asks)
    n_outs = count * parts
    return pl.pallas_call(
        functools.partial(pick_kernel, count, blocks, tile, parts),
        out_shape=[pltpu.VMEM((2, tile // parts, bands), own.dtype)] * n_outs,
        in_specs=[pl.BlockSpec(memory_space=pltpu.SMEM)]
        + [pl.BlockSpec(memory_space=pltpu.VMEM)] * count
        + [pl.BlockSpec(memory_space=pl.ANY)] * 2,
        out_specs=[pl.BlockSpec(memory_space=pltpu.VMEM)] * n_outs,
        scratch_shapes=[pltpu.SemaphoreType.DMA((n_outs, 2))],
        name="pick_blocks",
        compiler_params=pltpu.CompilerParams(vmem_limit_bytes=VMEM_LIMIT),
        cost_estimate=SOON,
    )(place, *asks, in_hbm(own), in_hbm(sib))


def keep_kernel(own, sib, own_out, sib_out, sems):
    copies = []
    for half, (source, out) in enumerate(((own, own_out), (sib, sib_out))):
        copies.append(pltpu.make_async_copy(source, out, sems.at[half]))
    for copy in copies:
        copy.start()
    for copy in copies:
        copy.wait()


def keep(own, sib):
    return pl.pallas_call(
        keep_kernel,
        out_shape=[pltpu.VMEM(own.shape, own.dtype)] * 2,
        in_specs=[pl.BlockSpec(memory_space=pl.ANY)] * 2,
        out_specs=[pl.BlockSpec(memory_space=pltpu.VMEM)] * 2,
        scratch_shapes=[pltpu.SemaphoreType.DMA((2,))],
        name="keep",
        compiler_params=pltpu.CompilerParams(vmem_limit_bytes=VMEM_LIMIT),
        cost_estimate=SOON,
    )(in_hbm(own), in_hbm(sib))


def tiles_kernel(heights, n_arrived, n_strips, tile, paired, place_ref, *refs):
    lefts, weights = refs[:2], refs[2:4]
    arrived, refs = refs[4 : 4 + n_arrived], refs[4 + n_arrived :]
    outs, (scaled, total) = refs[:-2], refs[-2:]
    if paired:
        outs = outs[:2] + tuple(out.at[index] for out in outs[2:] for index in range(2))
    strip = tile // n_strips
    n_left = lefts[0].shape[0] // tile
    unit = 0
    for j, height in enumerate(heights):
        slot = j % 2
        for half in range(2):
            if n_arrived:
                block = arrived[j][half]
            else:
                first = pl.multiple_of((place_ref[0] * len(heights) + j) * tile, tile)
                block = lefts[half][pl.ds(first, tile), :]
            block = block.astype(jnp.float32)
            for kind in range(2):
                value = block * weights[half][kind : kind + 1, :]
                rows = pl.ds(kind * height, height)
                scaled[slot, half, rows, :] = value.astype(scaled.dtype)
        width = 2 * height
        for half in range(2):
            value = lax.dot_general(
                lefts[half][...],
                scaled[slot, half, :width, :],
                (((1,), (1,)), ((), ())),
                preferred_element_type=jnp.float32,
            )
            if half == 0:
                total[slot, :, :width] = value
            else:
                total[slot, :, :width] += value
        for lane in range(0, width, tile):
            for index in range(n_strips):
                start = place_ref[1 + index] * strip
                for i in range(n_left):
                    rows = pl.ds(pl.multiple_of(i * tile + start, strip), strip)
                    value = total[slot, rows, lane : lane + tile]
                    outs[index][unit, i] = value.astype(outs[index].dtype)
            unit += 1


def tiles(place, own, sib, arrived, weights, n_strips, tile, paired):
    rows, bands = own.shape
    blocks = rows // tile
    heights = [value.shape[1] for value in arrived] or [tile] * (blocks // 2)
    strip = tile // n_strips
    slots = min(len(heights), 2)
    vmem = pl.BlockSpec(memory_space=pltpu.VMEM)
    units = sum(2 * height // tile for height in heights)
    out = jax.ShapeDtypeStruct((units, blocks, strip, tile), jnp.bfloat16)
    pair = jax.ShapeDtypeStruct((2, *out.shape), out.dtype)
    outs = [out, out] + [pair] * (n_strips // 2 - 1) if paired else [out] * n_strips
    return pl.pallas_call(
        functools.partial(tiles_kernel, heights, len(arrived), n_strips, tile, paired),
        out_shape=outs,
        in_specs=[pl.BlockSpec(memory_space=pltpu.SMEM)] + [vmem] * (4 + len(arrived)),
        out_specs=[vmem] * len(outs),
        scratch_shapes=[
            pltpu.VMEM((slots, 2, 2 * max(heights), bands), jnp.bfloat16),
            pltpu.VMEM((slots, rows, 2 * max(heights)), jnp.float32),
        ],
        name="tiles",
        compiler_params=pltpu.CompilerParams(vmem_limit_bytes=VMEM_LIMIT),
        cost_estimate=SOON,
    )(place, in_vmem(own), in_vmem(sib), *weights, *arrived)


def strip_sum(ins, chips, n_chunks, other_core, chunk, unit, i):
    total = None
    for step in range(chips):
        ref = ins[(step * 2 + other_core) * n_chunks + chunk]
        value = ref[unit, i].astype(jnp.float32)
        total = value if total is None else total + value
    return total


def list_kernel(per_core, where_ref, later):
    blocks, slots = where_ref.shape

    def step(entry, count):
        where = where_ref[lax.div(entry, slots), lax.rem(entry, slots)]
        later[count + 1] = entry
        return count + (lax.rem(where, per_core) == per_core - 1).astype(jnp.int32)

    later[0] = lax.fori_loop(0, blocks * slots, step, 0)


def list_open(where, per_core):
    smem = pl.BlockSpec(memory_space=pltpu.SMEM)
    return pl.pallas_call(
        functools.partial(list_kernel, per_core),
        out_shape=jax.ShapeDtypeStruct((where.size + 1,), jnp.int32),
        in_specs=[smem],
        out_specs=smem,
        name="list_open",
        cost_estimate=SOON,
    )(where)


def place_early_kernel(chips, sizes, per_core, where_ref, *refs):
    n_chunks = len(sizes)
    ins = refs[: 2 * chips * n_chunks]
    density, energy, pool, tiles_out, sems = refs[2 * chips * n_chunks :]
    blocks, slots = density.shape[:2]

    def copies(i, buffer):
        return [
            pltpu.make_async_copy(
                tiles_out.at[buffer, kind], out.at[i], sems.at[buffer, kind]
            )
            for kind, out in enumerate((density, energy))
        ]

    @pl.loop(0, blocks)
    def _(i):
        buffer = lax.rem(i, 2)
        for other_core in range(2):
            first = other_core * per_core
            for chunk in range(n_chunks):
                for unit in range(2 * sizes[chunk]):
                    pool[first + unit // 2, unit % 2] = strip_sum(
                        ins, chips, n_chunks, other_core, chunk, unit, i
                    )
                first += sizes[chunk]

        @pl.when(i >= 2)
        def _():
            for copy in copies(i - 2, buffer):
                copy.wait()

        for slot in range(slots):
            where = where_ref[i, slot]
            for kind in range(2):
                tiles_out[buffer, kind, slot] = pool[where, kind]

        for copy in copies(i, buffer):
            copy.start()

    for i in range(max(blocks - 2, 0), blocks):
        for copy in copies(i, i % 2):
            copy.wait()


def place_early(where, strips, sizes, chips, per_core):
    _, blocks, strip, tile = strips[0][0].shape
    slots = where.shape[1]
    out = jax.ShapeDtypeStruct((blocks, slots, strip, tile), jnp.float32)
    flat = [value for group in strips for value in group]
    smem = pl.BlockSpec(memory_space=pltpu.SMEM)
    return pl.pallas_call(
        functools.partial(place_early_kernel, chips, sizes, per_core),
        out_shape=[out, out],
        in_specs=[smem] + [pl.BlockSpec(memory_space=pltpu.VMEM)] * len(flat),
        out_specs=[pl.BlockSpec(memory_space=pl.ANY)] * 2,
        scratch_shapes=[
            pltpu.VMEM((2 * per_core, 2, strip, tile), jnp.float32),
            pltpu.VMEM((2, 2, slots, strip, tile), jnp.float32),
            pltpu.SemaphoreType.DMA((2, 2)),
        ],
        name="place_early",
        compiler_params=pltpu.CompilerParams(vmem_limit_bytes=VMEM_LIMIT),
        cost_estimate=SOON,
    )(where, *flat)


def place_late_kernel(chips, per_core, where_ref, later, *refs):
    lower, upper = refs[: 2 * chips], refs[2 * chips : 4 * chips]
    density, energy, pool, sems = refs[4 * chips + 2 :]
    blocks, slots = density.shape[:2]
    cut = density.shape[3] // 2
    unit = lower[0].shape[0] - 1
    for other_core in range(2):
        for i in range(blocks):
            low = strip_sum(lower, chips, 1, other_core, 0, unit, i)
            high = strip_sum(upper, chips, 1, other_core, 0, 0, i)
            pool[other_core, i, 0] = jnp.concatenate([low[:, :cut], high[:, :cut]], 1)
            pool[other_core, i, 1] = jnp.concatenate([low[:, cut:], high[:, cut:]], 1)
    count = later[0]

    def copies(n):
        entry = jnp.clip(later[n + 1], 0, blocks * slots - 1)
        i, slot = lax.div(entry, slots), lax.rem(entry, slots)
        other_core = jnp.clip(lax.div(where_ref[i, slot], per_core), 0, 1)
        return [
            pltpu.make_async_copy(
                pool.at[other_core, i, kind], out.at[i, slot], sems.at[kind]
            )
            for kind, out in enumerate((density, energy))
        ]

    @pl.loop(0, count)
    def _(n):
        for copy in copies(n):
            copy.start()

    @pl.loop(0, count)
    def _(n):
        for copy in copies(n):
            copy.wait()


def place_late(where, later, lower, upper, density, energy, chips, per_core):
    blocks, _, strip, tile = density.shape
    smem = pl.BlockSpec(memory_space=pltpu.SMEM)
    anywhere = pl.BlockSpec(memory_space=pl.ANY)
    out = jax.ShapeDtypeStruct(density.shape, density.dtype)
    strips = [*lower, *upper]
    return pl.pallas_call(
        functools.partial(place_late_kernel, chips, per_core),
        out_shape=[out, out],
        in_specs=[smem, smem]
        + [pl.BlockSpec(memory_space=pltpu.VMEM)] * len(strips)
        + [anywhere] * 2,
        out_specs=[anywhere] * 2,
        scratch_shapes=[
            pltpu.VMEM((2, blocks, 2, strip, tile), jnp.float32),
            pltpu.SemaphoreType.DMA((2,)),
        ],
        input_output_aliases={2 + len(strips): 0, 3 + len(strips): 1},
        name="place_late",
        compiler_params=pltpu.CompilerParams(vmem_limit_bytes=VMEM_LIMIT),
        cost_estimate=SOON,
    )(where, later, *strips, density, energy)


def body(eigvecs, occupations, energies, neighbours):
    n_atoms = lax.axis_size("atoms")
    n_bands = lax.axis_size("bands")
    chips = n_bands // 2
    own_index = lax.axis_index("atoms").astype(jnp.int32)
    group = lax.axis_index("bands").astype(jnp.int32)
    core = group & 1
    blocks = neighbours.shape[0]
    tile = eigvecs.shape[0] // blocks
    half_blocks = blocks // 2
    offsets = [-1, 1, 2, -2]

    asks = [shifted(neighbours, "atoms", offset) for offset in offsets]
    sib = to_strip_target(eigvecs, chips, 0, 1)
    own_weights = jnp.stack([occupations, occupations * energies], 0)

    targets = [
        strip_target(group, chips, step, other)
        for step in range(chips)
        for other in range(2)
    ]
    here = jnp.stack([own_index, core]).astype(jnp.int32)
    place = jnp.stack([core] + targets).astype(jnp.int32)

    asks, own_weights = lax.optimization_barrier((asks, own_weights))
    weights = (own_weights, to_strip_target(own_weights, chips, 0, 1))
    picked = list(pick(here, asks[2:3], eigvecs, sib, tile, 1))
    here, picked[0] = lax.optimization_barrier((here, picked[0]))
    picked = list(pick(here, asks[:2], eigvecs, sib, tile, 1)) + picked
    arrived = [
        shifted(value, "atoms", -offset) for value, offset in zip(picked, offsets)
    ]
    kept_eigvecs, picked[0] = lax.optimization_barrier((eigvecs, picked[0]))
    own, kept_sib = keep(kept_eigvecs, sib)

    def strips_of(arrived, paired):
        parts = list(tiles(place, own, kept_sib, arrived, weights, n_bands, tile, paired))
        for index in range(1, len(parts)):
            step, other = (max(index - 1, 0), index == 1) if paired else (index // 2, index % 2)
            parts[index] = to_strip_target(parts[index], chips, step, int(other))
        return parts

    def passed_on(parts):
        singles = parts[:2]
        for pair in parts[2:]:
            singles += [pair[0], to_strip_target(pair[1], chips, 0, 1)]
        return singles

    chunks = [strips_of((), True)]
    neighbours, here, chunks[0][0] = lax.optimization_barrier(
        (neighbours, here, chunks[0][0])
    )
    halves = list(pick(here, asks[3:], eigvecs, sib, tile, 2))

    owners = lax.div(neighbours, blocks)
    within = lax.rem(neighbours, blocks)
    distance = lax.rem(owners - own_index + n_atoms, n_atoms)
    spot = lax.rem(within, half_blocks)
    side = lax.div(within, half_blocks)
    for index, offset in enumerate(offsets):
        from_it = distance == offset % n_atoms
        highest = jnp.max(jnp.where(from_it, within, -1))
        side = jnp.where(from_it, (within == highest).astype(jnp.int32), side)
        spot = jnp.where(from_it, half_blocks + index, spot)
    per_core = half_blocks + len(offsets)
    where = ((side ^ core) * per_core + spot).astype(jnp.int32)

    *near, third = arrived
    third, halves, chunks[0][:1] = lax.optimization_barrier((third, halves, chunks[0][:1]))
    lower = shifted(halves[0], "atoms", -offsets[3])
    parts = list(tiles(place, own, kept_sib, [third], weights, n_bands, tile, True))
    pairs = [
        to_strip_target(pair, chips, step + 1, 0) for step, pair in enumerate(parts[2:])
    ]
    later = list_open(where, per_core)
    near, where, later, parts[:2], pairs, chunks, halves = lax.optimization_barrier(
        (near, where, later, parts[:2], pairs, chunks, halves)
    )
    upper = shifted(halves[1], "atoms", -offsets[3])
    chunks.append([parts[0], to_strip_target(parts[1], chips, 0, 1)] + pairs)
    chunks = [passed_on(chunk) for chunk in chunks]
    direct = strips_of(near, False)
    lower, direct[:2], chunks = lax.optimization_barrier((lower, direct[:2], chunks))
    lower = list(tiles(place, own, kept_sib, [lower], weights, n_bands, tile, False))
    lower_sib = lower[1]
    for index in range(2, n_bands):
        lower[index] = to_strip_target(lower[index], chips, index // 2, index % 2)
    where, upper, lower[0], direct[:3] = lax.optimization_barrier(
        (where, upper, lower[0], direct[:3])
    )
    chunks.append(direct)
    last = strips_of([upper], False)
    where, last[0] = lax.optimization_barrier((where, last[0]))
    lower[1] = to_strip_target(lower_sib, chips, 0, 1)
    where, lower = lax.optimization_barrier((where, lower))
    local, far, direct = chunks
    strips = list(zip(local, direct, far))
    sizes = [half_blocks, 2, 1]
    density, energy = place_early(where, strips, sizes, chips, per_core)
    return place_late(where, later, lower, last, density, energy, chips, per_core)


def solution(mesh):
    return jax.shard_map(
        body,
        mesh=mesh,
        in_specs=(P("atoms", "bands"), P("bands"), P("bands"), P("atoms", None)),
        out_specs=(P("atoms", None, "bands", None), P("atoms", None, "bands", None)),
        check_vma=False,
    )
```

```python
import functools

import jax
import jax.numpy as jnp
from jax import lax
from jax.experimental import pallas as pl
from jax.experimental.pallas import tpu as pltpu
from jax.sharding import PartitionSpec as P

R = 2
VMEM_LIMIT = 24 * 1024 * 1024
SOON = pl.CostEstimate(flops=0, bytes_accessed=0, transcendentals=0)


def in_hbm(value):
    return pltpu.with_memory_space_constraint(value, pltpu.HBM)


def in_vmem(value):
    return pltpu.with_memory_space_constraint(value, pltpu.VMEM)


def shifted(value, axis, steps):
    count = lax.axis_size(axis)
    pairs = [(source, (source + steps) % count) for source in range(count)]
    return lax.ppermute(value, axis, pairs)


def strip_target(group, chips, step, other_core):
    chip = lax.rem(lax.shift_right_logical(group, 1) + step, chips)
    return chip * 2 + ((group & 1) ^ other_core)


def to_strip_target(value, chips, step, other_core):
    pairs = [
        (group, (group // 2 + step) % chips * 2 + (group % 2 ^ other_core))
        for group in range(2 * chips)
    ]
    return lax.ppermute(value, "bands", pairs)


def pick_kernel(count, blocks, tile, parts, place_ref, *refs):
    asks, (own, sib), outs = refs[:count], refs[count : count + 2], refs[count + 2 : -1]
    sems = refs[-1]
    first = place_ref[0] * blocks
    copies = []
    for index in range(count):
        ids = asks[index][...] - first
        mine = (ids >= 0) & (ids < blocks)
        lowest = jnp.min(jnp.where(mine, ids, blocks - 1))
        highest = jnp.max(jnp.where(mine, ids, 0))
        block = jnp.where(place_ref[1] == 0, lowest, highest)
        for part in range(parts):
            height = tile // parts
            start = pl.multiple_of(block * tile + part * height, height)
            out = outs[index * parts + part]
            for half, source in enumerate((own, sib)):
                copy = pltpu.make_async_copy(
                    source.at[pl.ds(start, height), :],
                    out.at[half],
                    sems.at[index * parts + part, half],
                )
                copy.start()
                copies.append(copy)
    for copy in copies:
        copy.wait()


def pick(place, asks, own, sib, tile, parts):
    blocks, bands = asks[0].shape[0], own.shape[1]
    count = len(asks)
    n_outs = count * parts
    return pl.pallas_call(
        functools.partial(pick_kernel, count, blocks, tile, parts),
        out_shape=[pltpu.VMEM((2, tile // parts, bands), own.dtype)] * n_outs,
        in_specs=[pl.BlockSpec(memory_space=pltpu.SMEM)]
        + [pl.BlockSpec(memory_space=pltpu.VMEM)] * count
        + [pl.BlockSpec(memory_space=pl.ANY)] * 2,
        out_specs=[pl.BlockSpec(memory_space=pltpu.VMEM)] * n_outs,
        scratch_shapes=[pltpu.SemaphoreType.DMA((n_outs, 2))],
        name="pick_blocks",
        compiler_params=pltpu.CompilerParams(vmem_limit_bytes=VMEM_LIMIT),
        cost_estimate=SOON,
    )(place, *asks, in_hbm(own), in_hbm(sib))


def keep_kernel(own, sib, own_out, sib_out, sems):
    copies = []
    for half, (source, out) in enumerate(((own, own_out), (sib, sib_out))):
        copies.append(pltpu.make_async_copy(source, out, sems.at[half]))
    for copy in copies:
        copy.start()
    for copy in copies:
        copy.wait()


def keep(own, sib):
    return pl.pallas_call(
        keep_kernel,
        out_shape=[pltpu.VMEM(own.shape, own.dtype)] * 2,
        in_specs=[pl.BlockSpec(memory_space=pl.ANY)] * 2,
        out_specs=[pl.BlockSpec(memory_space=pltpu.VMEM)] * 2,
        scratch_shapes=[pltpu.SemaphoreType.DMA((2,))],
        name="keep",
        compiler_params=pltpu.CompilerParams(vmem_limit_bytes=VMEM_LIMIT),
        cost_estimate=SOON,
    )(in_hbm(own), in_hbm(sib))


def tiles_kernel(heights, n_arrived, n_strips, tile, paired, place_ref, *refs):
    lefts, weights = refs[:2], refs[2:4]
    arrived, refs = refs[4 : 4 + n_arrived], refs[4 + n_arrived :]
    outs, (scaled, total) = refs[:-2], refs[-2:]
    if paired:
        outs = outs[:2] + tuple(out.at[index] for out in outs[2:] for index in range(2))
    strip = tile // n_strips
    n_left = lefts[0].shape[0] // tile
    unit = 0
    for j, height in enumerate(heights):
        slot = j % 2
        for half in range(2):
            if n_arrived:
                block = arrived[j][half]
            else:
                first = pl.multiple_of((place_ref[0] * len(heights) + j) * tile, tile)
                block = lefts[half][pl.ds(first, tile), :]
            block = block.astype(jnp.float32)
            for kind in range(2):
                value = block * weights[half][kind : kind + 1, :]
                rows = pl.ds(kind * height, height)
                scaled[slot, half, rows, :] = value.astype(scaled.dtype)
        width = 2 * height
        for half in range(2):
            value = lax.dot_general(
                lefts[half][...],
                scaled[slot, half, :width, :],
                (((1,), (1,)), ((), ())),
                preferred_element_type=jnp.float32,
            )
            if half == 0:
                total[slot, :, :width] = value
            else:
                total[slot, :, :width] += value
        for lane in range(0, width, tile):
            for index in range(n_strips):
                start = place_ref[1 + index] * strip
                for i in range(n_left):
                    rows = pl.ds(pl.multiple_of(i * tile + start, strip), strip)
                    value = total[slot, rows, lane : lane + tile]
                    outs[index][unit, i] = value.astype(outs[index].dtype)
            unit += 1


def tiles(place, own, sib, arrived, weights, n_strips, tile, paired):
    rows, bands = own.shape
    blocks = rows // tile
    heights = [value.shape[1] for value in arrived] or [tile] * (blocks // 2)
    strip = tile // n_strips
    slots = min(len(heights), 2)
    vmem = pl.BlockSpec(memory_space=pltpu.VMEM)
    units = sum(2 * height // tile for height in heights)
    out = jax.ShapeDtypeStruct((units, blocks, strip, tile), jnp.bfloat16)
    pair = jax.ShapeDtypeStruct((2, *out.shape), out.dtype)
    outs = [out, out] + [pair] * (n_strips // 2 - 1) if paired else [out] * n_strips
    return pl.pallas_call(
        functools.partial(tiles_kernel, heights, len(arrived), n_strips, tile, paired),
        out_shape=outs,
        in_specs=[pl.BlockSpec(memory_space=pltpu.SMEM)] + [vmem] * (4 + len(arrived)),
        out_specs=[vmem] * len(outs),
        scratch_shapes=[
            pltpu.VMEM((slots, 2, 2 * max(heights), bands), jnp.bfloat16),
            pltpu.VMEM((slots, rows, 2 * max(heights)), jnp.float32),
        ],
        name="tiles",
        compiler_params=pltpu.CompilerParams(vmem_limit_bytes=VMEM_LIMIT),
        cost_estimate=SOON,
    )(place, in_vmem(own), in_vmem(sib), *weights, *arrived)


def strip_sum(ins, chips, n_chunks, other_core, chunk, unit, i):
    total = None
    for step in range(chips):
        ref = ins[(step * 2 + other_core) * n_chunks + chunk]
        value = ref[unit, i].astype(jnp.float32)
        total = value if total is None else total + value
    return total


def list_kernel(per_core, where_ref, later):
    blocks, slots = where_ref.shape

    def step(entry, count):
        where = where_ref[lax.div(entry, slots), lax.rem(entry, slots)]
        later[count + 1] = entry
        return count + (lax.rem(where, per_core) == per_core - 1).astype(jnp.int32)

    later[0] = lax.fori_loop(0, blocks * slots, step, 0)


def list_open(where, per_core):
    smem = pl.BlockSpec(memory_space=pltpu.SMEM)
    return pl.pallas_call(
        functools.partial(list_kernel, per_core),
        out_shape=jax.ShapeDtypeStruct((where.size + 1,), jnp.int32),
        in_specs=[smem],
        out_specs=smem,
        name="list_open",
        compiler_params=pltpu.CompilerParams(vmem_limit_bytes=VMEM_LIMIT),
        cost_estimate=SOON,
    )(where)


def place_early_kernel(chips, sizes, per_core, where_ref, *refs):
    n_chunks = len(sizes)
    ins = refs[: 2 * chips * n_chunks]
    density, energy, pool, tiles_out, sems = refs[2 * chips * n_chunks :]
    blocks, slots = density.shape[:2]

    def copies(i):
        return [
            pltpu.make_async_copy(tiles_out.at[i, kind], out.at[i], sems.at[i, kind])
            for kind, out in enumerate((density, energy))
        ]

    @pl.loop(0, blocks)
    def _(i):
        for other_core in range(2):
            first = other_core * per_core
            for chunk in range(n_chunks):
                for unit in range(2 * sizes[chunk]):
                    pool[first + unit // 2, unit % 2] = strip_sum(
                        ins, chips, n_chunks, other_core, chunk, unit, i
                    )
                first += sizes[chunk]
        for slot in range(slots):
            where = where_ref[i, slot]
            for kind in range(2):
                tiles_out[i, kind, slot] = pool[where, kind]
        for copy in copies(i):
            copy.start()

    for i in range(blocks):
        for copy in copies(i):
            copy.wait()


def place_early(where, strips, sizes, chips, per_core):
    _, blocks, strip, tile = strips[0][0].shape
    slots = where.shape[1]
    out = jax.ShapeDtypeStruct((blocks, slots, strip, tile), jnp.float32)
    flat = [value for group in strips for value in group]
    smem = pl.BlockSpec(memory_space=pltpu.SMEM)
    return pl.pallas_call(
        functools.partial(place_early_kernel, chips, sizes, per_core),
        out_shape=[out, out],
        in_specs=[smem] + [pl.BlockSpec(memory_space=pltpu.VMEM)] * len(flat),
        out_specs=[pl.BlockSpec(memory_space=pl.ANY)] * 2,
        scratch_shapes=[
            pltpu.VMEM((2 * per_core, 2, strip, tile), jnp.float32),
            pltpu.VMEM((blocks, 2, slots, strip, tile), jnp.float32),
            pltpu.SemaphoreType.DMA((blocks, 2)),
        ],
        name="place_early",
        compiler_params=pltpu.CompilerParams(vmem_limit_bytes=VMEM_LIMIT),
        cost_estimate=SOON,
    )(where, *flat)


def place_late_kernel(chips, per_core, where_ref, later, *refs):
    lower, upper = refs[: 2 * chips], refs[2 * chips : 4 * chips]
    density, energy, pool, sems = refs[4 * chips + 2 :]
    blocks, slots = density.shape[:2]
    cut = density.shape[3] // 2
    unit = lower[0].shape[0] - 1
    for other_core in range(2):
        for i in range(blocks):
            low = strip_sum(lower, chips, 1, other_core, 0, unit, i)
            high = strip_sum(upper, chips, 1, other_core, 0, 0, i)
            pool[other_core, i, 0] = jnp.concatenate([low[:, :cut], high[:, :cut]], 1)
            pool[other_core, i, 1] = jnp.concatenate([low[:, cut:], high[:, cut:]], 1)
    count = later[0]

    def copies(n):
        entry = jnp.clip(later[n + 1], 0, blocks * slots - 1)
        i, slot = lax.div(entry, slots), lax.rem(entry, slots)
        other_core = jnp.clip(lax.div(where_ref[i, slot], per_core), 0, 1)
        return [
            pltpu.make_async_copy(
                pool.at[other_core, i, kind], out.at[i, slot], sems.at[kind]
            )
            for kind, out in enumerate((density, energy))
        ]

    @pl.loop(0, count)
    def _(n):
        for copy in copies(n):
            copy.start()

    @pl.loop(0, count)
    def _(n):
        for copy in copies(n):
            copy.wait()


def place_late(where, later, lower, upper, density, energy, chips, per_core):
    blocks, _, strip, tile = density.shape
    smem = pl.BlockSpec(memory_space=pltpu.SMEM)
    anywhere = pl.BlockSpec(memory_space=pl.ANY)
    out = jax.ShapeDtypeStruct(density.shape, density.dtype)
    strips = [*lower, *upper]
    return pl.pallas_call(
        functools.partial(place_late_kernel, chips, per_core),
        out_shape=[out, out],
        in_specs=[smem, smem]
        + [pl.BlockSpec(memory_space=pltpu.VMEM)] * len(strips)
        + [anywhere] * 2,
        out_specs=[anywhere] * 2,
        scratch_shapes=[
            pltpu.VMEM((2, blocks, 2, strip, tile), jnp.float32),
            pltpu.SemaphoreType.DMA((2,)),
        ],
        input_output_aliases={2 + len(strips): 0, 3 + len(strips): 1},
        name="place_late",
        compiler_params=pltpu.CompilerParams(vmem_limit_bytes=VMEM_LIMIT),
        cost_estimate=SOON,
    )(where, later, *strips, density, energy)


def body(eigvecs, occupations, energies, neighbours):
    n_atoms = lax.axis_size("atoms")
    n_bands = lax.axis_size("bands")
    chips = n_bands // 2
    own_index = lax.axis_index("atoms").astype(jnp.int32)
    group = lax.axis_index("bands").astype(jnp.int32)
    core = group & 1
    blocks = neighbours.shape[0]
    tile = eigvecs.shape[0] // blocks
    half_blocks = blocks // 2
    offsets = [-1, 1, 2, -2]

    asks = [shifted(neighbours, "atoms", offset) for offset in offsets]
    sib = to_strip_target(eigvecs, chips, 0, 1)
    own_weights = jnp.stack([occupations, occupations * energies], 0)

    targets = [
        strip_target(group, chips, step, other)
        for step in range(chips)
        for other in range(2)
    ]
    here = jnp.stack([own_index, core]).astype(jnp.int32)
    place = jnp.stack([core] + targets).astype(jnp.int32)

    asks, own_weights = lax.optimization_barrier((asks, own_weights))
    weights = (own_weights, to_strip_target(own_weights, chips, 0, 1))
    picked = list(pick(here, asks[:3], eigvecs, sib, tile, 1))
    arrived = [
        shifted(value, "atoms", -offset) for value, offset in zip(picked, offsets)
    ]
    kept_eigvecs, picked[2] = lax.optimization_barrier((eigvecs, picked[2]))
    own, kept_sib = keep(kept_eigvecs, sib)

    def strips_of(arrived, paired):
        parts = list(tiles(place, own, kept_sib, arrived, weights, n_bands, tile, paired))
        for index in range(1, len(parts)):
            step, other = (max(index - 1, 0), index == 1) if paired else (index // 2, index % 2)
            parts[index] = to_strip_target(parts[index], chips, step, int(other))
        return parts

    def passed_on(parts):
        singles = parts[:2]
        for pair in parts[2:]:
            singles += [pair[0], to_strip_target(pair[1], chips, 0, 1)]
        return singles

    chunks = [strips_of((), True)]
    neighbours, here, chunks[0][0] = lax.optimization_barrier(
        (neighbours, here, chunks[0][0])
    )
    halves = list(pick(here, asks[3:], eigvecs, sib, tile, 2))

    owners = lax.div(neighbours, blocks)
    within = lax.rem(neighbours, blocks)
    distance = lax.rem(owners - own_index + n_atoms, n_atoms)
    spot = lax.rem(within, half_blocks)
    side = lax.div(within, half_blocks)
    for index, offset in enumerate(offsets):
        from_it = distance == offset % n_atoms
        highest = jnp.max(jnp.where(from_it, within, -1))
        side = jnp.where(from_it, (within == highest).astype(jnp.int32), side)
        spot = jnp.where(from_it, half_blocks + index, spot)
    per_core = half_blocks + len(offsets)
    where = ((side ^ core) * per_core + spot).astype(jnp.int32)

    *near, third = arrived
    third, halves, chunks[0][:1] = lax.optimization_barrier((third, halves, chunks[0][:1]))
    lower = shifted(halves[0], "atoms", -offsets[3])
    parts = list(tiles(place, own, kept_sib, [third], weights, n_bands, tile, True))
    pairs = [
        to_strip_target(pair, chips, step + 1, 0) for step, pair in enumerate(parts[2:])
    ]
    later = list_open(where, per_core)
    near, where, later, parts[:2], pairs, chunks, halves = lax.optimization_barrier(
        (near, where, later, parts[:2], pairs, chunks, halves)
    )
    upper = shifted(halves[1], "atoms", -offsets[3])
    chunks.append([parts[0], to_strip_target(parts[1], chips, 0, 1)] + pairs)
    chunks = [passed_on(chunk) for chunk in chunks]
    direct = strips_of(near, False)
    lower, direct[:2], chunks = lax.optimization_barrier((lower, direct[:2], chunks))
    lower = list(tiles(place, own, kept_sib, [lower], weights, n_bands, tile, False))
    lower_sib = lower[1]
    for index in range(2, n_bands):
        lower[index] = to_strip_target(lower[index], chips, index // 2, index % 2)
    where, upper, lower[0], direct[:3] = lax.optimization_barrier(
        (where, upper, lower[0], direct[:3])
    )
    chunks.append(direct)
    last = strips_of([upper], False)
    where, last[0] = lax.optimization_barrier((where, last[0]))
    lower[1] = to_strip_target(lower_sib, chips, 0, 1)
    where, lower = lax.optimization_barrier((where, lower))
    local, far, direct = chunks
    strips = list(zip(local, direct, far))
    sizes = [half_blocks, 2, 1]
    density, energy = place_early(where, strips, sizes, chips, per_core)
    return place_late(where, later, lower, last, density, energy, chips, per_core)


def solution(mesh):
    return jax.shard_map(
        body,
        mesh=mesh,
        in_specs=(P("atoms", "bands"), P("bands"), P("bands"), P("atoms", None)),
        out_specs=(P("atoms", None, "bands", None), P("atoms", None, "bands", None)),
        check_vma=False,
    )
```

```python
import functools

import jax
import jax.numpy as jnp
from jax import lax
from jax.experimental import pallas as pl
from jax.experimental.pallas import tpu as pltpu
from jax.sharding import PartitionSpec as P

R = 2
VMEM_LIMIT = 24 * 1024 * 1024
SOON = pl.CostEstimate(flops=0, bytes_accessed=0, transcendentals=0)


def in_hbm(value):
    return pltpu.with_memory_space_constraint(value, pltpu.HBM)


def in_vmem(value):
    return pltpu.with_memory_space_constraint(value, pltpu.VMEM)


def shifted(value, axis, steps):
    count = lax.axis_size(axis)
    pairs = [(source, (source + steps) % count) for source in range(count)]
    return lax.ppermute(value, axis, pairs)


def strip_target(group, chips, step, other_core):
    chip = lax.rem(lax.shift_right_logical(group, 1) + step, chips)
    return chip * 2 + ((group & 1) ^ other_core)


def to_strip_target(value, chips, step, other_core):
    pairs = [
        (group, (group // 2 + step) % chips * 2 + (group % 2 ^ other_core))
        for group in range(2 * chips)
    ]
    return lax.ppermute(value, "bands", pairs)


def pick_kernel(count, blocks, tile, parts, place_ref, *refs):
    asks, (own, sib), outs = refs[:count], refs[count : count + 2], refs[count + 2 : -1]
    sems = refs[-1]
    first = place_ref[0] * blocks
    copies = []
    for index in range(count):
        ids = asks[index][...] - first
        mine = (ids >= 0) & (ids < blocks)
        lowest = jnp.min(jnp.where(mine, ids, blocks - 1))
        highest = jnp.max(jnp.where(mine, ids, 0))
        block = jnp.where(place_ref[1] == 0, lowest, highest)
        for part in range(parts):
            height = tile // parts
            start = pl.multiple_of(block * tile + part * height, height)
            out = outs[index * parts + part]
            for half, source in enumerate((own, sib)):
                copy = pltpu.make_async_copy(
                    source.at[pl.ds(start, height), :],
                    out.at[half],
                    sems.at[index * parts + part, half],
                )
                copy.start()
                copies.append(copy)
    for copy in copies:
        copy.wait()


def pick(place, asks, own, sib, tile, parts):
    blocks, bands = asks[0].shape[0], own.shape[1]
    count = len(asks)
    n_outs = count * parts
    return pl.pallas_call(
        functools.partial(pick_kernel, count, blocks, tile, parts),
        out_shape=[pltpu.VMEM((2, tile // parts, bands), own.dtype)] * n_outs,
        in_specs=[pl.BlockSpec(memory_space=pltpu.SMEM)]
        + [pl.BlockSpec(memory_space=pltpu.VMEM)] * count
        + [pl.BlockSpec(memory_space=pl.ANY)] * 2,
        out_specs=[pl.BlockSpec(memory_space=pltpu.VMEM)] * n_outs,
        scratch_shapes=[pltpu.SemaphoreType.DMA((n_outs, 2))],
        name="pick_blocks",
        compiler_params=pltpu.CompilerParams(vmem_limit_bytes=VMEM_LIMIT),
        cost_estimate=SOON,
    )(place, *asks, in_hbm(own), in_hbm(sib))


def keep_kernel(own, sib, own_out, sib_out, sems):
    copies = []
    for half, (source, out) in enumerate(((own, own_out), (sib, sib_out))):
        copies.append(pltpu.make_async_copy(source, out, sems.at[half]))
    for copy in copies:
        copy.start()
    for copy in copies:
        copy.wait()


def keep(own, sib):
    return pl.pallas_call(
        keep_kernel,
        out_shape=[pltpu.VMEM(own.shape, own.dtype)] * 2,
        in_specs=[pl.BlockSpec(memory_space=pl.ANY)] * 2,
        out_specs=[pl.BlockSpec(memory_space=pltpu.VMEM)] * 2,
        scratch_shapes=[pltpu.SemaphoreType.DMA((2,))],
        name="keep",
        compiler_params=pltpu.CompilerParams(vmem_limit_bytes=VMEM_LIMIT),
        cost_estimate=SOON,
    )(in_hbm(own), in_hbm(sib))


def tiles_kernel(heights, n_arrived, n_strips, tile, paired, place_ref, *refs):
    lefts, weights = refs[:2], refs[2:4]
    arrived, refs = refs[4 : 4 + n_arrived], refs[4 + n_arrived :]
    outs, (scaled, total) = refs[:-2], refs[-2:]
    if paired:
        outs = outs[:2] + tuple(out.at[index] for out in outs[2:] for index in range(2))
    strip = tile // n_strips
    n_left = lefts[0].shape[0] // tile
    unit = 0
    for j, height in enumerate(heights):
        slot = j % 2
        for half in range(2):
            if n_arrived:
                block = arrived[j][half]
            else:
                first = pl.multiple_of((place_ref[0] * len(heights) + j) * tile, tile)
                block = lefts[half][pl.ds(first, tile), :]
            block = block.astype(jnp.float32)
            for kind in range(2):
                value = block * weights[half][kind : kind + 1, :]
                rows = pl.ds(kind * height, height)
                scaled[slot, half, rows, :] = value.astype(scaled.dtype)
        width = 2 * height
        for half in range(2):
            value = lax.dot_general(
                lefts[half][...],
                scaled[slot, half, :width, :],
                (((1,), (1,)), ((), ())),
                preferred_element_type=jnp.float32,
            )
            if half == 0:
                total[slot, :, :width] = value
            else:
                total[slot, :, :width] += value
        for lane in range(0, width, tile):
            for index in range(n_strips):
                start = place_ref[1 + index] * strip
                for i in range(n_left):
                    rows = pl.ds(pl.multiple_of(i * tile + start, strip), strip)
                    value = total[slot, rows, lane : lane + tile]
                    outs[index][unit, i] = value.astype(outs[index].dtype)
            unit += 1


def tiles(place, own, sib, arrived, weights, n_strips, tile, paired):
    rows, bands = own.shape
    blocks = rows // tile
    heights = [value.shape[1] for value in arrived] or [tile] * (blocks // 2)
    strip = tile // n_strips
    slots = min(len(heights), 2)
    vmem = pl.BlockSpec(memory_space=pltpu.VMEM)
    units = sum(2 * height // tile for height in heights)
    out = jax.ShapeDtypeStruct((units, blocks, strip, tile), jnp.bfloat16)
    pair = jax.ShapeDtypeStruct((2, *out.shape), out.dtype)
    outs = [out, out] + [pair] * (n_strips // 2 - 1) if paired else [out] * n_strips
    return pl.pallas_call(
        functools.partial(tiles_kernel, heights, len(arrived), n_strips, tile, paired),
        out_shape=outs,
        in_specs=[pl.BlockSpec(memory_space=pltpu.SMEM)] + [vmem] * (4 + len(arrived)),
        out_specs=[vmem] * len(outs),
        scratch_shapes=[
            pltpu.VMEM((slots, 2, 2 * max(heights), bands), jnp.bfloat16),
            pltpu.VMEM((slots, rows, 2 * max(heights)), jnp.float32),
        ],
        name="tiles",
        compiler_params=pltpu.CompilerParams(vmem_limit_bytes=VMEM_LIMIT),
        cost_estimate=SOON,
    )(place, in_vmem(own), in_vmem(sib), *weights, *arrived)


def strip_sum(ins, chips, n_chunks, other_core, chunk, unit, i):
    total = None
    for step in range(chips):
        ref = ins[(step * 2 + other_core) * n_chunks + chunk]
        value = ref[unit, i].astype(jnp.float32)
        total = value if total is None else total + value
    return total


def list_kernel(per_core, where_ref, later):
    blocks, slots = where_ref.shape

    def block(i, count):
        for slot in range(slots):
            where = where_ref[i, slot]
            other_core = (where >= per_core).astype(jnp.int32)
            later[2 * count + 1] = i * slots + slot
            later[2 * count + 2] = other_core * blocks + i
            count += (where - other_core * per_core == per_core - 1).astype(jnp.int32)
        return count

    later[0] = lax.fori_loop(0, blocks, block, 0)


def list_open(where, per_core):
    smem = pl.BlockSpec(memory_space=pltpu.SMEM)
    return pl.pallas_call(
        functools.partial(list_kernel, per_core),
        out_shape=jax.ShapeDtypeStruct((2 * where.size + 1,), jnp.int32),
        in_specs=[smem],
        out_specs=smem,
        name="list_open",
        compiler_params=pltpu.CompilerParams(vmem_limit_bytes=VMEM_LIMIT),
        cost_estimate=SOON,
    )(where)


def place_early_kernel(chips, sizes, per_core, where_ref, *refs):
    n_chunks = len(sizes)
    ins = refs[: 2 * chips * n_chunks]
    density, energy, pool, tiles_out, sems = refs[2 * chips * n_chunks :]
    blocks, slots = where_ref.shape

    def copies(i):
        return [
            pltpu.make_async_copy(
                tiles_out.at[i, kind], out.at[pl.ds(i * slots, slots)], sems.at[i, kind]
            )
            for kind, out in enumerate((density, energy))
        ]

    @pl.loop(0, blocks)
    def _(i):
        for other_core in range(2):
            first = other_core * per_core
            for chunk in range(n_chunks):
                for unit in range(2 * sizes[chunk]):
                    pool[first + unit // 2, unit % 2] = strip_sum(
                        ins, chips, n_chunks, other_core, chunk, unit, i
                    )
                first += sizes[chunk]
        for slot in range(slots):
            where = where_ref[i, slot]
            for kind in range(2):
                tiles_out[i, kind, slot] = pool[where, kind]
        for copy in copies(i):
            copy.start()

    for i in range(blocks):
        for copy in copies(i):
            copy.wait()


def place_early(where, strips, sizes, chips, per_core):
    _, blocks, strip, tile = strips[0][0].shape
    slots = where.shape[1]
    out = jax.ShapeDtypeStruct((blocks * slots, strip, tile), jnp.float32)
    flat = [value for group in strips for value in group]
    smem = pl.BlockSpec(memory_space=pltpu.SMEM)
    return pl.pallas_call(
        functools.partial(place_early_kernel, chips, sizes, per_core),
        out_shape=[out, out],
        in_specs=[smem] + [pl.BlockSpec(memory_space=pltpu.VMEM)] * len(flat),
        out_specs=[pl.BlockSpec(memory_space=pl.ANY)] * 2,
        scratch_shapes=[
            pltpu.VMEM((2 * per_core, 2, strip, tile), jnp.float32),
            pltpu.VMEM((blocks, 2, slots, strip, tile), jnp.float32),
            pltpu.SemaphoreType.DMA((blocks, 2)),
        ],
        name="place_early",
        compiler_params=pltpu.CompilerParams(vmem_limit_bytes=VMEM_LIMIT),
        cost_estimate=SOON,
    )(where, *flat)


def place_late_kernel(chips, later, *refs):
    lower, upper = refs[: 2 * chips], refs[2 * chips : 4 * chips]
    density, energy, pool, sems = refs[4 * chips + 2 :]
    blocks = pool.shape[0] // 2
    cut = density.shape[2] // 2
    for other_core in range(2):
        for i in range(blocks):
            low = strip_sum(lower, chips, 1, other_core, 0, 0, i)
            high = strip_sum(upper, chips, 1, other_core, 0, 0, i)
            spot = other_core * blocks + i
            pool[spot, 0] = jnp.concatenate([low[:, :cut], high[:, :cut]], 1)
            pool[spot, 1] = jnp.concatenate([low[:, cut:], high[:, cut:]], 1)
    count = later[0]

    def copies(source, target):
        return [
            pltpu.make_async_copy(pool.at[source, kind], out.at[target], sems.at[kind])
            for kind, out in enumerate((density, energy))
        ]

    @pl.loop(0, count)
    def _(n):
        for copy in copies(later[2 * n + 2], later[2 * n + 1]):
            copy.start()

    @pl.loop(0, count)
    def _(n):
        for copy in copies(0, 0):
            copy.wait()


def place_late(later, lower, upper, density, energy, chips):
    _, blocks, strip, tile = upper[0].shape
    smem = pl.BlockSpec(memory_space=pltpu.SMEM)
    anywhere = pl.BlockSpec(memory_space=pl.ANY)
    out = jax.ShapeDtypeStruct(density.shape, density.dtype)
    strips = [*lower, *upper]
    return pl.pallas_call(
        functools.partial(place_late_kernel, chips),
        out_shape=[out, out],
        in_specs=[smem]
        + [pl.BlockSpec(memory_space=pltpu.VMEM)] * len(strips)
        + [anywhere] * 2,
        out_specs=[anywhere] * 2,
        scratch_shapes=[
            pltpu.VMEM((2 * blocks, 2, strip, tile), jnp.float32),
            pltpu.SemaphoreType.DMA((2,)),
        ],
        input_output_aliases={1 + len(strips): 0, 2 + len(strips): 1},
        name="place_late",
        compiler_params=pltpu.CompilerParams(vmem_limit_bytes=VMEM_LIMIT),
        cost_estimate=SOON,
    )(later, *strips, density, energy)


def body(eigvecs, occupations, energies, neighbours):
    n_atoms = lax.axis_size("atoms")
    n_bands = lax.axis_size("bands")
    chips = n_bands // 2
    own_index = lax.axis_index("atoms").astype(jnp.int32)
    group = lax.axis_index("bands").astype(jnp.int32)
    core = group & 1
    blocks = neighbours.shape[0]
    tile = eigvecs.shape[0] // blocks
    half_blocks = blocks // 2
    offsets = [-1, 1, 2, -2]

    asks = [shifted(neighbours, "atoms", offset) for offset in offsets]
    sib = to_strip_target(eigvecs, chips, 0, 1)
    own_weights = jnp.stack([occupations, occupations * energies], 0)

    targets = [
        strip_target(group, chips, step, other)
        for step in range(chips)
        for other in range(2)
    ]
    here = jnp.stack([own_index, core]).astype(jnp.int32)
    place = jnp.stack([core] + targets).astype(jnp.int32)

    asks, own_weights = lax.optimization_barrier((asks, own_weights))
    weights = (own_weights, to_strip_target(own_weights, chips, 0, 1))
    picked = list(pick(here, asks[2:3], eigvecs, sib, tile, 1))
    here, picked[0] = lax.optimization_barrier((here, picked[0]))
    picked = list(pick(here, asks[:2], eigvecs, sib, tile, 1)) + picked
    arrived = [
        shifted(value, "atoms", -offset) for value, offset in zip(picked, offsets)
    ]
    kept_eigvecs, picked[0] = lax.optimization_barrier((eigvecs, picked[0]))
    own, kept_sib = keep(kept_eigvecs, sib)

    def strips_of(arrived, paired):
        parts = list(tiles(place, own, kept_sib, arrived, weights, n_bands, tile, paired))
        for index in range(1, len(parts)):
            step, other = (max(index - 1, 0), index == 1) if paired else (index // 2, index % 2)
            parts[index] = to_strip_target(parts[index], chips, step, int(other))
        return parts

    def passed_on(parts):
        singles = parts[:2]
        for pair in parts[2:]:
            singles += [pair[0], to_strip_target(pair[1], chips, 0, 1)]
        return singles

    chunks = [strips_of((), True)]
    neighbours, here, chunks[0][0] = lax.optimization_barrier(
        (neighbours, here, chunks[0][0])
    )
    halves = list(pick(here, asks[3:], eigvecs, sib, tile, 2))

    owners = lax.div(neighbours, blocks)
    within = lax.rem(neighbours, blocks)
    distance = lax.rem(owners - own_index + n_atoms, n_atoms)
    spot = lax.rem(within, half_blocks)
    side = lax.div(within, half_blocks)
    for index, offset in enumerate(offsets):
        from_it = distance == offset % n_atoms
        highest = jnp.max(jnp.where(from_it, within, -1))
        side = jnp.where(from_it, (within == highest).astype(jnp.int32), side)
        spot = jnp.where(from_it, half_blocks + index, spot)
    per_core = half_blocks + len(offsets)
    where = ((side ^ core) * per_core + spot).astype(jnp.int32)

    *near, third = arrived
    third, halves, chunks[0][:1] = lax.optimization_barrier((third, halves, chunks[0][:1]))
    lower = shifted(halves[0], "atoms", -offsets[3])
    parts = list(tiles(place, own, kept_sib, [third], weights, n_bands, tile, True))
    pairs = [
        to_strip_target(pair, chips, step + 1, 0) for step, pair in enumerate(parts[2:])
    ]
    later = list_open(where, per_core)
    near, where, later, parts[:2], pairs, chunks, halves = lax.optimization_barrier(
        (near, where, later, parts[:2], pairs, chunks, halves)
    )
    upper = shifted(halves[1], "atoms", -offsets[3])
    chunks.append([parts[0], to_strip_target(parts[1], chips, 0, 1)] + pairs)
    chunks = [passed_on(chunk) for chunk in chunks]
    direct = strips_of(near, False)
    lower, direct[:2], chunks = lax.optimization_barrier((lower, direct[:2], chunks))
    lower = list(tiles(place, own, kept_sib, [lower], weights, n_bands, tile, False))
    lower_sib = lower[1]
    for index in range(2, n_bands):
        lower[index] = to_strip_target(lower[index], chips, index // 2, index % 2)
    where, upper, lower[0], direct[:3] = lax.optimization_barrier(
        (where, upper, lower[0], direct[:3])
    )
    chunks.append(direct)
    last = strips_of([upper], False)
    where, last[0] = lax.optimization_barrier((where, last[0]))
    lower[1] = to_strip_target(lower_sib, chips, 0, 1)
    where, lower = lax.optimization_barrier((where, lower))
    local, far, direct = chunks
    strips = list(zip(local, direct, far))
    sizes = [half_blocks, 2, 1]
    density, energy = place_early(where, strips, sizes, chips, per_core)
    outs = place_late(later, lower, last, density, energy, chips)
    return tuple(out.reshape(*where.shape, *out.shape[1:]) for out in outs)


def solution(mesh):
    return jax.shard_map(
        body,
        mesh=mesh,
        in_specs=(P("atoms", "bands"), P("bands"), P("bands"), P("atoms", None)),
        out_specs=(P("atoms", None, "bands", None), P("atoms", None, "bands", None)),
        check_vma=False,
    )
```

```python
import functools

import jax
import jax.numpy as jnp
from jax import lax
from jax.experimental import pallas as pl
from jax.experimental.pallas import tpu as pltpu
from jax.sharding import PartitionSpec as P

R = 2
VMEM_LIMIT = 24 * 1024 * 1024
SOON = pl.CostEstimate(flops=0, bytes_accessed=0, transcendentals=0)


def in_hbm(value):
    return pltpu.with_memory_space_constraint(value, pltpu.HBM)


def in_vmem(value):
    return pltpu.with_memory_space_constraint(value, pltpu.VMEM)


def shifted(value, axis, steps):
    count = lax.axis_size(axis)
    pairs = [(source, (source + steps) % count) for source in range(count)]
    return lax.ppermute(value, axis, pairs)


def strip_target(group, chips, step, other_core):
    chip = lax.rem(lax.shift_right_logical(group, 1) + step, chips)
    return chip * 2 + ((group & 1) ^ other_core)


def to_strip_target(value, chips, step, other_core):
    pairs = [
        (group, (group // 2 + step) % chips * 2 + (group % 2 ^ other_core))
        for group in range(2 * chips)
    ]
    return lax.ppermute(value, "bands", pairs)


def pick_kernel(count, blocks, tile, parts, place_ref, *refs):
    asks, (own, sib), outs = refs[:count], refs[count : count + 2], refs[count + 2 : -1]
    sems = refs[-1]
    first = place_ref[0] * blocks
    copies = []
    for index in range(count):
        ids = asks[index][...] - first
        mine = (ids >= 0) & (ids < blocks)
        lowest = jnp.min(jnp.where(mine, ids, blocks - 1))
        highest = jnp.max(jnp.where(mine, ids, 0))
        block = jnp.where(place_ref[1] == 0, lowest, highest)
        for part in range(parts):
            height = tile // parts
            start = pl.multiple_of(block * tile + part * height, height)
            out = outs[index * parts + part]
            for half, source in enumerate((own, sib)):
                copy = pltpu.make_async_copy(
                    source.at[pl.ds(start, height), :],
                    out.at[half],
                    sems.at[index * parts + part, half],
                )
                copy.start()
                copies.append(copy)
    for copy in copies:
        copy.wait()


def pick(place, asks, own, sib, tile, parts):
    blocks, bands = asks[0].shape[0], own.shape[1]
    count = len(asks)
    n_outs = count * parts
    return pl.pallas_call(
        functools.partial(pick_kernel, count, blocks, tile, parts),
        out_shape=[pltpu.VMEM((2, tile // parts, bands), own.dtype)] * n_outs,
        in_specs=[pl.BlockSpec(memory_space=pltpu.SMEM)]
        + [pl.BlockSpec(memory_space=pltpu.VMEM)] * count
        + [pl.BlockSpec(memory_space=pl.ANY)] * 2,
        out_specs=[pl.BlockSpec(memory_space=pltpu.VMEM)] * n_outs,
        scratch_shapes=[pltpu.SemaphoreType.DMA((n_outs, 2))],
        name="pick_blocks",
        compiler_params=pltpu.CompilerParams(vmem_limit_bytes=VMEM_LIMIT),
        cost_estimate=SOON,
    )(place, *asks, in_hbm(own), in_hbm(sib))


def keep_kernel(own, sib, own_out, sib_out, sems):
    copies = []
    for half, (source, out) in enumerate(((own, own_out), (sib, sib_out))):
        copies.append(pltpu.make_async_copy(source, out, sems.at[half]))
    for copy in copies:
        copy.start()
    for copy in copies:
        copy.wait()


def keep(own, sib):
    return pl.pallas_call(
        keep_kernel,
        out_shape=[pltpu.VMEM(own.shape, own.dtype)] * 2,
        in_specs=[pl.BlockSpec(memory_space=pl.ANY)] * 2,
        out_specs=[pl.BlockSpec(memory_space=pltpu.VMEM)] * 2,
        scratch_shapes=[pltpu.SemaphoreType.DMA((2,))],
        name="keep",
        compiler_params=pltpu.CompilerParams(vmem_limit_bytes=VMEM_LIMIT),
        cost_estimate=SOON,
    )(in_hbm(own), in_hbm(sib))


def tiles_kernel(heights, n_arrived, n_strips, tile, paired, place_ref, *refs):
    lefts, weights = refs[:2], refs[2:4]
    arrived, refs = refs[4 : 4 + n_arrived], refs[4 + n_arrived :]
    outs, (scaled, total) = refs[:-2], refs[-2:]
    if paired:
        outs = outs[:2] + tuple(out.at[index] for out in outs[2:] for index in range(2))
    strip = tile // n_strips
    n_left = lefts[0].shape[0] // tile
    unit = 0
    for j, height in enumerate(heights):
        slot = j % 2
        for half in range(2):
            if n_arrived:
                block = arrived[j][half]
            else:
                first = pl.multiple_of((place_ref[0] * len(heights) + j) * tile, tile)
                block = lefts[half][pl.ds(first, tile), :]
            block = block.astype(jnp.float32)
            for kind in range(2):
                value = block * weights[half][kind : kind + 1, :]
                rows = pl.ds(kind * height, height)
                scaled[slot, half, rows, :] = value.astype(scaled.dtype)
        width = 2 * height
        for half in range(2):
            value = lax.dot_general(
                lefts[half][...],
                scaled[slot, half, :width, :],
                (((1,), (1,)), ((), ())),
                preferred_element_type=jnp.float32,
            )
            if half == 0:
                total[slot, :, :width] = value
            else:
                total[slot, :, :width] += value
        for lane in range(0, width, tile):
            for index in range(n_strips):
                start = place_ref[1 + index] * strip
                for i in range(n_left):
                    rows = pl.ds(pl.multiple_of(i * tile + start, strip), strip)
                    value = total[slot, rows, lane : lane + tile]
                    outs[index][unit, i] = value.astype(outs[index].dtype)
            unit += 1


def tiles(place, own, sib, arrived, weights, n_strips, tile, paired):
    rows, bands = own.shape
    blocks = rows // tile
    heights = [value.shape[1] for value in arrived] or [tile] * (blocks // 2)
    strip = tile // n_strips
    slots = min(len(heights), 2)
    vmem = pl.BlockSpec(memory_space=pltpu.VMEM)
    units = sum(2 * height // tile for height in heights)
    out = jax.ShapeDtypeStruct((units, blocks, strip, tile), jnp.bfloat16)
    pair = jax.ShapeDtypeStruct((2, *out.shape), out.dtype)
    outs = [out, out] + [pair] * (n_strips // 2 - 1) if paired else [out] * n_strips
    return pl.pallas_call(
        functools.partial(tiles_kernel, heights, len(arrived), n_strips, tile, paired),
        out_shape=outs,
        in_specs=[pl.BlockSpec(memory_space=pltpu.SMEM)] + [vmem] * (4 + len(arrived)),
        out_specs=[vmem] * len(outs),
        scratch_shapes=[
            pltpu.VMEM((slots, 2, 2 * max(heights), bands), jnp.bfloat16),
            pltpu.VMEM((slots, rows, 2 * max(heights)), jnp.float32),
        ],
        name="tiles",
        compiler_params=pltpu.CompilerParams(vmem_limit_bytes=VMEM_LIMIT),
        cost_estimate=SOON,
    )(place, in_vmem(own), in_vmem(sib), *weights, *arrived)


def strip_sum(ins, chips, n_chunks, other_core, chunk, unit, i):
    total = None
    for step in range(chips):
        ref = ins[(step * 2 + other_core) * n_chunks + chunk]
        value = ref[unit, i].astype(jnp.float32)
        total = value if total is None else total + value
    return total


def list_kernel(per_core, where_ref, later):
    blocks, slots = where_ref.shape

    def block(i, count):
        for slot in range(slots):
            where = where_ref[i, slot]
            other_core = (where >= per_core).astype(jnp.int32)
            later[2 * count + 1] = i * slots + slot
            later[2 * count + 2] = other_core * blocks + i
            count += (where - other_core * per_core == per_core - 1).astype(jnp.int32)
        return count

    later[0] = lax.fori_loop(0, blocks, block, 0)


def list_open(where, per_core):
    smem = pl.BlockSpec(memory_space=pltpu.SMEM)
    return pl.pallas_call(
        functools.partial(list_kernel, per_core),
        out_shape=jax.ShapeDtypeStruct((2 * where.size + 1,), jnp.int32),
        in_specs=[smem],
        out_specs=smem,
        name="list_open",
        compiler_params=pltpu.CompilerParams(vmem_limit_bytes=VMEM_LIMIT),
        cost_estimate=SOON,
    )(where)


def place_early_kernel(chips, sizes, per_core, where_ref, *refs):
    n_chunks = len(sizes)
    ins = refs[: 2 * chips * n_chunks]
    density, energy, pool, tiles_out, sems = refs[2 * chips * n_chunks :]
    blocks, slots = where_ref.shape

    def copies(i):
        return [
            pltpu.make_async_copy(
                tiles_out.at[i, kind], out.at[pl.ds(i * slots, slots)], sems.at[i, kind]
            )
            for kind, out in enumerate((density, energy))
        ]

    @pl.loop(0, blocks)
    def _(i):
        for other_core in range(2):
            first = other_core * per_core
            for chunk in range(n_chunks):
                for unit in range(2 * sizes[chunk]):
                    pool[first + unit // 2, unit % 2] = strip_sum(
                        ins, chips, n_chunks, other_core, chunk, unit, i
                    )
                first += sizes[chunk]
        for slot in range(slots):
            where = where_ref[i, slot]
            for kind in range(2):
                tiles_out[i, kind, slot] = pool[where, kind]
        for copy in copies(i):
            copy.start()

    for i in range(blocks):
        for copy in copies(i):
            copy.wait()


def place_early(where, strips, sizes, chips, per_core):
    _, blocks, strip, tile = strips[0][0].shape
    slots = where.shape[1]
    out = jax.ShapeDtypeStruct((blocks * slots, strip, tile), jnp.float32)
    flat = [value for group in strips for value in group]
    smem = pl.BlockSpec(memory_space=pltpu.SMEM)
    return pl.pallas_call(
        functools.partial(place_early_kernel, chips, sizes, per_core),
        out_shape=[out, out],
        in_specs=[smem] + [pl.BlockSpec(memory_space=pltpu.VMEM)] * len(flat),
        out_specs=[pl.BlockSpec(memory_space=pl.ANY)] * 2,
        scratch_shapes=[
            pltpu.VMEM((2 * per_core, 2, strip, tile), jnp.float32),
            pltpu.VMEM((blocks, 2, slots, strip, tile), jnp.float32),
            pltpu.SemaphoreType.DMA((blocks, 2)),
        ],
        name="place_early",
        compiler_params=pltpu.CompilerParams(vmem_limit_bytes=VMEM_LIMIT),
        cost_estimate=SOON,
    )(where, *flat)


def place_late_kernel(chips, later, *refs):
    lower, upper = refs[: 2 * chips], refs[2 * chips : 4 * chips]
    density, energy, pool, sems = refs[4 * chips + 2 :]
    blocks = pool.shape[0] // 2
    cut = density.shape[2] // 2
    for other_core in range(2):
        for i in range(blocks):
            low = strip_sum(lower, chips, 1, other_core, 0, 0, i)
            high = strip_sum(upper, chips, 1, other_core, 0, 0, i)
            spot = other_core * blocks + i
            pool[spot, 0] = jnp.concatenate([low[:, :cut], high[:, :cut]], 1)
            pool[spot, 1] = jnp.concatenate([low[:, cut:], high[:, cut:]], 1)
    count = later[0]

    def copies(source, target):
        return [
            pltpu.make_async_copy(pool.at[source, kind], out.at[target], sems.at[kind])
            for kind, out in enumerate((density, energy))
        ]

    @pl.loop(0, count)
    def _(n):
        for copy in copies(later[2 * n + 2], later[2 * n + 1]):
            copy.start()

    @pl.loop(0, count)
    def _(n):
        for copy in copies(0, 0):
            copy.wait()


def place_late(later, lower, upper, density, energy, chips):
    _, blocks, strip, tile = upper[0].shape
    smem = pl.BlockSpec(memory_space=pltpu.SMEM)
    anywhere = pl.BlockSpec(memory_space=pl.ANY)
    out = jax.ShapeDtypeStruct(density.shape, density.dtype)
    strips = [*lower, *upper]
    return pl.pallas_call(
        functools.partial(place_late_kernel, chips),
        out_shape=[out, out],
        in_specs=[smem]
        + [pl.BlockSpec(memory_space=pltpu.VMEM)] * len(strips)
        + [anywhere] * 2,
        out_specs=[anywhere] * 2,
        scratch_shapes=[
            pltpu.VMEM((2 * blocks, 2, strip, tile), jnp.float32),
            pltpu.SemaphoreType.DMA((2,)),
        ],
        input_output_aliases={1 + len(strips): 0, 2 + len(strips): 1},
        name="place_late",
        compiler_params=pltpu.CompilerParams(vmem_limit_bytes=VMEM_LIMIT),
        cost_estimate=SOON,
    )(later, *strips, density, energy)


def body(eigvecs, occupations, energies, neighbours):
    n_atoms = lax.axis_size("atoms")
    n_bands = lax.axis_size("bands")
    chips = n_bands // 2
    own_index = lax.axis_index("atoms").astype(jnp.int32)
    group = lax.axis_index("bands").astype(jnp.int32)
    core = group & 1
    blocks = neighbours.shape[0]
    tile = eigvecs.shape[0] // blocks
    half_blocks = blocks // 2
    offsets = [-1, 1, 2, -2]

    asks = [shifted(neighbours, "atoms", offset) for offset in offsets]
    sib = to_strip_target(eigvecs, chips, 0, 1)
    own_weights = jnp.stack([occupations, occupations * energies], 0)

    targets = [
        strip_target(group, chips, step, other)
        for step in range(chips)
        for other in range(2)
    ]
    here = jnp.stack([own_index, core]).astype(jnp.int32)
    place = jnp.stack([core] + targets).astype(jnp.int32)

    asks, own_weights = lax.optimization_barrier((asks, own_weights))
    weights = (own_weights, to_strip_target(own_weights, chips, 0, 1))
    picked = list(pick(here, asks[2:3], eigvecs, sib, tile, 1))
    here, picked[0] = lax.optimization_barrier((here, picked[0]))
    picked = list(pick(here, asks[:2], eigvecs, sib, tile, 1)) + picked
    arrived = [
        shifted(value, "atoms", -offset) for value, offset in zip(picked, offsets)
    ]
    kept_eigvecs, picked[0] = lax.optimization_barrier((eigvecs, picked[0]))
    own, kept_sib = keep(kept_eigvecs, sib)

    def strips_of(arrived, paired):
        parts = list(tiles(place, own, kept_sib, arrived, weights, n_bands, tile, paired))
        for index in range(1, len(parts)):
            step, other = (max(index - 1, 0), index == 1) if paired else (index // 2, index % 2)
            parts[index] = to_strip_target(parts[index], chips, step, int(other))
        return parts

    def passed_on(parts):
        singles = parts[:2]
        for pair in parts[2:]:
            singles += [pair[0], to_strip_target(pair[1], chips, 0, 1)]
        return singles

    chunks = [strips_of((), True)]
    neighbours, here, chunks[0][0] = lax.optimization_barrier(
        (neighbours, here, chunks[0][0])
    )
    halves = list(pick(here, asks[3:], eigvecs, sib, tile, 2))

    owners = lax.div(neighbours, blocks)
    within = lax.rem(neighbours, blocks)
    distance = lax.rem(owners - own_index + n_atoms, n_atoms)
    spot = lax.rem(within, half_blocks)
    side = lax.div(within, half_blocks)
    for index, offset in enumerate(offsets):
        from_it = distance == offset % n_atoms
        highest = jnp.max(jnp.where(from_it, within, -1))
        side = jnp.where(from_it, (within == highest).astype(jnp.int32), side)
        spot = jnp.where(from_it, half_blocks + index, spot)
    per_core = half_blocks + len(offsets)
    where = ((side ^ core) * per_core + spot).astype(jnp.int32)

    *near, third = arrived
    third, halves, chunks[0][:1] = lax.optimization_barrier((third, halves, chunks[0][:1]))
    lower = shifted(halves[0], "atoms", -offsets[3])
    parts = list(tiles(place, own, kept_sib, [third], weights, n_bands, tile, True))
    pairs = [
        to_strip_target(pair, chips, step + 1, 0) for step, pair in enumerate(parts[2:])
    ]
    later = list_open(where, per_core)
    near, where, later, parts[:2], pairs, chunks, halves = lax.optimization_barrier(
        (near, where, later, parts[:2], pairs, chunks, halves)
    )
    upper = shifted(halves[1], "atoms", -offsets[3])
    chunks.append([parts[0], to_strip_target(parts[1], chips, 0, 1)] + pairs)
    chunks = [passed_on(chunk) for chunk in chunks]
    before = strips_of(near[:1], False)
    near[1], before[:1] = lax.optimization_barrier((near[1], before[:1]))
    after = strips_of(near[1:], False)
    lower, before, after[:2], chunks = lax.optimization_barrier(
        (lower, before, after[:2], chunks)
    )
    lower = list(tiles(place, own, kept_sib, [lower], weights, n_bands, tile, False))
    lower_sib = lower[1]
    for index in range(2, n_bands):
        lower[index] = to_strip_target(lower[index], chips, index // 2, index % 2)
    where, upper, lower[0], after[:3] = lax.optimization_barrier(
        (where, upper, lower[0], after[:3])
    )
    chunks += [before, after]
    last = strips_of([upper], False)
    where, last[0] = lax.optimization_barrier((where, last[0]))
    lower[1] = to_strip_target(lower_sib, chips, 0, 1)
    where, lower = lax.optimization_barrier((where, lower))
    local, far, before, after = chunks
    strips = list(zip(local, before, after, far))
    sizes = [half_blocks, 1, 1, 1]
    density, energy = place_early(where, strips, sizes, chips, per_core)
    outs = place_late(later, lower, last, density, energy, chips)
    return tuple(out.reshape(*where.shape, *out.shape[1:]) for out in outs)


def solution(mesh):
    return jax.shard_map(
        body,
        mesh=mesh,
        in_specs=(P("atoms", "bands"), P("bands"), P("bands"), P("atoms", None)),
        out_specs=(P("atoms", None, "bands", None), P("atoms", None, "bands", None)),
        check_vma=False,
    )
```

```python
import functools

import jax
import jax.numpy as jnp
from jax import lax
from jax.experimental import pallas as pl
from jax.experimental.pallas import tpu as pltpu
from jax.sharding import PartitionSpec as P

R = 2
VMEM_LIMIT = 24 * 1024 * 1024
SOON = pl.CostEstimate(flops=0, bytes_accessed=0, transcendentals=0)


def in_hbm(value):
    return pltpu.with_memory_space_constraint(value, pltpu.HBM)


def in_vmem(value):
    return pltpu.with_memory_space_constraint(value, pltpu.VMEM)


def shifted(value, axis, steps):
    count = lax.axis_size(axis)
    pairs = [(source, (source + steps) % count) for source in range(count)]
    return lax.ppermute(value, axis, pairs)


def strip_target(group, chips, step, other_core):
    chip = lax.rem(lax.shift_right_logical(group, 1) + step, chips)
    return chip * 2 + ((group & 1) ^ other_core)


def to_strip_target(value, chips, step, other_core):
    pairs = [
        (group, (group // 2 + step) % chips * 2 + (group % 2 ^ other_core))
        for group in range(2 * chips)
    ]
    return lax.ppermute(value, "bands", pairs)


def pick_kernel(count, blocks, tile, parts, place_ref, *refs):
    asks, (own, sib), outs = refs[:count], refs[count : count + 2], refs[count + 2 : -1]
    sems = refs[-1]
    first = place_ref[0] * blocks
    copies = []
    for index in range(count):
        ids = asks[index][...] - first
        mine = (ids >= 0) & (ids < blocks)
        lowest = jnp.min(jnp.where(mine, ids, blocks - 1))
        highest = jnp.max(jnp.where(mine, ids, 0))
        block = jnp.where(place_ref[1] == 0, lowest, highest)
        for part in range(parts):
            height = tile // parts
            start = pl.multiple_of(block * tile + part * height, height)
            out = outs[index * parts + part]
            for half, source in enumerate((own, sib)):
                copy = pltpu.make_async_copy(
                    source.at[pl.ds(start, height), :],
                    out.at[half],
                    sems.at[index * parts + part, half],
                )
                copy.start()
                copies.append(copy)
    for copy in copies:
        copy.wait()


def pick(place, asks, own, sib, tile, parts):
    blocks, bands = asks[0].shape[0], own.shape[1]
    count = len(asks)
    n_outs = count * parts
    return pl.pallas_call(
        functools.partial(pick_kernel, count, blocks, tile, parts),
        out_shape=[pltpu.VMEM((2, tile // parts, bands), own.dtype)] * n_outs,
        in_specs=[pl.BlockSpec(memory_space=pltpu.SMEM)]
        + [pl.BlockSpec(memory_space=pltpu.VMEM)] * count
        + [pl.BlockSpec(memory_space=pl.ANY)] * 2,
        out_specs=[pl.BlockSpec(memory_space=pltpu.VMEM)] * n_outs,
        scratch_shapes=[pltpu.SemaphoreType.DMA((n_outs, 2))],
        name="pick_blocks",
        compiler_params=pltpu.CompilerParams(vmem_limit_bytes=VMEM_LIMIT),
        cost_estimate=SOON,
    )(place, *asks, in_hbm(own), in_hbm(sib))


def keep_kernel(own, sib, own_out, sib_out, sems):
    copies = []
    for half, (source, out) in enumerate(((own, own_out), (sib, sib_out))):
        copies.append(pltpu.make_async_copy(source, out, sems.at[half]))
    for copy in copies:
        copy.start()
    for copy in copies:
        copy.wait()


def keep(own, sib):
    return pl.pallas_call(
        keep_kernel,
        out_shape=[pltpu.VMEM(own.shape, own.dtype)] * 2,
        in_specs=[pl.BlockSpec(memory_space=pl.ANY)] * 2,
        out_specs=[pl.BlockSpec(memory_space=pltpu.VMEM)] * 2,
        scratch_shapes=[pltpu.SemaphoreType.DMA((2,))],
        name="keep",
        compiler_params=pltpu.CompilerParams(vmem_limit_bytes=VMEM_LIMIT),
        cost_estimate=SOON,
    )(in_hbm(own), in_hbm(sib))


def tiles_kernel(heights, n_arrived, n_strips, tile, paired, place_ref, *refs):
    lefts, weights = refs[:2], refs[2:4]
    arrived, refs = refs[4 : 4 + n_arrived], refs[4 + n_arrived :]
    outs, (scaled, total) = refs[:-2], refs[-2:]
    if paired:
        outs = outs[:2] + tuple(out.at[index] for out in outs[2:] for index in range(2))
    strip = tile // n_strips
    n_left = lefts[0].shape[0] // tile
    unit = 0
    for j, height in enumerate(heights):
        slot = j % 2
        for half in range(2):
            if n_arrived:
                block = arrived[j][half]
            else:
                first = pl.multiple_of((place_ref[0] * len(heights) + j) * tile, tile)
                block = lefts[half][pl.ds(first, tile), :]
            block = block.astype(jnp.float32)
            for kind in range(2):
                value = block * weights[half][kind : kind + 1, :]
                rows = pl.ds(kind * height, height)
                scaled[slot, half, rows, :] = value.astype(scaled.dtype)
        width = 2 * height
        for half in range(2):
            value = lax.dot_general(
                lefts[half][...],
                scaled[slot, half, :width, :],
                (((1,), (1,)), ((), ())),
                preferred_element_type=jnp.float32,
            )
            if half == 0:
                total[slot, :, :width] = value
            else:
                total[slot, :, :width] += value
        for lane in range(0, width, tile):
            for index in range(n_strips):
                start = place_ref[1 + index] * strip
                for i in range(n_left):
                    rows = pl.ds(pl.multiple_of(i * tile + start, strip), strip)
                    value = total[slot, rows, lane : lane + tile]
                    outs[index][unit, i] = value.astype(outs[index].dtype)
            unit += 1


def tiles(place, own, sib, arrived, weights, n_strips, tile, paired):
    rows, bands = own.shape
    blocks = rows // tile
    heights = [value.shape[1] for value in arrived] or [tile] * (blocks // 2)
    strip = tile // n_strips
    slots = min(len(heights), 2)
    vmem = pl.BlockSpec(memory_space=pltpu.VMEM)
    units = sum(2 * height // tile for height in heights)
    out = jax.ShapeDtypeStruct((units, blocks, strip, tile), jnp.bfloat16)
    pair = jax.ShapeDtypeStruct((2, *out.shape), out.dtype)
    outs = [out, out] + [pair] * (n_strips // 2 - 1) if paired else [out] * n_strips
    return pl.pallas_call(
        functools.partial(tiles_kernel, heights, len(arrived), n_strips, tile, paired),
        out_shape=outs,
        in_specs=[pl.BlockSpec(memory_space=pltpu.SMEM)] + [vmem] * (4 + len(arrived)),
        out_specs=[vmem] * len(outs),
        scratch_shapes=[
            pltpu.VMEM((slots, 2, 2 * max(heights), bands), jnp.bfloat16),
            pltpu.VMEM((slots, rows, 2 * max(heights)), jnp.float32),
        ],
        name="tiles",
        compiler_params=pltpu.CompilerParams(vmem_limit_bytes=VMEM_LIMIT),
        cost_estimate=SOON,
    )(place, in_vmem(own), in_vmem(sib), *weights, *arrived)


def strip_sum(ins, chips, n_chunks, other_core, chunk, unit, i):
    total = None
    for step in range(chips):
        ref = ins[(step * 2 + other_core) * n_chunks + chunk]
        value = ref[unit, i].astype(jnp.float32)
        total = value if total is None else total + value
    return total


def list_kernel(per_core, where_ref, later):
    blocks, slots = where_ref.shape

    def block(i, count):
        for slot in range(slots):
            where = where_ref[i, slot]
            other_core = (where >= per_core).astype(jnp.int32)
            later[2 * count + 1] = i * slots + slot
            later[2 * count + 2] = other_core * blocks + i
            count += (where - other_core * per_core == per_core - 1).astype(jnp.int32)
        return count

    later[0] = lax.fori_loop(0, blocks, block, 0)


def list_open(where, per_core):
    smem = pl.BlockSpec(memory_space=pltpu.SMEM)
    return pl.pallas_call(
        functools.partial(list_kernel, per_core),
        out_shape=jax.ShapeDtypeStruct((2 * where.size + 1,), jnp.int32),
        in_specs=[smem],
        out_specs=smem,
        name="list_open",
        compiler_params=pltpu.CompilerParams(vmem_limit_bytes=VMEM_LIMIT),
        cost_estimate=SOON,
    )(where)


def place_early_kernel(chips, sizes, per_core, where_ref, *refs):
    n_chunks = len(sizes)
    ins = refs[: 2 * chips * n_chunks]
    density, energy, pool, tiles_out, sems = refs[2 * chips * n_chunks :]
    blocks, slots = where_ref.shape

    def copies(i):
        return [
            pltpu.make_async_copy(
                tiles_out.at[i, kind], out.at[pl.ds(i * slots, slots)], sems.at[i, kind]
            )
            for kind, out in enumerate((density, energy))
        ]

    @pl.loop(0, blocks)
    def _(i):
        for other_core in range(2):
            first = other_core * per_core
            for chunk in range(n_chunks):
                for unit in range(2 * sizes[chunk]):
                    pool[first + unit // 2, unit % 2] = strip_sum(
                        ins, chips, n_chunks, other_core, chunk, unit, i
                    )
                first += sizes[chunk]
        for slot in range(slots):
            where = where_ref[i, slot]
            for kind in range(2):
                tiles_out[i, kind, slot] = pool[where, kind]
        for copy in copies(i):
            copy.start()

    for i in range(blocks):
        for copy in copies(i):
            copy.wait()


def place_early(where, strips, sizes, chips, per_core):
    _, blocks, strip, tile = strips[0][0].shape
    slots = where.shape[1]
    out = jax.ShapeDtypeStruct((blocks * slots, strip, tile), jnp.float32)
    flat = [value for group in strips for value in group]
    smem = pl.BlockSpec(memory_space=pltpu.SMEM)
    return pl.pallas_call(
        functools.partial(place_early_kernel, chips, sizes, per_core),
        out_shape=[out, out],
        in_specs=[smem] + [pl.BlockSpec(memory_space=pltpu.VMEM)] * len(flat),
        out_specs=[pl.BlockSpec(memory_space=pl.ANY)] * 2,
        scratch_shapes=[
            pltpu.VMEM((2 * per_core, 2, strip, tile), jnp.float32),
            pltpu.VMEM((blocks, 2, slots, strip, tile), jnp.float32),
            pltpu.SemaphoreType.DMA((blocks, 2)),
        ],
        name="place_early",
        compiler_params=pltpu.CompilerParams(vmem_limit_bytes=VMEM_LIMIT),
        cost_estimate=SOON,
    )(where, *flat)


def place_late_kernel(chips, later, *refs):
    lower, upper = refs[: 2 * chips], refs[2 * chips : 4 * chips]
    density, energy, pool, sems = refs[4 * chips + 2 :]
    blocks = pool.shape[0] // 2
    cut = density.shape[2] // 2
    for other_core in range(2):
        for i in range(blocks):
            low = strip_sum(lower, chips, 1, other_core, 0, 0, i)
            high = strip_sum(upper, chips, 1, other_core, 0, 0, i)
            spot = other_core * blocks + i
            pool[spot, 0] = jnp.concatenate([low[:, :cut], high[:, :cut]], 1)
            pool[spot, 1] = jnp.concatenate([low[:, cut:], high[:, cut:]], 1)
    count = later[0]

    def copies(source, target):
        return [
            pltpu.make_async_copy(pool.at[source, kind], out.at[target], sems.at[kind])
            for kind, out in enumerate((density, energy))
        ]

    @pl.loop(0, count)
    def _(n):
        for copy in copies(later[2 * n + 2], later[2 * n + 1]):
            copy.start()

    @pl.loop(0, count)
    def _(n):
        for copy in copies(0, 0):
            copy.wait()


def place_late(later, lower, upper, density, energy, chips):
    _, blocks, strip, tile = upper[0].shape
    smem = pl.BlockSpec(memory_space=pltpu.SMEM)
    anywhere = pl.BlockSpec(memory_space=pl.ANY)
    out = jax.ShapeDtypeStruct(density.shape, density.dtype)
    strips = [*lower, *upper]
    return pl.pallas_call(
        functools.partial(place_late_kernel, chips),
        out_shape=[out, out],
        in_specs=[smem]
        + [pl.BlockSpec(memory_space=pltpu.VMEM)] * len(strips)
        + [anywhere] * 2,
        out_specs=[anywhere] * 2,
        scratch_shapes=[
            pltpu.VMEM((2 * blocks, 2, strip, tile), jnp.float32),
            pltpu.SemaphoreType.DMA((2,)),
        ],
        input_output_aliases={1 + len(strips): 0, 2 + len(strips): 1},
        name="place_late",
        compiler_params=pltpu.CompilerParams(vmem_limit_bytes=VMEM_LIMIT),
        cost_estimate=SOON,
    )(later, *strips, density, energy)


def body(eigvecs, occupations, energies, neighbours):
    n_atoms = lax.axis_size("atoms")
    n_bands = lax.axis_size("bands")
    chips = n_bands // 2
    own_index = lax.axis_index("atoms").astype(jnp.int32)
    group = lax.axis_index("bands").astype(jnp.int32)
    core = group & 1
    blocks = neighbours.shape[0]
    tile = eigvecs.shape[0] // blocks
    half_blocks = blocks // 2
    offsets = [-1, 1, 2, -2]

    asks = [shifted(neighbours, "atoms", offset) for offset in offsets]
    sib = to_strip_target(eigvecs, chips, 0, 1)
    own_weights = jnp.stack([occupations, occupations * energies], 0)

    targets = [
        strip_target(group, chips, step, other)
        for step in range(chips)
        for other in range(2)
    ]
    here = jnp.stack([own_index, core]).astype(jnp.int32)
    place = jnp.stack([core] + targets).astype(jnp.int32)

    asks, own_weights = lax.optimization_barrier((asks, own_weights))
    weights = (own_weights, to_strip_target(own_weights, chips, 0, 1))
    picked = list(pick(here, asks[:3], eigvecs, sib, tile, 1))
    arrived = [
        shifted(value, "atoms", -offset) for value, offset in zip(picked, offsets)
    ]
    kept_eigvecs, picked[0] = lax.optimization_barrier((eigvecs, picked[0]))
    own, kept_sib = keep(kept_eigvecs, sib)

    def strips_of(arrived, paired):
        parts = list(tiles(place, own, kept_sib, arrived, weights, n_bands, tile, paired))
        for index in range(1, len(parts)):
            step, other = (max(index - 1, 0), index == 1) if paired else (index // 2, index % 2)
            parts[index] = to_strip_target(parts[index], chips, step, int(other))
        return parts

    def passed_on(parts):
        singles = parts[:2]
        for pair in parts[2:]:
            singles += [pair[0], to_strip_target(pair[1], chips, 0, 1)]
        return singles

    chunks = [strips_of((), True)]
    neighbours, here, chunks[0][0] = lax.optimization_barrier(
        (neighbours, here, chunks[0][0])
    )
    halves = list(pick(here, asks[3:], eigvecs, sib, tile, 2))

    owners = lax.div(neighbours, blocks)
    within = lax.rem(neighbours, blocks)
    distance = lax.rem(owners - own_index + n_atoms, n_atoms)
    spot = lax.rem(within, half_blocks)
    side = lax.div(within, half_blocks)
    for index, offset in enumerate(offsets):
        from_it = distance == offset % n_atoms
        highest = jnp.max(jnp.where(from_it, within, -1))
        side = jnp.where(from_it, (within == highest).astype(jnp.int32), side)
        spot = jnp.where(from_it, half_blocks + index, spot)
    per_core = half_blocks + len(offsets)
    where = ((side ^ core) * per_core + spot).astype(jnp.int32)

    *near, third = arrived
    third, halves, chunks[0][:1] = lax.optimization_barrier((third, halves, chunks[0][:1]))
    lower = shifted(halves[0], "atoms", -offsets[3])
    parts = list(tiles(place, own, kept_sib, [third], weights, n_bands, tile, True))
    pairs = [
        to_strip_target(pair, chips, step + 1, 0) for step, pair in enumerate(parts[2:])
    ]
    later = list_open(where, per_core)
    near, where, later, parts[:2], pairs, chunks, halves = lax.optimization_barrier(
        (near, where, later, parts[:2], pairs, chunks, halves)
    )
    upper = shifted(halves[1], "atoms", -offsets[3])
    chunks.append([parts[0], to_strip_target(parts[1], chips, 0, 1)] + pairs)
    chunks = [passed_on(chunk) for chunk in chunks]
    direct = strips_of(near, False)
    lower, direct[:2], chunks = lax.optimization_barrier((lower, direct[:2], chunks))
    lower = list(tiles(place, own, kept_sib, [lower], weights, n_bands, tile, False))
    lower_sib = lower[1]
    for index in range(2, n_bands):
        lower[index] = to_strip_target(lower[index], chips, index // 2, index % 2)
    where, upper, lower[0], direct[:3] = lax.optimization_barrier(
        (where, upper, lower[0], direct[:3])
    )
    chunks.append(direct)
    last = strips_of([upper], False)
    where, last[0] = lax.optimization_barrier((where, last[0]))
    lower[1] = to_strip_target(lower_sib, chips, 0, 1)
    where, lower = lax.optimization_barrier((where, lower))
    local, far, direct = chunks
    strips = list(zip(local, direct, far))
    sizes = [half_blocks, 2, 1]
    density, energy = place_early(where, strips, sizes, chips, per_core)
    outs = place_late(later, lower, last, density, energy, chips)
    return tuple(out.reshape(*where.shape, *out.shape[1:]) for out in outs)


def solution(mesh):
    return jax.shard_map(
        body,
        mesh=mesh,
        in_specs=(P("atoms", "bands"), P("bands"), P("bands"), P("atoms", None)),
        out_specs=(P("atoms", None, "bands", None), P("atoms", None, "bands", None)),
        check_vma=False,
    )
```
